32 devices in a mesh: dp: 8 (over y, x, core), table: 4 (over z).
Axes of the slice: x: 2, y: 2, z: 4, core: 2. Of those that a mesh axis runs over, the one named last changes fastest.
Arguments:
- knowledge: bfloat16 [5, 4608, 768], P(None, ('dp', 'table')), may hold values from -2.390625 to 2.390625
- expr_table: bfloat16 [128, 768], replicated, may hold values from -2.390625 to 2.390625
- gene_owner: int32 [8192, 1], P(('dp', 'table')), may hold values from 0 to 31; in each aligned block of 256 rows (0 to 255, 256 to 511, ...) at most 16 rows name the same one
- gene_row: int32 [8192], P(('dp', 'table')), may hold values from 0 to 143
- expr_bin: int32 [8192], P(('dp', 'table')), may hold values from 0 to 127
- cell_lengths: int32 [256], P(('dp', 'table')), may hold values from 0 to 256, as said below
- norm1_gain: float32 [768], replicated, may hold values from 0.5 to 1.5
- norm1_bias: float32 [768], replicated, may hold values from -1.8 to 1.8
- w_query: bfloat16 [768, 768], replicated, may hold values from -0.21875 to 0.21875
- b_query: float32 [768], replicated, may hold values from -1.8 to 1.8
- w_key: bfloat16 [768, 768], replicated, may hold values from -0.21875 to 0.21875
- w_value: bfloat16 [768, 768], replicated, may hold values from -0.21875 to 0.21875
- b_value: float32 [768], replicated, may hold values from -1.8 to 1.8
- w_attn_out: bfloat16 [768, 768], replicated, may hold values from -0.875 to 0.875
- b_attn_out: float32 [768], replicated, may hold values from -1.8 to 1.8
- norm2_gain: float32 [768], replicated, may hold values from 0.5 to 1.5
- norm2_bias: float32 [768], replicated, may hold values from -1.8 to 1.8
- w_in: bfloat16 [768, 3072], replicated, may hold values from -0.21875 to 0.21875
- b_in: float32 [3072], replicated, may hold values from -1.8 to 1.8
- w_out: bfloat16 [3072, 768], replicated, may hold values from -0.109375 to 0.109375
- b_out: float32 [768], replicated, may hold values from -1.8 to 1.8
- cotangent: bfloat16 [8192, 768], P(('dp', 'table')), may hold values from -6 to 6
Outputs:
- mixed: bfloat16 [8192, 768], P(('dp', 'table'))
- knowledge_grad: float32 [5, 4608, 768], P(None, ('dp', 'table'))
- expr_table_grad: float32 [128, 768], replicated
- norm1_gain_grad: float32 [768], replicated
- norm1_bias_grad: float32 [768], replicated
- w_query_grad: float32 [768, 768], replicated
- b_query_grad: float32 [768], replicated
- w_key_grad: float32 [768, 768], replicated
- w_value_grad: float32 [768, 768], replicated
- b_value_grad: float32 [768], replicated
- w_attn_out_grad: float32 [768, 768], replicated
- b_attn_out_grad: float32 [768], replicated
- norm2_gain_grad: float32 [768], replicated
- norm2_bias_grad: float32 [768], replicated
- w_in_grad: float32 [768, 3072], replicated
- b_in_grad: float32 [3072], replicated
- w_out_grad: float32 [3072, 768], replicated
- b_out_grad: float32 [768], replicated
The draws below stay inside these ranges and needn't reach their ends.
Inputs may be any that keep to these rules, and one draw needn't show every extreme that they name: `gene_owner`: within the rows of one device no owner index is named by more than 16 rows, and in every draw some device names some owner exactly 16 times. `cell_lengths`: the 8 entries of one device sum to at most 256; the first is positive and zeros stand only after the positive ones. In every draw some device holds a single cell of 256 tokens.
All inputs are finite; a program needn't handle non-finite values.
Results may differ from the reference program's by a relative error of at most 0.012.
Values may be sent and summed in bfloat16 or wider, within the bound.
A program may use at most 192 MiB of HBM per device.

```python
import math
import jax
import jax.numpy as jnp
import numpy as np
from jax import lax

D = 768
HEADS = 12
HEAD_DIM = 64
FF = 3072
TABLES = 5
ROWS_DEV = 144
BINS = 128
TOK_DEV = 256
CELLS_DEV = 8
TOKENS = 8192
CELLS = 256
VOCAB = 4608
CAP = 16
N_DP = 8
N_TABLE = 4
DEVICES = 32


def draw_cell_lengths(key, part):
    devices = CELLS // CELLS_DEV
    shift_key, base_key, pick_key = jax.random.split(jax.random.fold_in(key, 17), 3)
    powers = jax.random.randint(shift_key, (devices, CELLS_DEV), 0, 6)
    base_len = jax.random.randint(base_key, (devices, CELLS_DEV), 8, 33)
    drawn = jnp.left_shift(base_len, powers) * TOK_DEV // 1024
    drawn = jnp.clip(drawn, 1, TOK_DEV)
    cell_ends = jnp.cumsum(drawn, axis=1)
    kept_len = jnp.where(cell_ends <= TOK_DEV, drawn, 0)
    chosen = jax.random.randint(pick_key, (), 0, devices)
    whole_cell = jnp.zeros((CELLS_DEV,), jnp.int32).at[0].set(TOK_DEV)
    table_rows = jnp.where((jnp.arange(devices) == chosen)[:, None], whole_cell[None, :], kept_len)
    return table_rows.reshape(-1).astype(jnp.int32)


def with_ends(array, stream_key, low, high):
    shape = array.shape
    index_at = [jax.random.randint(jax.random.fold_in(stream_key, axis), (), 0, shape[axis]) for axis in range(len(shape))]
    array = array.at[tuple(index_at)].set(low)
    longest = shape.index(max(shape))
    index_at[longest] = (index_at[longest] + 1) % shape[longest]
    return array.at[tuple(index_at)].set(high)


def steps_of(own_key, dims, shards, smallest, top_value):
    factor_of = 1.0
    for dim, shards_of in shards:
        steps = jax.random.uniform(jax.random.fold_in(jax.random.fold_in(own_key, 6), dim), (shards_of,), jnp.float32, smallest / len(shards), top_value / len(shards))
        factor_of = factor_of * jnp.repeat(jnp.exp(steps), dims[dim] // shards_of).reshape((-1,) + (1,) * (len(dims) - 1 - dim))
    return factor_of


def rank_table(number_of, slope):
    loads = [(1 << 20) // math.isqrt(standing ** slope) + 1 for standing in range(1, number_of + 1)]
    deviation = 1 + sum(loads) // (1 << 30)
    return np.cumsum(np.array([max(1, weight // deviation) for weight in loads]))


def ranked_ids(stream_key, shape, number_of, lean):
    grid = rank_table(number_of, lean)
    ticket = jax.random.randint(jax.random.fold_in(stream_key, 1), shape, 0, int(grid[number_of - 1]))
    standing = jnp.searchsorted(jnp.asarray(grid, jnp.int32), ticket, side="right")
    return jax.random.permutation(jax.random.fold_in(stream_key, 2), number_of)[standing].astype(jnp.int32)


def assign_block(key, own, number, rows, number_of, top, reach, skew):
    ranking = jax.random.permutation(key, number_of)
    packed, common = shares(number_of, rows * top, reach, skew, True), shares(number_of, rows * top, reach, skew, False)
    places = jnp.arange(number_of)

    def named(sizes, rotation):
        used = int((sizes > 0).sum())
        fixed = max(1, used // 4)
        passed = fixed + (places - fixed + rotation * (used - fixed)) % max(1, number_of - fixed)
        return jnp.zeros((number_of,), jnp.int32).at[ranking[jnp.where(places < fixed, places, passed)]].set(jnp.asarray(sizes, jnp.int32))

    sizes = jnp.where(number % 4 == 0, named(packed, number // 4), named(common, number - number // 4 - 1))
    mixed = jax.random.permutation(jax.random.fold_in(own, 3), number_of)
    donor, taker = mixed[0:number_of // 2 * 2:2], mixed[1:number_of // 2 * 2:2]
    margin = jnp.minimum(sizes[donor] - 1, reach - sizes[taker]) // 2
    margin = jnp.where((donor == ranking[0]) | (taker == ranking[0]) | (sizes[taker] == 0), 0, jnp.maximum(margin, 0))
    passed = jax.random.randint(jax.random.fold_in(own, 4), (number_of // 2,), 0, 1 << 20) % (margin + 1)
    sizes = sizes.at[donor].add(-passed).at[taker].add(passed)
    members = jnp.searchsorted(jnp.cumsum(sizes), jnp.arange(rows * top), side="right").astype(jnp.int32)
    listing = members.reshape(top, rows).T
    listing = listing[jax.random.permutation(jax.random.fold_in(own, 1), rows)]
    rotation = jax.random.randint(jax.random.fold_in(own, 2), (rows, 1), 0, top)
    return jnp.take_along_axis(listing, (jnp.arange(top)[None, :] + rotation) % top, axis=1)


def shares(count, total, bound, skew, full):
    portions = [(1 << 20) // math.isqrt(rank ** skew) + 1 for rank in range(1, count + 1)]
    largest = bound if full else min(bound, max(-(-total // count), total * portions[0] // sum(portions)))
    least = 1 if total - largest >= count - 1 else 0
    given, rest = [largest] + [least] * (count - 1), total - largest - least * (count - 1)
    while rest > 0:
        free = [i for i in range(1, count) if given[i] < largest] or [i for i in range(1, count) if given[i] < bound]
        mass, remaining = sum([portions[i] for i in free]), rest
        for i in free:
            extra = min(bound - given[i], max(1, remaining * portions[i] // mass), rest)
            given[i] = given[i] + extra
            rest = rest - extra
    return np.array(given)


def gaussian(stream_key, extent, width, limit, shards=(), kind=jnp.bfloat16):
    values = width * jax.random.normal(stream_key, extent, jnp.float32)
    if shards:
        values = values * steps_of(stream_key, extent, shards, -0.22, 0.18)
    return jnp.clip(values, -limit, limit).astype(kind)


def setup_inputs(seed: int = 0) -> dict:
    streams_of = jax.random.split(jax.random.key(seed), 23)
    knowledge = gaussian(streams_of[0], (TABLES, VOCAB, D), 0.4, 2.390625, ((1, 32),))
    expr_table = gaussian(streams_of[1], (BINS, D), 0.4, 2.390625)
    gene_owner_keys = jax.random.split(jax.random.fold_in(streams_of[2], 1), TOKENS // TOK_DEV)
    gene_owner_turns = jax.random.permutation(jax.random.fold_in(streams_of[2], 3), TOKENS // TOK_DEV)
    gene_owner = jax.vmap(lambda own, number: assign_block(jax.random.fold_in(streams_of[2], 2), own, number, TOK_DEV, DEVICES, 1, CAP, 1))(gene_owner_keys, gene_owner_turns).reshape((TOKENS, 1))
    gene_row = with_ends(ranked_ids(streams_of[3], (TOKENS,), ROWS_DEV, 2), jax.random.fold_in(streams_of[3], 3), 0, ROWS_DEV - 1).astype(jnp.int32)
    expr_bin = with_ends(jax.random.randint(streams_of[4], (TOKENS,), 0, BINS), jax.random.fold_in(streams_of[4], 1), 0, BINS - 1).astype(jnp.int32)
    cell_lengths = draw_cell_lengths(jax.random.fold_in(streams_of[22], 71), 0)
    norm1_gain = jnp.clip(1.0 + 0.1 * jax.random.normal(streams_of[6], (D,), jnp.float32), 0.5, 1.5)
    norm1_bias = gaussian(streams_of[7], (D,), 0.3, 1.8, (), jnp.float32)
    w_query = gaussian(streams_of[8], (D, D), D ** -0.5, 0.21875)
    b_query = gaussian(streams_of[9], (D,), 0.3, 1.8, (), jnp.float32)
    w_key = gaussian(streams_of[10], (D, D), D ** -0.5, 0.21875)
    w_value = gaussian(streams_of[11], (D, D), D ** -0.5, 0.21875)
    b_value = gaussian(streams_of[12], (D,), 0.3, 1.8, (), jnp.float32)
    w_attn_out = gaussian(streams_of[13], (D, D), (D // 16) ** -0.5, 0.875)
    b_attn_out = gaussian(streams_of[14], (D,), 0.3, 1.8, (), jnp.float32)
    norm2_gain = jnp.clip(1.0 + 0.1 * jax.random.normal(streams_of[15], (D,), jnp.float32), 0.5, 1.5)
    norm2_bias = gaussian(streams_of[16], (D,), 0.3, 1.8, (), jnp.float32)
    w_in = gaussian(streams_of[17], (D, FF), D ** -0.5, 0.21875)
    b_in = gaussian(streams_of[18], (FF,), 0.3, 1.8, (), jnp.float32)
    w_out = gaussian(streams_of[19], (FF, D), FF ** -0.5, 0.109375)
    b_out = gaussian(streams_of[20], (D,), 0.3, 1.8, (), jnp.float32)
    cotangent = gaussian(streams_of[21], (TOKENS, D), 1.0, 6.0, ((0, 32),))
    return dict(knowledge=knowledge, expr_table=expr_table, gene_owner=gene_owner, gene_row=gene_row, expr_bin=expr_bin, cell_lengths=cell_lengths, norm1_gain=norm1_gain, norm1_bias=norm1_bias, w_query=w_query, b_query=b_query, w_key=w_key, w_value=w_value, b_value=b_value, w_attn_out=w_attn_out, b_attn_out=b_attn_out, norm2_gain=norm2_gain, norm2_bias=norm2_bias, w_in=w_in, b_in=b_in, w_out=w_out, b_out=b_out, cotangent=cotangent)


LAYER_EPS = 1e-05
GELU_SLOPE = 0.7978845608028654
GELU_CUBIC = 0.044715
MASKED = -1e+30
EXACT_PRECISION = lax.Precision.HIGHEST

@jax.custom_vjp
def low(v):
    return lax.optimization_barrier(v.astype(jnp.bfloat16)).astype(jnp.float32)

@jax.custom_vjp
def low_back(v):
    return v

def low_keep(v):
    return (low(v), None)

def low_pass(kept, grad):
    return (grad,)

def back_keep(v):
    return (v, None)

def back_low(kept, grad):
    return (low(grad),)
low.defvjp(low_keep, low_pass)
low_back.defvjp(back_keep, back_low)

def round_both(value):
    return low(low_back(value))

def matmul(left, right):
    return jnp.dot(left, right, precision=EXACT_PRECISION, preferred_element_type=jnp.float32)

def gelu_tanh(pre_act):
    return 0.5 * pre_act * (1.0 + jnp.tanh(GELU_SLOPE * (pre_act + GELU_CUBIC * pre_act * pre_act * pre_act)))

def layer_norm(inputs, gain, shift):
    average = lax.optimization_barrier(jnp.mean(inputs, axis=-1, keepdims=True))
    centred = inputs - average
    spread = lax.optimization_barrier(jnp.mean(centred * centred, axis=-1, keepdims=True))
    return centred * lax.rsqrt(spread + LAYER_EPS) * gain + shift

def cell_masks(lengths):
    cell_ends = jnp.cumsum(lengths).astype(jnp.int32)
    places = jnp.arange(TOK_DEV, dtype=jnp.int32)
    segment = lax.optimization_barrier(jnp.sum((places[:, None] >= cell_ends[None, :]).astype(jnp.int32), axis=1)).astype(jnp.int32)
    live_mask = (places < cell_ends[-1]).astype(jnp.float32)
    return (segment, live_mask)

def attend(query_rows, key_rows, value_rows, segment):
    count = query_rows.shape[0]
    query_heads = query_rows.reshape(count, HEADS, HEAD_DIM)
    key_heads = key_rows.reshape(count, HEADS, HEAD_DIM)
    value_heads = value_rows.reshape(count, HEADS, HEAD_DIM)
    scores = jnp.einsum('qhd,khd->hqk', query_heads, key_heads, precision=EXACT_PRECISION) * HEAD_DIM ** (-0.5)
    scores = low_back(scores)
    same_cell = segment[:, None] == segment[None, :]
    scores = jnp.where(same_cell[None], scores, MASKED)
    attn_probs = low(jax.nn.softmax(scores, axis=-1))
    context = jnp.einsum('hqk,khd->qhd', attn_probs, value_heads, precision=EXACT_PRECISION)
    return context.reshape(count, HEADS * HEAD_DIM)

def device_layer(params, embedded, segment, live_mask):
    norm1_gain, norm1_bias, w_query, b_query, w_key, w_value, b_value, w_attn_out, b_attn_out, norm2_gain, norm2_bias, w_in, b_in, w_out, b_out = params
    embedded = low_back(embedded)
    attn_in = low(layer_norm(embedded, norm1_gain, norm1_bias))
    query_rows = round_both(matmul(attn_in, w_query) + b_query)
    key_rows = round_both(matmul(attn_in, w_key))
    value_rows = round_both(matmul(attn_in, w_value) + b_value)
    context = round_both(attend(query_rows, key_rows, value_rows, segment))
    hidden1 = embedded + low_back(matmul(context, w_attn_out) + b_attn_out)
    ffn_in = low(layer_norm(hidden1, norm2_gain, norm2_bias))
    pre_act = low_back(matmul(ffn_in, w_in) + b_in)
    act_low = low(gelu_tanh(pre_act))
    hidden2 = hidden1 + low_back(matmul(act_low, w_out) + b_out)
    return hidden2 * live_mask[:, None]

def reference(knowledge, expr_table, gene_owner, gene_row, expr_bin, cell_lengths, norm1_gain, norm1_bias, w_query, b_query, w_key, w_value, b_value, w_attn_out, b_attn_out, norm2_gain, norm2_bias, w_in, b_in, w_out, b_out, cotangent):
    devices = N_DP * N_TABLE
    genes = (gene_owner[:, 0] * ROWS_DEV + gene_row).astype(jnp.int32)
    segment, live_mask = jax.vmap(cell_masks)(cell_lengths.reshape(devices, CELLS_DEV))
    params = (norm1_gain, norm1_bias, w_query.astype(jnp.float32), b_query, w_key.astype(jnp.float32), w_value.astype(jnp.float32), b_value, w_attn_out.astype(jnp.float32), b_attn_out, norm2_gain, norm2_bias, w_in.astype(jnp.float32), b_in, w_out.astype(jnp.float32), b_out)

    def forward(tables, expr_rows, layer_params):
        embedded = expr_rows[expr_bin]
        for table_index in range(TABLES):
            embedded = embedded + tables[table_index][genes]
        blocks = embedded.reshape(devices, TOK_DEV, D)

        def one_device(inputs):
            return device_layer(layer_params, inputs[0], inputs[1], inputs[2])
        outputs = lax.map(jax.checkpoint(one_device), (blocks, segment, live_mask))
        return outputs.reshape(devices * TOK_DEV, D)
    result, pullback = jax.vjp(forward, knowledge.astype(jnp.float32), expr_table.astype(jnp.float32), params)
    table_grads, expr_grads, param_grads = pullback(cotangent.astype(jnp.float32))
    return (result.astype(jnp.bfloat16), table_grads, expr_grads, param_grads[0], param_grads[1], param_grads[2], param_grads[3], param_grads[4], param_grads[5], param_grads[6], param_grads[7], param_grads[8], param_grads[9], param_grads[10], param_grads[11], param_grads[12], param_grads[13], param_grads[14])
```

```python
import functools
import math

import jax
import jax.numpy as jnp
from jax import lax
from jax.sharding import PartitionSpec as P
from jax.experimental import pallas as pl
from jax.experimental.pallas import tpu as pltpu
MESH = pl.DeviceIdType.MESH
BF=jnp.bfloat16; F32=jnp.float32

def ar_stages(n, nz, refs, coords):
    inp, gath, cb, xb, zb, yb, zf, (rc, rx, rz, ry, gz, gf, gc), (sc, sx, sz, sy, sgz, sgf, sgc) = refs
    a, b, core, t = coords
    def dev(a_, b_, c_, t_): return ((a_*n+b_)*2+c_, t_)
    me = dev(a,b,core,t)
    def axes(k):
        even = lax.rem(k,2)==0
        f = jnp.where(even,b,a); s = jnp.where(even,a,b)
        def fpeer(m):
            q=lax.rem(f+m,n)
            return q, dev(jnp.where(even,a,q), jnp.where(even,q,b), core, t)
        def speer(m):
            q=lax.rem(s+m,n)
            return q, dev(jnp.where(even,q,a), jnp.where(even,b,q), core, t)
        return f,s,fpeer,speer
    corepeer = dev(a,b,1-core,t)
    right = dev(a,b,core,jnp.minimum(t+1,nz-1)); left = dev(a,b,core,jnp.maximum(t-1,0))
    def rcopy(src,dst,ss,rs,to): return pltpu.make_async_remote_copy(src_ref=src,dst_ref=dst,send_sem=ss,recv_sem=rs,device_id=to,device_id_type=MESH)
    def send(src,dst,ss,rs,to): rcopy(src,dst,ss,rs,to).start()
    def wait(dst,rs,ss): rcopy(dst,dst,ss,rs,corepeer).wait_recv()
    def s0(k):
        send(inp.at[k,1-core], cb.at[k], sc, rc.at[k], corepeer)
    def s1(k):
        f,s,fpeer,speer=axes(k)
        wait(cb.at[k], rc.at[k], sc)
        cb[k] = (cb[k].astype(F32)+inp[k,core].astype(F32)).astype(BF)
        for m in range(1,n):
            q,to=fpeer(m)
            send(cb.at[k,q], xb.at[k,m-1], sx, rx.at[k,m-1], to)
    def s2(k):
        f,s,fpeer,speer=axes(k)
        for m in range(1,n): wait(xb.at[k,m-1], rx.at[k,m-1], sx)
        acc = cb[k,f].astype(F32)
        for m in range(1,n): acc = acc + xb[k,m-1].astype(F32)
        xb[k,0]=acc.astype(BF)
        @pl.when(t==0)
        def _():
            for j in range(nz-1,0,-1):
                send(xb.at[k,0,j], zb.at[k, j if j>1 else nz], sz, rz.at[k, j if j>1 else nz], right)
        @pl.when(t==nz-1)
        def _():
            for j in range(0,nz-1):
                send(xb.at[k,0,j], zb.at[k,j], sz, rz.at[k,j], left)
    def zstep(s):
        def f_(k):
            @pl.when(t==s)
            def _():
                for j in range(nz-1,s,-1):
                    wait(zb.at[k,j], rz.at[k,j], sz)
                    zb[k,j]=(zb[k,j].astype(F32)+xb[k,0,j].astype(F32)).astype(BF)
                    sl = j if j>s+1 else nz
                    send(zb.at[k,j], zb.at[k,sl], sz, rz.at[k,sl], right)
            @pl.when(t==nz-1-s)
            def _():
                for j in range(0,nz-1-s):
                    wait(zb.at[k,j], rz.at[k,j], sz)
                    zb[k,j]=(zb[k,j].astype(F32)+xb[k,0,j].astype(F32)).astype(BF)
                    send(zb.at[k,j], zb.at[k,j], sz, rz.at[k,j], left)
        return f_
    def zfin(k):
        f,s,fpeer,speer=axes(k)
        @pl.when(t==0)
        def _():
            wait(zb.at[k,0], rz.at[k,0], sz)
            zf[k]=(xb[k,0,0].astype(F32)+zb[k,0].astype(F32)).astype(BF)
        @pl.when(t==nz-1)
        def _():
            wait(zb.at[k,nz], rz.at[k,nz], sz)
            zf[k]=(xb[k,0,nz-1].astype(F32)+zb[k,nz].astype(F32)).astype(BF)
        @pl.when((t>0)&(t<nz-1))
        def _():
            wait(zb.at[k,nz], rz.at[k,nz], sz)
            wait(zb.at[k,t], rz.at[k,t], sz)
            zf[k]=(xb[k,0,t].astype(F32)+zb[k,nz].astype(F32)+zb[k,t].astype(F32)).astype(BF)
        for m in range(1,n):
            q,to=speer(m)
            send(zf.at[k], yb.at[k,m-1], sy, ry.at[k,m-1], to)
    def yfin(k):
        f,s,fpeer,speer=axes(k)
        for m in range(1,n): wait(yb.at[k,m-1], ry.at[k,m-1], sy)
        if n==2:
            acc = zf[k].astype(F32)+yb[k,0].astype(F32)
        else:
            acc = None
            for q in range(n):
                m = lax.rem(s-q+n,n)
                v = jnp.where(m==0, zf[k].astype(F32), yb[k,jnp.maximum(m-1,0)].astype(F32))
                acc = v if acc is None else acc+v
        gath[k,core,f,t]=acc.astype(BF)
        g=gath.at[k,core,f,t]
        @pl.when(t<nz-1)
        def _(): send(g,g,sgz,gz.at[k,t],right)
        @pl.when(t>0)
        def _(): send(g,g,sgz,gz.at[k,t],left)
    def gstep(s):
        def f_(k):
            f,_,fpeer,_2=axes(k)
            @pl.when(t>=s)
            def _():
                j=jnp.maximum(t-s,0)
                g=gath.at[k,core,f,j]
                wait(g,gz.at[k,j],sgz)
                @pl.when(t<nz-1)
                def _(): send(g,g,sgz,gz.at[k,j],right)
            @pl.when(t<=nz-1-s)
            def _():
                j=jnp.minimum(t+s,nz-1)
                g=gath.at[k,core,f,j]
                wait(g,gz.at[k,j],sgz)
                @pl.when(t>0)
                def _(): send(g,g,sgz,gz.at[k,j],left)
            if s==nz-1:
                g=gath.at[k,core,f]
                for m in range(1,n):
                    q,to=fpeer(m)
                    send(g,g,sgf,gf.at[k,m-1],to)
        return f_
    def gcore(k):
        f,_,fpeer,_2=axes(k)
        for m in range(1,n):
            q=lax.rem(f-m+n,n)
            wait(gath.at[k,core,q],gf.at[k,m-1],sgf)
        g=gath.at[k,core]
        send(g,g,sgc,gc.at[k],corepeer)
    def gfin(k):
        wait(gath.at[k,1-core],gc.at[k],sgc)
    def drain(K):
        def ws(ref,ss): rcopy(ref,ref,ss,rc.at[0],corepeer).wait_send()
        ws(cb,sc); ws(xb,sx); ws(zb.at[:,pl.ds(0,nz-1)],sz); ws(yb,sy)
        mid=(t>0)&(t<nz-1)
        @pl.when(mid)
        def _(): ws(zb,sgz)
        @pl.when(jnp.logical_not(mid))
        def _(): ws(zb.at[:,pl.ds(0,1)],sgz)
        ws(xb,sgf); ws(cb,sgc)
    stages=[s0,s1,s2]+[zstep(s) for s in range(1,nz-1)]+[zfin,yfin]+[gstep(s) for s in range(1,nz)]+[gcore,gfin]
    return stages, drain

def ar_scratch(K,n,nz,r,L):
    D=pltpu.SemaphoreType.DMA
    bufs=[pltpu.VMEM((K,n,nz,r,L),BF), pltpu.VMEM((K,n-1,nz,r,L),BF), pltpu.VMEM((K,nz+1,r,L),BF), pltpu.VMEM((K,n-1,r,L),BF), pltpu.VMEM((K,r,L),BF)]
    rs=[D((K,)),D((K,n-1)),D((K,nz+1)),D((K,n-1)),D((K,nz)),D((K,n-1)),D((K,))]
    ss=[D(())]*7
    return bufs+rs+ss
def barrier_neighbors(n,nz,coords):
    a,b,core,t=coords
    def dev(a_, b_, c_, t_): return ((a_*n+b_)*2+c_, t_)
    bar=pltpu.get_barrier_semaphore()
    sig=lambda to: pl.semaphore_signal(bar,inc=1,device_id=to,device_id_type=MESH)
    sig(dev(a,b,1-core,t))
    for m in range(1,n):
        sig(dev(lax.rem(a+m,n),b,core,t)); sig(dev(a,lax.rem(b+m,n),core,t))
    @pl.when(t>0)
    def _(): sig(dev(a,b,core,t-1))
    @pl.when(t<nz-1)
    def _(): sig(dev(a,b,core,t+1))
    pl.semaphore_wait(bar,1+2*(n-1)+jnp.where((t>0)&(t<nz-1),2,1))
def coords_of(n):
    d=lax.axis_index("dp"); t=lax.axis_index("table")
    return d//(2*n), (d//2)%n, d%2, t
def ar_kernel(K,n,nz,offs,inp,gath,*scr):
    bufs=scr[:5]; rs=scr[5:12]; ss=scr[12:19]
    coords=coords_of(n)
    barrier_neighbors(n,nz,coords)
    stages,drain=ar_stages(n,nz,(inp,gath,*bufs,rs,ss),coords)
    cum=[0]
    for o in offs: cum.append(cum[-1]+o)
    assert len(cum)==len(stages),(len(cum),len(stages))
    def body(i,_):
        for st,o in reversed(list(zip(stages,cum))):
            k=i-o
            @pl.when((k>=0)&(k<K))
            def _(): st(k)
        return 0
    lax.fori_loop(0,K+cum[-1],body,0)
    drain(K)
def ar_call(K,n,nz,r,L,offs,cid=1):
    return pl.pallas_call(functools.partial(ar_kernel,K,n,nz,offs),
      out_shape=jax.ShapeDtypeStruct((K,2,n,nz,r,L),BF),
      in_specs=[pl.BlockSpec(memory_space=pltpu.VMEM)],out_specs=pl.BlockSpec(memory_space=pltpu.VMEM),
      scratch_shapes=ar_scratch(K,n,nz,r,L),
      compiler_params=pltpu.CompilerParams(collective_id=cid,has_side_effects=True,vmem_limit_bytes=60*2**20))

HEADS = 12
HEAD_DIM = 64
TABLES = 5


LAYER_EPS = 1e-05
GELU_SLOPE = 0.7978845608028654
GELU_CUBIC = 0.044715
MASKED = -1e30


def gelu_tanh(pre_act):
    return (
        0.5
        * pre_act
        * (1.0 + jnp.tanh(GELU_SLOPE * (pre_act + GELU_CUBIC * pre_act * pre_act * pre_act)))
    )


def layer_norm(inputs, gain, shift):
    average = jnp.mean(inputs, axis=-1, keepdims=True)
    centred = inputs - average
    spread = jnp.mean(centred * centred, axis=-1, keepdims=True)
    return centred * lax.rsqrt(spread + LAYER_EPS) * gain + shift


def cell_masks(lengths, count):
    order = jnp.arange(lengths.shape[0])
    cell_ends = jnp.sum(jnp.where(order[:, None] <= order[None, :], lengths[:, None], 0), axis=0)
    places = jnp.arange(count, dtype=jnp.int32)
    segment = jnp.sum((places[:, None] >= cell_ends[None, :]).astype(jnp.int32), axis=1)
    live_mask = (places < cell_ends[-1]).astype(jnp.float32)
    return (segment, live_mask)


def local(
    knowledge,
    expr_table,
    gene_owner,
    gene_row,
    expr_bin,
    cell_lengths,
    norm1_gain,
    norm1_bias,
    w_query,
    b_query,
    w_key,
    w_value,
    b_value,
    w_attn_out,
    b_attn_out,
    norm2_gain,
    norm2_bias,
    w_in,
    b_in,
    w_out,
    b_out,
    cotangent,
):
    devices = lax.axis_size(("dp", "table"))
    tok_count = cotangent.shape[0]
    model_width = cotangent.shape[1]
    table_rows = knowledge.shape[1]
    capacity = 2 * tok_count // devices
    owner_ids = gene_owner[:, 0]
    owner_hot = (owner_ids[:, None] == jnp.arange(devices, dtype=jnp.int32)[None, :]).astype(
        jnp.int32
    )
    spots = jnp.arange(tok_count)
    earlier = (spots[:, None] > spots[None, :]).astype(jnp.bfloat16)
    running = jnp.dot(
        earlier, owner_hot.astype(jnp.bfloat16), preferred_element_type=jnp.float32
    ).astype(jnp.int32)
    slot_rank = jnp.sum(running * owner_hot, axis=1)
    send_slot = owner_ids * capacity + slot_rank
    outgoing = jnp.full((devices * capacity,), -1, jnp.int32).at[send_slot].set(gene_row)
    outgoing = outgoing.reshape(devices, capacity)
    arrived = lax.all_to_all(outgoing, ("dp", "table"), split_axis=0, concat_axis=0, tiled=True)
    slot_count = arrived.shape[1]
    flat_ids = arrived.reshape(-1)
    row_hot = (flat_ids[:, None] == jnp.arange(table_rows, dtype=jnp.int32)[None, :]).astype(
        jnp.bfloat16
    )
    table_sum = jnp.sum(knowledge, axis=0, dtype=jnp.float32).astype(jnp.bfloat16)
    picked = jnp.dot(row_hot, table_sum, preferred_element_type=jnp.float32).astype(jnp.bfloat16)
    returned_rows = lax.all_to_all(
        picked.reshape(devices, slot_count, model_width),
        ("dp", "table"),
        split_axis=0,
        concat_axis=0,
        tiled=True,
    )
    owner_hot_rows = row_hot.reshape(devices, slot_count, table_rows)
    own_rows = returned_rows.reshape(devices * capacity, returned_rows.shape[2])[send_slot]
    gene_part = own_rows.astype(jnp.float32)
    expr_hot = (
        expr_bin[:, None] == jnp.arange(expr_table.shape[0], dtype=jnp.int32)[None, :]
    ).astype(jnp.bfloat16)
    embedded = gene_part + jnp.dot(expr_hot, expr_table, preferred_element_type=jnp.float32)
    segment, live_mask = cell_masks(cell_lengths, tok_count)
    normed1, norm1_back = jax.vjp(layer_norm, embedded, norm1_gain, norm1_bias)
    attn_in = normed1.astype(jnp.bfloat16)
    query_rows = (jnp.dot(attn_in, w_query, preferred_element_type=jnp.float32) + b_query).astype(
        jnp.bfloat16
    )
    key_rows = jnp.dot(attn_in, w_key, preferred_element_type=jnp.float32).astype(jnp.bfloat16)
    value_rows = (jnp.dot(attn_in, w_value, preferred_element_type=jnp.float32) + b_value).astype(
        jnp.bfloat16
    )
    block_rows = min(512, tok_count)
    block_count = tok_count // block_rows
    score_scale = HEAD_DIM ** (-0.5)
    key_heads = key_rows.reshape(tok_count, HEADS, HEAD_DIM)
    value_heads = value_rows.reshape(tok_count, HEADS, HEAD_DIM)
    query_blocks = query_rows.reshape(block_count, block_rows, HEADS, HEAD_DIM)
    segment_blocks = segment.reshape(block_count, block_rows)

    def block_scores(query_part, segment_part):
        scores = (
            jnp.einsum("qhd,khd->hqk", query_part, key_heads, preferred_element_type=jnp.float32)
            * score_scale
        )
        same_cell = segment_part[:, None] == segment[None, :]
        return jnp.where(same_cell[None], scores, MASKED)

    def attend_forward(inputs):
        query_part, segment_part = inputs
        scores = block_scores(query_part, segment_part)
        row_max = jnp.max(scores, axis=-1, keepdims=True)
        exp_scores = jnp.exp(scores - row_max)
        row_total = jnp.sum(exp_scores, axis=-1, keepdims=True)
        attn_probs = (exp_scores / row_total).astype(jnp.bfloat16)
        context_part = jnp.einsum(
            "hqk,khd->qhd", attn_probs, value_heads, preferred_element_type=jnp.float32
        )
        return (context_part.astype(jnp.bfloat16), row_max + jnp.log(row_total))

    context_blocks, log_totals = lax.map(attend_forward, (query_blocks, segment_blocks))
    context = context_blocks.reshape(tok_count, model_width)
    attended = jnp.dot(context, w_attn_out, preferred_element_type=jnp.float32) + b_attn_out
    hidden1 = embedded + attended
    normed2, norm2_back = jax.vjp(layer_norm, hidden1, norm2_gain, norm2_bias)
    ffn_in = normed2.astype(jnp.bfloat16)
    pre_act = jnp.dot(ffn_in, w_in, preferred_element_type=jnp.float32) + b_in
    activated, gelu_back = jax.vjp(gelu_tanh, pre_act)
    act_low = activated.astype(jnp.bfloat16)
    hidden2 = hidden1 + jnp.dot(act_low, w_out, preferred_element_type=jnp.float32) + b_out
    mixed = (hidden2 * live_mask[:, None]).astype(jnp.bfloat16)
    grad_hidden2 = cotangent.astype(jnp.float32) * live_mask[:, None]
    grad_ffn = grad_hidden2.astype(jnp.bfloat16)
    b_out_grad = jnp.sum(grad_ffn, axis=0, dtype=jnp.float32)
    w_out_grad = jnp.einsum("tf,td->fd", act_low, grad_ffn, preferred_element_type=jnp.float32)
    grad_act = jnp.einsum("td,fd->tf", grad_ffn, w_out, preferred_element_type=jnp.float32)
    grad_pre = gelu_back(grad_act)[0].astype(jnp.bfloat16)
    b_in_grad = jnp.sum(grad_pre, axis=0, dtype=jnp.float32)
    w_in_grad = jnp.einsum("td,tf->df", ffn_in, grad_pre, preferred_element_type=jnp.float32)
    grad_normed2 = jnp.einsum("tf,df->td", grad_pre, w_in, preferred_element_type=jnp.float32)
    grad_from2, norm2_gain_grad, norm2_bias_grad = norm2_back(grad_normed2)
    grad_hidden1 = grad_hidden2 + grad_from2
    grad_attn = grad_hidden1.astype(jnp.bfloat16)
    b_attn_out_grad = jnp.sum(grad_attn, axis=0, dtype=jnp.float32)
    w_attn_out_grad = jnp.einsum(
        "td,te->de", context, grad_attn, preferred_element_type=jnp.float32
    )
    grad_context = jnp.einsum(
        "te,de->td", grad_attn, w_attn_out, preferred_element_type=jnp.float32
    ).astype(jnp.bfloat16)
    grad_blocks = grad_context.reshape(block_count, block_rows, HEADS, HEAD_DIM)

    def attend_backward(carry, inputs):
        key_sum, value_sum = carry
        query_part, segment_part, log_part, grad_part = inputs
        scores = block_scores(query_part, segment_part)
        attn_probs = jnp.exp(scores - log_part)
        grad_probs = jnp.einsum(
            "qhd,khd->hqk", grad_part, value_heads, preferred_element_type=jnp.float32
        )
        value_sum = value_sum + jnp.einsum(
            "hqk,qhd->khd",
            attn_probs.astype(jnp.bfloat16),
            grad_part,
            preferred_element_type=jnp.float32,
        )
        grad_scores = attn_probs * (
            grad_probs - jnp.sum(attn_probs * grad_probs, axis=-1, keepdims=True)
        )
        grad_scores = grad_scores.astype(jnp.bfloat16)
        grad_query_part = (
            jnp.einsum("hqk,khd->qhd", grad_scores, key_heads, preferred_element_type=jnp.float32)
            * score_scale
        )
        key_sum = (
            key_sum
            + jnp.einsum(
                "hqk,qhd->khd", grad_scores, query_part, preferred_element_type=jnp.float32
            )
            * score_scale
        )
        return ((key_sum, value_sum), grad_query_part.astype(jnp.bfloat16))

    zero_heads = jnp.zeros((tok_count, HEADS, HEAD_DIM), jnp.float32)
    (key_sum, value_sum), grad_query_blocks = lax.scan(
        attend_backward,
        (zero_heads, zero_heads),
        (query_blocks, segment_blocks, log_totals, grad_blocks),
    )
    grad_query = grad_query_blocks.reshape(tok_count, model_width)
    grad_keys = key_sum.reshape(tok_count, model_width).astype(jnp.bfloat16)
    grad_values = value_sum.reshape(tok_count, model_width).astype(jnp.bfloat16)
    w_query_grad = jnp.einsum("td,te->de", attn_in, grad_query, preferred_element_type=jnp.float32)
    b_query_grad = jnp.sum(grad_query, axis=0, dtype=jnp.float32)
    w_key_grad = jnp.einsum("td,te->de", attn_in, grad_keys, preferred_element_type=jnp.float32)
    w_value_grad = jnp.einsum("td,te->de", attn_in, grad_values, preferred_element_type=jnp.float32)
    b_value_grad = jnp.sum(grad_values, axis=0, dtype=jnp.float32)
    grad_normed1 = jnp.einsum("te,de->td", grad_query, w_query, preferred_element_type=jnp.float32)
    grad_normed1 = grad_normed1 + jnp.einsum(
        "te,de->td", grad_keys, w_key, preferred_element_type=jnp.float32
    )
    grad_normed1 = grad_normed1 + jnp.einsum(
        "te,de->td", grad_values, w_value, preferred_element_type=jnp.float32
    )
    grad_from1, norm1_gain_grad, norm1_bias_grad = norm1_back(grad_normed1)
    grad_embedded = (grad_hidden1 + grad_from1).astype(jnp.bfloat16)
    expr_table_grad = jnp.einsum(
        "tb,td->bd", expr_hot, grad_embedded, preferred_element_type=jnp.float32
    )
    outgoing_grads = (
        jnp.zeros((devices * capacity, model_width), jnp.bfloat16).at[send_slot].set(grad_embedded)
    )
    arrived_grads = lax.all_to_all(
        outgoing_grads.reshape(devices, capacity, model_width),
        ("dp", "table"),
        split_axis=0,
        concat_axis=0,
        tiled=True,
    )
    table_grad = jnp.einsum(
        "gsr,gsd->rd", owner_hot_rows, arrived_grads, preferred_element_type=jnp.float32
    )
    knowledge_grad = jnp.broadcast_to(table_grad[None], (TABLES, table_rows, model_width))
    rows = lambda v: v.reshape(-1, model_width)
    small = jnp.concatenate(
        [
            expr_table_grad,
            rows(b_in_grad),
            rows(b_out_grad),
            rows(norm2_gain_grad),
            rows(norm2_bias_grad),
            rows(norm1_gain_grad),
            rows(norm1_bias_grad),
            rows(b_query_grad),
            rows(b_value_grad),
            rows(b_attn_out_grad),
        ]
    )
    half = model_width // 2

    def pack(mat):
        tall, wide = mat.shape[0] // model_width, mat.shape[1] // half
        mat = mat.astype(jnp.bfloat16).reshape(tall, model_width, wide, half)
        return mat.transpose(0, 2, 1, 3).reshape(-1, model_width, half)

    def unpack(chunks, tall, wide):
        chunks = chunks.reshape(tall, wide, model_width, half).transpose(0, 2, 1, 3)
        return chunks.reshape(tall * model_width, wide * half).astype(jnp.float32)

    small_rows = small.shape[0]
    small = small.astype(jnp.bfloat16)
    small = jnp.concatenate([small[:, :half], small[:, half:]])
    small = jnp.pad(small, ((0, model_width - small.shape[0]), (0, 0)))
    mats = [w_out_grad, w_in_grad, w_attn_out_grad, w_query_grad, w_key_grad, w_value_grad]
    packed = jnp.concatenate([pack(m) for m in mats] + [small[None]])
    count = packed.shape[0]
    side, layers = math.isqrt(lax.axis_size("dp") // 2), lax.axis_size("table")
    shard = model_width // (2 * side * layers)
    total = ar_call(count, side, layers, shard, half, [1, 3] + [2] * (2 * layers - 1) + [3, 1])(
        packed.reshape(count, 2, side, layers, shard, half)
    ).reshape(count, model_width, half)
    grads, at = [], 0
    for mat in mats:
        tall, wide = mat.shape[0] // model_width, mat.shape[1] // half
        grads.append(unpack(total[at : at + tall * wide], tall, wide))
        at += tall * wide
    small = total[count - 1, : 2 * small_rows].astype(jnp.float32)
    small = jnp.concatenate([small[:small_rows], small[small_rows:]], axis=1)
    bins, wide_rows = expr_table.shape[0], b_in.shape[0] // model_width
    tail = small[bins + wide_rows :]
    return (
        mixed,
        knowledge_grad,
        small[:bins],
        tail[3],
        tail[4],
        grads[3],
        tail[5],
        grads[4],
        grads[5],
        tail[6],
        grads[2],
        tail[7],
        tail[1],
        tail[2],
        grads[1],
        small[bins : bins + wide_rows].reshape(-1),
        grads[0],
        tail[0],
    )


def solution(mesh):
    in_specs = (
        P(None, ("dp", "table"), None),
        P(),
        P(("dp", "table"), None),
        P(("dp", "table")),
        P(("dp", "table")),
        P(("dp", "table")),
        P(),
        P(),
        P(),
        P(),
        P(),
        P(),
        P(),
        P(),
        P(),
        P(),
        P(),
        P(),
        P(),
        P(),
        P(),
        P(("dp", "table"), None),
    )
    out_specs = (
        P(("dp", "table"), None),
        P(None, ("dp", "table"), None),
        P(),
        P(),
        P(),
        P(),
        P(),
        P(),
        P(),
        P(),
        P(),
        P(),
        P(),
        P(),
        P(),
        P(),
        P(),
        P(),
    )
    return jax.shard_map(local, mesh=mesh, in_specs=in_specs, out_specs=out_specs, check_vma=False)
```

```python
import functools
import math

import jax
import jax.numpy as jnp
from jax import lax
from jax.experimental import pallas as pl
from jax.experimental.pallas import tpu as pltpu
from jax.sharding import PartitionSpec as P

HEAD_DIM = 64
PAIR = 2 * HEAD_DIM
SCALE = HEAD_DIM ** (-0.5)
LAYER_EPS = 1e-05
GELU_SLOPE = 0.7978845608028654
GELU_CUBIC = 0.044715
MASKED = -1e30
MESH = pl.DeviceIdType.MESH
BF = jnp.bfloat16
F32 = jnp.float32
DMA = pltpu.SemaphoreType.DMA


def dot(lhs, rhs, lhs_dim=1, rhs_dim=0):
    return lax.dot_general(
        lhs, rhs, (((lhs_dim,), (rhs_dim,)), ((), ())), preferred_element_type=F32
    )


def column_sum(values):
    return jnp.sum(values, axis=0, keepdims=True)


def row_mean(values):
    return jnp.mean(values, axis=1, keepdims=True)


def standardise(values):
    centred = values - row_mean(values)
    recip = lax.rsqrt(row_mean(centred * centred) + LAYER_EPS)
    return centred * recip, recip


def norm_back(xhat, recip, gain, grad):
    scaled = gain * grad
    return recip * (scaled - row_mean(scaled) - xhat * row_mean(scaled * xhat))


class Place:
    def __init__(self, side, layers):
        self.side, self.layers = side, layers
        dp = lax.axis_index("dp")
        self.z = lax.axis_index("table")
        self.a, self.b, self.core = dp // (2 * side), (dp // 2) % side, dp % 2
        self.me = dp * layers + self.z
        self.count = 2 * side * side * layers
        self.other_core = self.at(self.a, self.b, 1 - self.core, self.z)
        self.up = self.at(self.a, self.b, self.core, jnp.minimum(self.z + 1, layers - 1))
        self.down = self.at(self.a, self.b, self.core, jnp.maximum(self.z - 1, 0))

    def at(self, a, b, core, z):
        return ((a * self.side + b) * 2 + core, z)

    def flat(self, index):
        return (index // self.layers, lax.rem(index, self.layers))

    def copy(self, src, dst, send_sem, recv_sem, to):
        return pltpu.make_async_remote_copy(
            src_ref=src,
            dst_ref=dst,
            send_sem=send_sem,
            recv_sem=recv_sem,
            device_id=to,
            device_id_type=MESH,
        )

    def send(self, src, dst, send_sem, recv_sem, to):
        self.copy(src, dst, send_sem, recv_sem, to).start()

    def arrived(self, dst, recv_sem):
        self.copy(dst, dst, recv_sem, recv_sem, self.other_core).wait_recv()

    def sent(self, src, send_sem):
        self.copy(src, src, send_sem, send_sem, self.other_core).wait_send()

    def greet_all(self):
        bar = pltpu.get_barrier_semaphore()

        def greet(step, carry):
            to = self.flat(lax.rem(self.me + step, self.count))
            pl.semaphore_signal(bar, inc=1, device_id=to, device_id_type=MESH)
            return carry

        lax.fori_loop(1, self.count, greet, 0)

    def await_all(self):
        pl.semaphore_wait(pltpu.get_barrier_semaphore(), self.count - 1)

    def exchange_start(self, out, into, send_sem, recv_sems):
        def start(step, carry):
            to = lax.rem(self.me + step, self.count)
            self.send(out.at[to], into.at[self.me], send_sem, recv_sems.at[step], self.flat(to))
            return carry

        lax.fori_loop(1, self.count, start, 0)

    def exchange_wait(self, into, recv_sems):
        def wait(step, carry):
            origin = lax.rem(self.me + self.count - step, self.count)
            self.arrived(into.at[origin], recv_sems.at[step])
            return carry

        lax.fori_loop(1, self.count, wait, 0)


class Reducer:
    def __init__(self, place, part, gath, bufs, recv, sent):
        self.p = place
        self.part, self.gath = part, gath
        self.core_buf, self.first_buf, self.z_buf, self.last_buf, self.z_sum, self.final = bufs
        (
            self.core_in,
            self.first_in,
            self.z_in,
            self.last_in,
            self.own_in,
            self.z_back,
            self.first_back,
            self.core_back,
        ) = recv
        (
            self.core_out,
            self.first_out,
            self.z_out,
            self.last_out,
            self.z_ret,
            self.first_ret,
            self.core_ret,
        ) = sent
        n = place.side
        layers = place.layers
        self.stages = (
            [self.first_sum]
            + [functools.partial(self.z_step, s) for s in range(1, layers - 1)]
            + [self.z_final, self.last_sum]
            + [functools.partial(self.z_return, s) for s in range(1, layers)]
            + [self.core_return, self.finish]
        )

    def axes(self, k):
        p = self.p
        even = lax.rem(k, 2) == 0
        first = jnp.where(even, p.b, p.a)
        last = jnp.where(even, p.a, p.b)

        def first_peer(m):
            q = lax.rem(first + m, p.side)
            return q, p.at(jnp.where(even, p.a, q), jnp.where(even, q, p.b), p.core, p.z)

        def last_peer(m):
            q = lax.rem(last + m, p.side)
            return q, p.at(jnp.where(even, q, p.a), jnp.where(even, p.b, q), p.core, p.z)

        return first, last, first_peer, last_peer

    def core_send(self, k):
        p = self.p
        p.send(
            self.part.at[k, 1 - p.core],
            self.core_buf.at[k],
            self.core_out,
            self.core_in.at[k],
            p.other_core,
        )

    def core_sum(self, k):
        p = self.p
        _, _, first_peer, _ = self.axes(k)
        p.arrived(self.core_buf.at[k], self.core_in.at[k])
        self.core_buf[k] = (
            self.core_buf[k].astype(F32) + self.part[k, p.core].astype(F32)
        ).astype(BF)
        for m in range(1, p.side):
            q, to = first_peer(m)
            p.send(
                self.core_buf.at[k, q],
                self.first_buf.at[k, m - 1],
                self.first_out,
                self.first_in.at[k, m - 1],
                to,
            )

    def first_sum(self, k):
        p = self.p
        first, _, _, _ = self.axes(k)
        for m in range(1, p.side):
            p.arrived(self.first_buf.at[k, m - 1], self.first_in.at[k, m - 1])
        total = self.core_buf[k, first].astype(F32)
        for m in range(1, p.side):
            total = total + self.first_buf[k, m - 1].astype(F32)
        self.first_buf[k, 0] = total.astype(BF)
        top = p.layers - 1

        @pl.when(p.z == 0)
        def _():
            for j in range(top, 0, -1):
                slot = j if j > 1 else p.layers
                p.send(
                    self.first_buf.at[k, 0, j],
                    self.z_buf.at[k, slot],
                    self.z_out,
                    self.z_in.at[k, slot],
                    p.up,
                )

        @pl.when(p.z == top)
        def _():
            for j in range(0, top):
                p.send(
                    self.first_buf.at[k, 0, j],
                    self.z_buf.at[k, j],
                    self.z_out,
                    self.z_in.at[k, j],
                    p.down,
                )

    def z_add(self, k, j):
        self.p.arrived(self.z_buf.at[k, j], self.z_in.at[k, j])
        self.z_buf[k, j] = (
            self.z_buf[k, j].astype(F32) + self.first_buf[k, 0, j].astype(F32)
        ).astype(BF)

    def z_step(self, s, k):
        p = self.p
        top = p.layers - 1

        @pl.when(p.z == s)
        def _():
            for j in range(top, s, -1):
                self.z_add(k, j)
                slot = j if j > s + 1 else p.layers
                p.send(
                    self.z_buf.at[k, j],
                    self.z_buf.at[k, slot],
                    self.z_out,
                    self.z_in.at[k, slot],
                    p.up,
                )

        @pl.when(p.z == top - s)
        def _():
            for j in range(0, top - s):
                self.z_add(k, j)
                p.send(
                    self.z_buf.at[k, j],
                    self.z_buf.at[k, j],
                    self.z_out,
                    self.z_in.at[k, j],
                    p.down,
                )

    def z_final(self, k):
        p = self.p
        top = p.layers - 1
        _, _, _, last_peer = self.axes(k)

        def arrival(slot):
            p.arrived(self.z_buf.at[k, slot], self.z_in.at[k, slot])
            return self.z_buf[k, slot].astype(F32)

        own = self.first_buf[k, 0, p.z].astype(F32)

        @pl.when(p.z == 0)
        def _():
            self.z_sum[k] = (own + arrival(0)).astype(BF)

        @pl.when(p.z == top)
        def _():
            self.z_sum[k] = (own + arrival(p.layers)).astype(BF)

        @pl.when((p.z > 0) & (p.z < top))
        def _():
            self.z_sum[k] = (own + arrival(p.layers) + arrival(p.z)).astype(BF)

        for m in range(1, p.side):
            _, to = last_peer(m)
            p.send(
                self.z_sum.at[k],
                self.last_buf.at[k, m - 1],
                self.last_out,
                self.last_in.at[k, m - 1],
                to,
            )

    def last_sum(self, k):
        p = self.p
        first, last, _, _ = self.axes(k)
        for m in range(1, p.side):
            p.arrived(self.last_buf.at[k, m - 1], self.last_in.at[k, m - 1])
        total = None
        for q in range(p.side):
            m = lax.rem(last - q + p.side, p.side)
            term = jnp.where(
                m == 0,
                self.z_sum[k].astype(F32),
                self.last_buf[k, jnp.maximum(m - 1, 0)].astype(F32),
            )
            total = term if total is None else total + term
        self.final[k] = total.astype(BF)
        own = self.final.at[k]
        there = self.gath.at[k, p.core, first, p.z]
        pltpu.make_async_copy(own, there, self.own_in.at[k]).start()

        @pl.when(p.z < p.layers - 1)
        def _():
            p.send(own, there, self.z_ret, self.z_back.at[k, p.z], p.up)

        @pl.when(p.z > 0)
        def _():
            p.send(own, there, self.z_ret, self.z_back.at[k, p.z], p.down)

    def z_return(self, s, k):
        p = self.p
        first, _, first_peer, _ = self.axes(k)
        top = p.layers - 1

        @pl.when(p.z >= s)
        def _():
            j = jnp.maximum(p.z - s, 0)
            shard = self.gath.at[k, p.core, first, j]
            p.arrived(shard, self.z_back.at[k, j])

            @pl.when(p.z < top)
            def _():
                p.send(shard, shard, self.z_ret, self.z_back.at[k, j], p.up)

        @pl.when(p.z <= top - s)
        def _():
            j = jnp.minimum(p.z + s, top)
            shard = self.gath.at[k, p.core, first, j]
            p.arrived(shard, self.z_back.at[k, j])

            @pl.when(p.z > 0)
            def _():
                p.send(shard, shard, self.z_ret, self.z_back.at[k, j], p.down)

        if s == top:
            own = self.final.at[k]
            pltpu.make_async_copy(
                own, self.gath.at[k, p.core, first, p.z], self.own_in.at[k]
            ).wait()
            mine = self.gath.at[k, p.core, first]
            for m in range(1, p.side):
                _, to = first_peer(m)
                p.send(mine, mine, self.first_ret, self.first_back.at[k, m - 1], to)

    def core_return(self, k):
        p = self.p
        first, _, _, _ = self.axes(k)
        for m in range(1, p.side):
            q = lax.rem(first - m + p.side, p.side)
            p.arrived(self.gath.at[k, p.core, q], self.first_back.at[k, m - 1])
        mine = self.gath.at[k, p.core]
        p.send(mine, mine, self.core_ret, self.core_back.at[k], p.other_core)

    def finish(self, k):
        p = self.p
        p.arrived(self.gath.at[k, 1 - p.core], self.core_back.at[k])

    def drain(self):
        p = self.p
        p.sent(self.core_buf, self.core_out)
        p.sent(self.first_buf, self.first_out)
        p.sent(self.z_buf.at[:, pl.ds(0, p.layers - 1)], self.z_out)
        p.sent(self.last_buf, self.last_out)
        middle = (p.z > 0) & (p.z < p.layers - 1)

        @pl.when(middle)
        def _():
            p.sent(self.z_buf, self.z_ret)

        @pl.when(jnp.logical_not(middle))
        def _():
            p.sent(self.z_buf.at[:, pl.ds(0, 1)], self.z_ret)

        p.sent(self.first_buf, self.first_ret)
        p.sent(self.core_buf, self.core_ret)


def reducer_scratch(count, side, layers, rows, wide):
    bufs = [
        pltpu.VMEM((count, side, layers, rows, wide), BF),
        pltpu.VMEM((count, side - 1, layers, rows, wide), BF),
        pltpu.VMEM((count, layers + 1, rows, wide), BF),
        pltpu.VMEM((count, side - 1, rows, wide), BF),
        pltpu.VMEM((count, rows, wide), BF),
        pltpu.VMEM((count, rows, wide), BF),
    ]
    recv = [
        DMA((count,)),
        DMA((count, side - 1)),
        DMA((count, layers + 1)),
        DMA((count, side - 1)),
        DMA((count,)),
        DMA((count, layers)),
        DMA((count, side - 1)),
        DMA((count,)),
    ]
    return bufs, recv, [DMA(())] * 7


def layer_kernel(cfg, *refs):
    refs = list(refs)

    def take(number):
        taken = refs[:number]
        del refs[:number]
        return taken

    (knowledge, expr_table, owner_ids, gene_row, expr_bin, lengths) = take(6)
    (gain1, bias1, w_query, b_query, w_key, w_value, b_value, w_out1, b_out1) = take(9)
    (gain2, bias2, w_in, b_in, w_out, b_out, cotangent) = take(7)
    mixed, table_grad, gath = take(3)
    know_v, wq_v, wk_v, wv_v, wo_v, win_v, wout_v, cot_v = take(8)
    load_sems, ids_out, ids_in, rows_out, rows_in, back_in, row_hot_v, slot_hot_v = take(8)
    ids_sem, rows_sem, ids_sent, rows_sent, back_sent = take(5)
    (embedded_v, attn_in_v, query_v, key_v, value_v, probs_v, context_v) = take(7)
    (hidden1_v, ffn_in_v, grad_ffn_v, acc_v, gn2_v, biases_v) = take(6)
    (part,) = take(1)
    bufs, recv, sent = take(6), take(8), take(7)
    assert not refs

    side, layers, cap, offsets = cfg
    place = Place(side, layers)
    devices = place.count
    red = Reducer(place, part, gath, bufs, recv, sent)
    tokens, width = embedded_v.shape
    table_rows = knowledge.shape[1]
    half = width // 2
    blocks = w_in.shape[1] // width
    count = part.shape[0]
    slots = devices * cap

    loads = [
        (knowledge, know_v),
        (w_query, wq_v),
        (w_key, wk_v),
        (w_value, wv_v),
        (w_out1, wo_v),
        (cotangent, cot_v),
    ]
    for j in range(blocks):
        loads.append((w_in.at[:, pl.ds(j * width, width)], win_v.at[j % 2]))
        loads.append((w_out.at[pl.ds(j * width, width)], wout_v.at[j % 2]))
    loads = [
        pltpu.make_async_copy(src, dst, load_sems.at[i]) for i, (src, dst) in enumerate(loads)
    ]
    for load in loads[: 6 + 4]:
        load.start()
    place.greet_all()

    def iota(shape, dim):
        return lax.broadcasted_iota(jnp.int32, shape, dim)

    def hot(condition):
        return jnp.where(condition, 1.0, 0.0).astype(BF)

    owner_row = owner_ids[...]
    owner_hot = hot(iota((devices, tokens), 0) == owner_row)
    earlier = hot(iota((tokens, tokens), 0) < iota((tokens, tokens), 1))
    before = dot(owner_hot, earlier)
    rank_row = column_sum(before * owner_hot.astype(F32)).astype(jnp.int32)
    slot_hot_v[...] = hot(iota((slots, tokens), 0) == owner_row * cap + rank_row)
    rank_hot = hot(iota((128, tokens), 0) == rank_row)
    named = (owner_hot.astype(F32) * (gene_row[...] + 1).astype(F32)).astype(BF)
    wanted = dot(named, rank_hot, 1, 1)
    for d in range(devices):
        ids_out[d] = wanted[d : d + 1]

    place.await_all()
    place.exchange_start(ids_out, ids_in, ids_sent, ids_sem)
    ids_in[place.me] = ids_out[place.me]
    loads[0].wait()
    table_sum = know_v[0].astype(F32)
    for k in range(1, know_v.shape[0]):
        table_sum = table_sum + know_v[k].astype(F32)
    table_sum = table_sum.astype(BF)
    expr_hot = hot(iota((expr_table.shape[0], tokens), 0) == expr_bin[...])
    expr_part = dot(expr_hot, expr_table[...], 0, 0)
    place.exchange_wait(ids_in, ids_sem)
    asked = ids_in[...].reshape(devices, 128).astype(BF)
    spread = hot(iota((slots, devices), 0) // cap == iota((slots, devices), 1))
    asked = dot(spread, asked)
    own_lane = lax.rem(iota((slots, 128), 0), cap) == iota((slots, 128), 1)
    asked = jnp.sum(jnp.where(own_lane, asked, 0.0), axis=1, keepdims=True)
    row_hot = hot(iota((slots, table_rows), 1) + 1 == asked.astype(jnp.int32))
    row_hot_v[...] = row_hot
    rows_out[...] = dot(row_hot, table_sum).astype(BF).reshape(devices, cap, width)
    place.exchange_start(rows_out, rows_in, rows_sent, rows_sem)
    rows_in[place.me] = rows_out[place.me]

    end = lengths[0]
    ends = [end]
    for c in range(1, lengths.shape[0]):
        end = end + lengths[c]
        ends.append(end)

    def segments(shape, dim):
        spot = iota(shape, dim)
        segment = jnp.zeros(shape, jnp.int32)
        for stop in ends:
            segment = segment + jnp.where(spot >= stop, 1, 0)
        return segment

    spot = lax.rem(iota((2 * tokens, tokens), 0), tokens)
    segment = jnp.zeros((2 * tokens, tokens), jnp.int32)
    for stop in ends:
        segment = segment + jnp.where(spot >= stop, 1, 0)
    same_cell = segment == segments((2 * tokens, tokens), 1)
    live = jnp.where(iota((tokens, 1), 0) < ends[-1], 1.0, 0.0)

    place.exchange_wait(rows_in, rows_sem)
    gathered = rows_in[...].reshape(slots, width)
    embedded_v[...] = dot(slot_hot_v[...], gathered, 0, 0) + expr_part
    for load in loads[1:5]:
        load.wait()

    xhat1, recip1 = standardise(embedded_v[...])
    attn_in_v[...] = (xhat1 * gain1[...].reshape(1, width) + bias1[...].reshape(1, width)).astype(BF)
    query_v[...] = (dot(attn_in_v[...], wq_v[...]) + b_query[...].reshape(1, width)).astype(BF)
    key_v[...] = dot(attn_in_v[...], wk_v[...]).astype(BF)
    value_v[...] = (dot(attn_in_v[...], wv_v[...]) + b_value[...].reshape(1, width)).astype(BF)
    low_lane = iota((tokens, PAIR), 1) < HEAD_DIM

    def two_heads(values):
        zero = jnp.zeros_like(values)
        return jnp.concatenate(
            [jnp.where(low_lane, values, zero), jnp.where(low_lane, zero, values)], axis=0
        )

    def one_of_two(values):
        return jnp.where(low_lane, values[:tokens], values[tokens:])

    for pair in range(width // PAIR):
        lanes = slice(pair * PAIR, (pair + 1) * PAIR)
        scores = dot(two_heads(query_v[:, lanes]), key_v[:, lanes], 1, 1) * SCALE
        scores = jnp.where(same_cell, scores, MASKED)
        scores = jnp.exp(scores - jnp.max(scores, axis=1, keepdims=True))
        probs = scores / jnp.sum(scores, axis=1, keepdims=True)
        probs_v[pair] = probs
        context_v[:, lanes] = one_of_two(dot(probs.astype(BF), value_v[:, lanes])).astype(BF)
    hidden1_v[...] = (
        embedded_v[...] + dot(context_v[...], wo_v[...]) + b_out1[...].reshape(1, width)
    )
    loads[5].wait()

    xhat2, recip2 = standardise(hidden1_v[...])
    ffn_in_v[...] = (xhat2 * gain2[...].reshape(1, width) + bias2[...].reshape(1, width)).astype(BF)
    grad_hidden2 = cot_v[...].astype(F32) * live
    grad_ffn_v[...] = grad_hidden2.astype(BF)
    acc_v[...] = jnp.zeros_like(acc_v)
    gn2_v[...] = jnp.zeros_like(gn2_v)
    biases_v[...] = jnp.zeros_like(biases_v)
    shard = part.shape[1:]

    def put(k, values):
        part[k] = values.reshape(shard).astype(BF)
        red.core_send(k)

    def put_bias(row, values):
        biases_v[pl.ds(2 * row, 1), :] = values[:, :half]
        biases_v[pl.ds(2 * row + 1, 1), :] = values[:, half:]

    for j in range(blocks):
        loads[6 + 2 * j].wait()
        loads[7 + 2 * j].wait()
        win, wout = win_v.at[j % 2], wout_v.at[j % 2]
        pre = dot(ffn_in_v[...], win[...]) + b_in[pl.ds(j * width, width)].reshape(1, width)
        square = pre * pre
        bend = jnp.tanh(GELU_SLOPE * (pre + GELU_CUBIC * square * pre))
        act = (0.5 * pre * (1.0 + bend)).astype(BF)
        slope = 0.5 * (1.0 + bend) + 0.5 * pre * (1.0 - bend * bend) * (
            GELU_SLOPE * (1.0 + 3.0 * GELU_CUBIC * square)
        )
        grad_pre = dot(grad_ffn_v[...], wout[...], 1, 1) * slope
        grad_pre = grad_pre.astype(BF)
        for h in range(2):
            put(4 * j + h, dot(act, grad_ffn_v[:, h * half : (h + 1) * half], 0, 0))
        for h in range(2):
            put(4 * j + 2 + h, dot(ffn_in_v[...], grad_pre[:, h * half : (h + 1) * half], 0, 0))
        acc_v[...] += dot(act, wout[...])
        gn2_v[...] += dot(grad_pre, win[...], 1, 1)
        if j + 2 < blocks:
            loads[10 + 2 * j].start()
            loads[11 + 2 * j].start()
        put_bias(j, column_sum(grad_pre.astype(F32)))
        if j:
            for q in range(4):
                red.core_sum(4 * (j - 1) + q)
    at = 4 * blocks
    mixed[...] = (
        (hidden1_v[...] + acc_v[...] + b_out[...].reshape(1, width)) * live
    ).astype(BF)
    put_bias(blocks, column_sum(grad_ffn_v[...].astype(F32)))
    grad_normed2 = gn2_v[...]
    put_bias(blocks + 1, column_sum(grad_normed2 * xhat2))
    put_bias(blocks + 2, column_sum(grad_normed2))
    for q in range(4):
        red.core_sum(at - 4 + q)
    grad_hidden1 = grad_hidden2 + norm_back(xhat2, recip2, gain2[...].reshape(1, width), grad_normed2)
    acc_v[...] = grad_hidden1
    grad_attn = grad_hidden1.astype(BF)
    put_bias(blocks + 3, column_sum(grad_attn.astype(F32)))
    for h in range(2):
        put(at + h, dot(context_v[...], grad_attn[:, h * half : (h + 1) * half], 0, 0))
    gctx_v = ffn_in_v
    gctx_v[...] = dot(grad_attn, wo_v[...], 1, 1).astype(BF)
    gq_v, gk_v, gv_v = query_v, key_v, value_v

    for pair in range(width // PAIR):
        lanes = slice(pair * PAIR, (pair + 1) * PAIR)
        probs = probs_v[pair]
        grads = two_heads(gctx_v[:, lanes])
        grad_probs = dot(grads, value_v[:, lanes], 1, 1)
        inner = jnp.sum(probs * grad_probs, axis=1, keepdims=True)
        grad_scores = (probs * (grad_probs - inner)).astype(BF)
        grad_query = one_of_two(dot(grad_scores, key_v[:, lanes])) * SCALE
        grad_key = dot(grad_scores, two_heads(query_v[:, lanes]), 0, 0) * SCALE
        gq_v[:, lanes] = grad_query.astype(BF)
        gk_v[:, lanes] = grad_key.astype(BF)
        gv_v[:, lanes] = dot(probs.astype(BF), grads, 0, 0).astype(BF)
    for q in range(2):
        red.core_sum(at + q)
    at += 2
    for grad in (gq_v, gk_v, gv_v):
        for h in range(2):
            put(at + h, dot(attn_in_v[...], grad[:, h * half : (h + 1) * half], 0, 0))
        at += 2
    put_bias(blocks + 4, column_sum(gq_v[...].astype(F32)))
    put_bias(blocks + 5, column_sum(gv_v[...].astype(F32)))
    grad_normed1 = dot(gq_v[...], wq_v[...], 1, 1)
    grad_normed1 = grad_normed1 + dot(gk_v[...], wk_v[...], 1, 1)
    grad_normed1 = grad_normed1 + dot(gv_v[...], wv_v[...], 1, 1)
    xhat1, recip1 = standardise(embedded_v[...])
    put_bias(blocks + 6, column_sum(grad_normed1 * xhat1))
    put_bias(blocks + 7, column_sum(grad_normed1))
    grad_embedded = acc_v[...] + norm_back(
        xhat1, recip1, gain1[...].reshape(1, width), grad_normed1
    )
    grad_embedded = grad_embedded.astype(BF)
    back_out = rows_out
    place.sent(rows_out.at[pl.ds(0, devices - 1)], rows_sent)
    back_out[...] = dot(slot_hot_v[...], grad_embedded).astype(BF).reshape(devices, cap, width)
    expr_grad = dot(expr_hot, grad_embedded)
    bins = expr_grad.shape[0]
    filler = jnp.zeros((width - 2 * bins - biases_v.shape[0], half), F32)
    put(
        at,
        jnp.concatenate([expr_grad[:, :half], expr_grad[:, half:], biases_v[...], filler], axis=0),
    )
    place.exchange_start(back_out, back_in, back_sent, ids_sem)
    back_in[place.me] = back_out[place.me]
    for k in range(at - 6, at + 1):
        red.core_sum(k)

    reach = [0]
    for offset in offsets:
        reach.append(reach[-1] + offset)
    assert len(reach) == len(red.stages)

    def step(i, carry):
        for stage, lag in reversed(list(zip(red.stages, reach))):
            k = i - lag

            @pl.when((k >= 0) & (k < count))
            def _():
                stage(k)

        return carry

    lax.fori_loop(0, count + reach[-1], step, 0)
    place.exchange_wait(back_in, ids_sem)
    table_grad[...] = dot(row_hot_v[...], back_in[...].reshape(slots, width), 0, 0)
    place.sent(ids_out.at[pl.ds(0, devices - 1)], ids_sent)
    place.sent(back_out.at[pl.ds(0, devices - 1)], back_sent)
    red.drain()


def layer(side, layers, args):
    (knowledge, expr_table, gene_owner, gene_row, expr_bin, cell_lengths) = args[:6]
    cotangent, w_in = args[21], args[17]
    tokens, width = cotangent.shape
    devices = 2 * side * side * layers
    cap = max(8, 2 * tokens // devices)
    slots = devices * cap
    table_rows = knowledge.shape[1]
    blocks = w_in.shape[1] // width
    count = 4 * blocks + 9
    half = width // 2
    shard = width // (2 * side * layers)
    whole = (count, 2, side, layers, shard, half)
    bufs, recv, sent = reducer_scratch(count, side, layers, shard, half)
    wide = lambda dtype: pltpu.VMEM((tokens, width), dtype)
    square = pltpu.VMEM((width, width), BF)
    scratch = [
        pltpu.VMEM(knowledge.shape, BF),
        square,
        square,
        square,
        square,
        pltpu.VMEM((2, width, width), BF),
        pltpu.VMEM((2, width, width), BF),
        wide(BF),
        DMA((6 + 2 * blocks,)),
        pltpu.VMEM((devices, 1, 128), F32),
        pltpu.VMEM((devices, 1, 128), F32),
        pltpu.VMEM((devices, cap, width), BF),
        pltpu.VMEM((devices, cap, width), BF),
        pltpu.VMEM((devices, cap, width), BF),
        pltpu.VMEM((slots, table_rows), BF),
        pltpu.VMEM((slots, tokens), BF),
        DMA((devices,)),
        DMA((devices,)),
        DMA(()),
        DMA(()),
        DMA(()),
        wide(F32),
        wide(BF),
        wide(BF),
        wide(BF),
        wide(BF),
        pltpu.VMEM((width // PAIR, 2 * tokens, tokens), F32),
        wide(BF),
        wide(F32),
        wide(BF),
        wide(BF),
        wide(F32),
        wide(F32),
        pltpu.VMEM((8 * ((2 * (blocks + 8) + 7) // 8), half), F32),
        pltpu.VMEM(whole, BF),
    ]
    vmem = pl.BlockSpec(memory_space=pltpu.VMEM)
    hbm = pl.BlockSpec(memory_space=pl.ANY)
    smem = pl.BlockSpec(memory_space=pltpu.SMEM)
    in_hbm = {0, 8, 10, 11, 13, 17, 19, 21}
    specs = [hbm if i in in_hbm else smem if i == 5 else vmem for i in range(22)]
    offsets = OFFSETS
    flops = 2 * tokens * (3 * (4 * width * width + 2 * width * w_in.shape[1]))
    return pl.pallas_call(
        functools.partial(layer_kernel, (side, layers, cap, offsets)),
        out_shape=(
            jax.ShapeDtypeStruct((tokens, width), BF),
            jax.ShapeDtypeStruct((table_rows, width), F32),
            jax.ShapeDtypeStruct(whole, BF),
        ),
        in_specs=specs,
        out_specs=(vmem, vmem, hbm),
        scratch_shapes=scratch + bufs + recv + sent,
        compiler_params=pltpu.CompilerParams(
            collective_id=1, has_side_effects=True, vmem_limit_bytes=VMEM_BYTES
        ),
        cost_estimate=pl.CostEstimate(flops=flops, bytes_accessed=40 << 20, transcendentals=0),
    )(
        knowledge,
        expr_table,
        gene_owner.reshape(1, tokens),
        gene_row.reshape(1, tokens),
        expr_bin.reshape(1, tokens),
        *args[5:],
    )


OFFSETS = [2, 2, 2, 2, 2, 2, 2, 3, 1]
VMEM_BYTES = 62 << 20
DEPTH = 4


def spread_kernel(gath, table_grad, *refs):
    (know_out, expr_out, gain1_out, bias1_out, wq_out, bq_out, wk_out, wv_out, bv_out) = refs[:9]
    (wo_out, bo1_out, gain2_out, bias2_out, win_out, bin_out, wout_out, bout_out) = refs[9:17]
    narrow, broad, in_sems, out_sems, know_sems = refs[17:]
    count, width, half = gath.shape
    blocks = win_out.shape[1] // width
    places = []
    for j in range(blocks):
        rows = pl.ds(j * width, width)
        for h in range(2):
            places.append(wout_out.at[rows, pl.ds(h * half, half)])
        for h in range(2):
            places.append(win_out.at[:, pl.ds(j * width + h * half, half)])
    for out in (wo_out, wq_out, wk_out, wv_out):
        for h in range(2):
            places.append(out.at[:, pl.ds(h * half, half)])
    assert len(places) == count - 1

    def fetch(k):
        return pltpu.make_async_copy(gath.at[k], narrow.at[k % DEPTH], in_sems.at[k % DEPTH])

    def store(k):
        return pltpu.make_async_copy(broad.at[k % DEPTH], places[k], out_sems.at[k % DEPTH])

    for k in range(DEPTH - 1):
        fetch(k).start()
    knows = [
        pltpu.make_async_copy(table_grad, know_out.at[i], know_sems.at[i])
        for i in range(know_out.shape[0])
    ]
    for know in knows:
        know.start()
    for k in range(count):
        if k + DEPTH - 1 < count:
            fetch(k + DEPTH - 1).start()
        fetch(k).wait()
        if k == count - 1:
            break
        if k >= DEPTH:
            store(k - DEPTH).wait()
        broad[k % DEPTH] = narrow[k % DEPTH].astype(F32)
        store(k).start()
    small = narrow.at[(count - 1) % DEPTH]
    bins = expr_out.shape[0]
    expr_out[:, :half] = small[pl.ds(0, bins), :].astype(F32)
    expr_out[:, half:] = small[pl.ds(bins, bins), :].astype(F32)
    biases = small[pl.ds(2 * bins, 8 * ((2 * (blocks + 8) + 7) // 8)), :].astype(F32)

    def bias(i):
        return jnp.concatenate([biases[2 * i : 2 * i + 1], biases[2 * i + 1 : 2 * i + 2]], axis=1)[0]

    for j in range(blocks):
        bin_out[pl.ds(j * width, width)] = bias(j)
    for i, out in enumerate(
        (bout_out, gain2_out, bias2_out, bo1_out, bq_out, bv_out, gain1_out, bias1_out)
    ):
        out[...] = bias(blocks + i)
    for k in range(max(0, count - 1 - DEPTH), count - 1):
        store(k).wait()
    for know in knows:
        know.wait()


def spread(gath, table_grad, tables, bins, hidden):
    count, width, half = gath.shape
    shape = lambda *dims: jax.ShapeDtypeStruct(dims, F32)
    vector, square = shape(width), shape(width, width)
    vmem = pl.BlockSpec(memory_space=pltpu.VMEM)
    hbm = pl.BlockSpec(memory_space=pl.ANY)
    outs = (
        (shape(tables, *table_grad.shape), hbm),
        (shape(bins, width), vmem),
        (vector, vmem),
        (vector, vmem),
        (square, hbm),
        (vector, vmem),
        (square, hbm),
        (square, hbm),
        (vector, vmem),
        (square, hbm),
        (vector, vmem),
        (vector, vmem),
        (vector, vmem),
        (shape(width, hidden), hbm),
        (shape(hidden), vmem),
        (shape(hidden, width), hbm),
        (vector, vmem),
    )
    return pl.pallas_call(
        spread_kernel,
        out_shape=tuple(out for out, _ in outs),
        in_specs=[pl.BlockSpec(memory_space=pltpu.HBM), vmem],
        out_specs=tuple(spec for _, spec in outs),
        scratch_shapes=[
            pltpu.VMEM((DEPTH, width, half), BF),
            pltpu.VMEM((DEPTH, width, half), F32),
            DMA((DEPTH,)),
            DMA((DEPTH,)),
            DMA((tables,)),
        ],
        compiler_params=pltpu.CompilerParams(vmem_limit_bytes=56 << 20),
        cost_estimate=pl.CostEstimate(flops=0, bytes_accessed=48 << 20, transcendentals=0),
    )(gath, table_grad)


def local(*args):
    layers = lax.axis_size("table")
    side = math.isqrt(lax.axis_size("dp") // 2)
    knowledge, expr_table, w_in = args[0], args[1], args[17]
    width, hidden = w_in.shape
    mixed, table_grad, total = layer(side, layers, args)
    total = total.reshape(-1, width, width // 2)
    return (mixed, *spread(total, table_grad, knowledge.shape[0], expr_table.shape[0], hidden))


def solution(mesh):
    rows = P(("dp", "table"))
    by_token = P(("dp", "table"), None)
    by_row = P(None, ("dp", "table"), None)
    in_specs = (by_row, P(), by_token, rows, rows, rows) + (P(),) * 15 + (by_token,)
    out_specs = (by_token, by_row) + (P(),) * 16
    return jax.shard_map(local, mesh=mesh, in_specs=in_specs, out_specs=out_specs, check_vma=False)
```

```python
import functools
import math

import jax
import jax.numpy as jnp
from jax import lax
from jax.experimental import pallas as pl
from jax.experimental.pallas import tpu as pltpu
from jax.sharding import PartitionSpec as P

HEAD_DIM = 64
PAIR = 2 * HEAD_DIM
SCALE = HEAD_DIM ** (-0.5)
LAYER_EPS = 1e-05
GELU_SLOPE = 0.7978845608028654
GELU_CUBIC = 0.044715
MASKED = -1e30
MESH = pl.DeviceIdType.MESH
BF = jnp.bfloat16
F32 = jnp.float32
DMA = pltpu.SemaphoreType.DMA


def dot(lhs, rhs, lhs_dim=1, rhs_dim=0):
    return lax.dot_general(
        lhs, rhs, (((lhs_dim,), (rhs_dim,)), ((), ())), preferred_element_type=F32
    )


def column_sum(values):
    return jnp.sum(values, axis=0, keepdims=True)


def row_mean(values):
    return jnp.mean(values, axis=1, keepdims=True)


def standardise(values):
    centred = values - row_mean(values)
    recip = lax.rsqrt(row_mean(centred * centred) + LAYER_EPS)
    return centred * recip, recip


def norm_back(xhat, recip, gain, grad):
    scaled = gain * grad
    return recip * (scaled - row_mean(scaled) - xhat * row_mean(scaled * xhat))


class Place:
    def __init__(self, side, layers):
        self.side, self.layers = side, layers
        dp = lax.axis_index("dp")
        self.z = lax.axis_index("table")
        self.a, self.b, self.core = dp // (2 * side), (dp // 2) % side, dp % 2
        self.me = dp * layers + self.z
        self.count = 2 * side * side * layers
        self.other_core = self.at(self.a, self.b, 1 - self.core, self.z)
        self.up = self.at(self.a, self.b, self.core, jnp.minimum(self.z + 1, layers - 1))
        self.down = self.at(self.a, self.b, self.core, jnp.maximum(self.z - 1, 0))

    def at(self, a, b, core, z):
        return ((a * self.side + b) * 2 + core, z)

    def flat(self, index):
        return (index // self.layers, lax.rem(index, self.layers))

    def copy(self, src, dst, send_sem, recv_sem, to):
        return pltpu.make_async_remote_copy(
            src_ref=src,
            dst_ref=dst,
            send_sem=send_sem,
            recv_sem=recv_sem,
            device_id=to,
            device_id_type=MESH,
        )

    def send(self, src, dst, send_sem, recv_sem, to):
        self.copy(src, dst, send_sem, recv_sem, to).start()

    def arrived(self, dst, recv_sem):
        self.copy(dst, dst, recv_sem, recv_sem, self.other_core).wait_recv()

    def sent(self, src, send_sem):
        self.copy(src, src, send_sem, send_sem, self.other_core).wait_send()

    def each_other(self, act):
        layers = self.layers
        for dz in sorted(range(layers), key=lambda d: -min(d, layers - d)):

            def one(i, carry):
                act(i * layers + dz)
                return carry

            lax.fori_loop(0 if dz else 1, self.count // layers, one, 0)

    def greet_all(self):
        bar = pltpu.get_barrier_semaphore()

        def greet(step):
            to = self.flat(lax.rem(self.me + step, self.count))
            pl.semaphore_signal(bar, inc=1, device_id=to, device_id_type=MESH)

        self.each_other(greet)

    def await_all(self):
        pl.semaphore_wait(pltpu.get_barrier_semaphore(), self.count - 1)

    def exchange_start(self, out, into, send_sem, recv_sems):
        def start(step):
            to = lax.rem(self.me + step, self.count)
            self.send(out.at[to], into.at[self.me], send_sem, recv_sems.at[step], self.flat(to))

        self.each_other(start)

    def exchange_wait(self, into, recv_sems):
        def wait(step):
            origin = lax.rem(self.me + self.count - step, self.count)
            self.arrived(into.at[origin], recv_sems.at[step])

        self.each_other(wait)


class Reducer:
    def __init__(self, place, part, gath, bufs, recv, sent):
        self.p = place
        self.part, self.gath = part, gath
        self.core_buf, self.first_buf, self.z_buf, self.last_buf, self.z_sum, self.final = bufs
        self.core_in, self.first_in, self.z_in, self.last_in, self.own_in = recv[:5]
        self.z_back, self.first_back, self.core_back, self.last_back = recv[5:]
        self.core_out, self.first_out, self.first_ret, self.core_ret = sent[:4]
        self.z_out, self.z_ret, self.last_out, self.slim_out, self.slim_ret = sent[4:]
        layers = place.layers
        self.count = part.shape[0]
        self.slims = SLIM // place.side * place.side
        bind = functools.partial
        steps, returns = range(1, layers - 1), range(1, layers)
        self.wide_stages = (
            [self.first_sum]
            + [bind(self.z_step, s) for s in steps]
            + [self.z_final, self.last_sum]
            + [bind(self.z_return, s) for s in returns[:-1]]
            + [self.wide_z_return, self.core_return, self.finish]
        )
        self.slim_stages = (
            [self.slim_first_sum, self.slim_last_sum]
            + [self.of_own(bind(self.z_step, s)) for s in steps]
            + [self.slim_z_final]
            + [self.of_own(bind(self.z_return, s)) for s in returns[:-1]]
            + [self.slim_z_return, self.slim_last_return, self.slim_core_return, self.slim_finish]
        )

    def axes(self, k):
        p = self.p
        if isinstance(k, int):
            even = (k // p.side if k < self.slims else k) % 2 == 0
        else:
            even = lax.rem(jnp.where(k < self.slims, k // p.side, k), 2) == 0
        first = jnp.where(even, p.b, p.a)
        last = jnp.where(even, p.a, p.b)

        def first_peer(m):
            q = lax.rem(first + m, p.side)
            return q, p.at(jnp.where(even, p.a, q), jnp.where(even, q, p.b), p.core, p.z)

        def last_peer(m):
            q = lax.rem(last + m, p.side)
            return q, p.at(jnp.where(even, q, p.a), jnp.where(even, p.b, q), p.core, p.z)

        return first, last, first_peer, last_peer

    def before(self, position, m):
        return lax.rem(position - m + self.p.side, self.p.side)

    def of_own(self, act):
        return lambda base: act(base + self.axes(base)[1])

    def core_send(self, k):
        p = self.p
        p.send(
            self.part.at[k, 1 - p.core],
            self.core_buf.at[k],
            self.core_out,
            self.core_in.at[k],
            p.other_core,
        )

    def core_sum(self, k):
        p = self.p
        _, _, first_peer, _ = self.axes(k)
        p.arrived(self.core_buf.at[k], self.core_in.at[k])
        self.core_buf[k] = (
            self.core_buf[k].astype(F32) + self.part[k, p.core].astype(F32)
        ).astype(BF)
        for m in range(1, p.side):
            q, to = first_peer(m)
            p.send(
                self.core_buf.at[k, q],
                self.first_buf.at[k, m - 1],
                self.first_out,
                self.first_in.at[k, m - 1],
                to,
            )

    def add_first(self, k):
        p = self.p
        first, _, _, _ = self.axes(k)
        for m in range(1, p.side):
            p.arrived(self.first_buf.at[k, m - 1], self.first_in.at[k, m - 1])
        total = self.core_buf[k, first].astype(F32)
        for m in range(1, p.side):
            total = total + self.first_buf[k, m - 1].astype(F32)
        self.first_buf[k, 0] = total.astype(BF)

    def first_sum(self, k):
        self.add_first(k)
        self.z_start(k)

    def slim_first_sum(self, base):
        p = self.p
        for q in range(p.side):
            self.add_first(base + q)
        _, last, _, last_peer = self.axes(base)
        for m in range(1, p.side):
            q, to = last_peer(m)
            p.send(
                self.first_buf.at[base + q, 0],
                self.z_buf.at[base + last, pl.ds(0, p.layers)],
                self.slim_out,
                self.last_in.at[base + q, m - 1],
                to,
            )

    def slim_last_sum(self, base):
        p = self.p
        _, last, _, _ = self.axes(base)
        own = base + last
        total = self.first_buf[own, 0].astype(F32)
        for m in range(1, p.side):
            came = self.z_buf.at[base + self.before(last, m), pl.ds(0, p.layers)]
            p.arrived(came, self.last_in.at[own, m - 1])
            total = total + came[...].astype(F32)
        self.first_buf[own, 0] = total.astype(BF)
        self.z_start(own)

    def z_send(self, k, src, slot, to):
        self.p.send(src, self.z_buf.at[k, slot], self.z_out, self.z_in.at[k, slot], to)

    def z_start(self, k):
        p = self.p
        top = p.layers - 1

        @pl.when(p.z == 0)
        def _():
            for j in range(top, 0, -1):
                self.z_send(k, self.first_buf.at[k, 0, j], j if j > 1 else p.layers, p.up)

        @pl.when(p.z == top)
        def _():
            for j in range(0, top):
                self.z_send(k, self.first_buf.at[k, 0, j], j, p.down)

    def z_step(self, s, k):
        p = self.p
        top = p.layers - 1

        def add(j):
            p.arrived(self.z_buf.at[k, j], self.z_in.at[k, j])
            self.z_buf[k, j] = (
                self.z_buf[k, j].astype(F32) + self.first_buf[k, 0, j].astype(F32)
            ).astype(BF)
            return self.z_buf.at[k, j]

        @pl.when(p.z == s)
        def _():
            for j in range(top, s, -1):
                self.z_send(k, add(j), j if j > s + 1 else p.layers, p.up)

        @pl.when(p.z == top - s)
        def _():
            for j in range(0, top - s):
                self.z_send(k, add(j), j, p.down)

    def z_total(self, k, into):
        p = self.p
        top = p.layers - 1

        def arrival(slot):
            p.arrived(self.z_buf.at[k, slot], self.z_in.at[k, slot])
            return self.z_buf[k, slot].astype(F32)

        mine = self.first_buf[k, 0, p.z].astype(F32)

        @pl.when(p.z == 0)
        def _():
            into[k] = (mine + arrival(0)).astype(BF)

        @pl.when(p.z == top)
        def _():
            into[k] = (mine + arrival(p.layers)).astype(BF)

        @pl.when((p.z > 0) & (p.z < top))
        def _():
            into[k] = (mine + arrival(p.layers) + arrival(p.z)).astype(BF)

    def z_final(self, k):
        p = self.p
        _, _, _, last_peer = self.axes(k)
        self.z_total(k, self.z_sum)
        for m in range(1, p.side):
            _, to = last_peer(m)
            p.send(
                self.z_sum.at[k],
                self.last_buf.at[k, m - 1],
                self.last_out,
                self.last_in.at[k, m - 1],
                to,
            )

    def slim_z_final(self, base):
        own = base + self.axes(base)[1]
        self.z_total(own, self.final)
        self.z_return_start(own)

    def last_sum(self, k):
        p = self.p
        _, last, _, _ = self.axes(k)
        for m in range(1, p.side):
            p.arrived(self.last_buf.at[k, m - 1], self.last_in.at[k, m - 1])
        total = None
        for q in range(p.side):
            m = self.before(last, q)
            term = jnp.where(
                m == 0,
                self.z_sum[k].astype(F32),
                self.last_buf[k, jnp.maximum(m - 1, 0)].astype(F32),
            )
            total = term if total is None else total + term
        self.final[k] = total.astype(BF)
        self.z_return_start(k)

    def own_copy(self, k):
        p = self.p
        there = self.gath.at[k, p.core, self.axes(k)[0], p.z]
        return there, pltpu.make_async_copy(self.final.at[k], there, self.own_in.at[k])

    def z_return_start(self, k):
        p = self.p
        there, copy = self.own_copy(k)
        copy.start()

        @pl.when(p.z < p.layers - 1)
        def _():
            p.send(self.final.at[k], there, self.z_ret, self.z_back.at[k, p.z], p.up)

        @pl.when(p.z > 0)
        def _():
            p.send(self.final.at[k], there, self.z_ret, self.z_back.at[k, p.z], p.down)

    def z_return(self, s, k):
        p = self.p
        first, _, _, _ = self.axes(k)
        top = p.layers - 1

        def forward(j, ahead, to):
            shard = self.gath.at[k, p.core, first, j]
            p.arrived(shard, self.z_back.at[k, j])

            @pl.when(ahead)
            def _():
                p.send(shard, shard, self.z_ret, self.z_back.at[k, j], to)

        @pl.when(p.z >= s)
        def _():
            forward(jnp.maximum(p.z - s, 0), p.z < top, p.up)

        @pl.when(p.z <= top - s)
        def _():
            forward(jnp.minimum(p.z + s, top), p.z > 0, p.down)

        if s == top:
            self.own_copy(k)[1].wait()

    def send_first(self, k, chunks):
        p = self.p
        first, _, first_peer, _ = self.axes(k)
        mine = self.gath.at[chunks, p.core, first]
        for m in range(1, p.side):
            p.send(mine, mine, self.first_ret, self.first_back.at[k, m - 1], first_peer(m)[1])

    def send_core(self, k, chunks):
        p = self.p
        first, _, _, _ = self.axes(k)
        for m in range(1, p.side):
            came = self.gath.at[chunks, p.core, self.before(first, m)]
            p.arrived(came, self.first_back.at[k, m - 1])
        mine = self.gath.at[chunks, p.core]
        p.send(mine, mine, self.core_ret, self.core_back.at[k], p.other_core)

    def wide_z_return(self, k):
        self.z_return(self.p.layers - 1, k)
        self.send_first(k, k)

    def core_return(self, k):
        self.send_core(k, k)

    def finish(self, k):
        self.p.arrived(self.gath.at[k, 1 - self.p.core], self.core_back.at[k])

    def slim_z_return(self, base):
        p = self.p
        first, last, _, last_peer = self.axes(base)
        own = base + last
        self.z_return(p.layers - 1, own)
        mine = self.gath.at[own, p.core, first]
        for m in range(1, p.side):
            p.send(mine, mine, self.slim_ret, self.last_back.at[own, m - 1], last_peer(m)[1])

    def slim_last_return(self, base):
        p = self.p
        first, last, _, _ = self.axes(base)
        for m in range(1, p.side):
            k = base + self.before(last, m)
            p.arrived(self.gath.at[k, p.core, first], self.last_back.at[k, m - 1])
        self.send_first(base, pl.ds(base, p.side))

    def slim_core_return(self, base):
        self.send_core(base, pl.ds(base, self.p.side))

    def slim_finish(self, base):
        unit = self.gath.at[pl.ds(base, self.p.side), 1 - self.p.core]
        self.p.arrived(unit, self.core_back.at[base])

    def drain(self):
        p = self.p
        units = self.slims // p.side
        wides = self.count - self.slims
        chains = pl.ds(0, wides + units)
        p.sent(self.core_buf, self.core_out)
        p.sent(self.first_buf, self.first_out)
        p.sent(self.first_buf, self.first_ret)
        p.sent(self.core_buf, self.core_ret)
        p.sent(self.z_buf.at[chains, pl.ds(0, p.layers - 1)], self.z_out)
        middle = (p.z > 0) & (p.z < p.layers - 1)

        @pl.when(middle)
        def _():
            p.sent(self.z_buf.at[chains], self.z_ret)

        @pl.when(jnp.logical_not(middle))
        def _():
            p.sent(self.z_buf.at[chains, pl.ds(0, 1)], self.z_ret)

        if wides:
            p.sent(self.last_buf.at[pl.ds(0, wides)], self.last_out)
        if units:
            p.sent(self.first_buf.at[pl.ds(0, units)], self.slim_out)
            p.sent(self.first_buf.at[pl.ds(0, units)], self.slim_ret)


def reducer_scratch(count, side, layers, rows, wide):
    bufs = [
        pltpu.VMEM((count, side, layers, rows, wide), BF),
        pltpu.VMEM((count, side - 1, layers, rows, wide), BF),
        pltpu.VMEM((count, layers + 1, rows, wide), BF),
        pltpu.VMEM((count, side - 1, rows, wide), BF),
        pltpu.VMEM((count, rows, wide), BF),
        pltpu.VMEM((count, rows, wide), BF),
    ]
    recv = [
        DMA((count,)),
        DMA((count, side - 1)),
        DMA((count, layers + 1)),
        DMA((count, side - 1)),
        DMA((count,)),
        DMA((count, layers)),
        DMA((count, side - 1)),
        DMA((count,)),
        DMA((count, side - 1)),
    ]
    return bufs, recv, [DMA(())] * 9


def layer_kernel(cfg, *refs):
    refs = list(refs)

    def take(number):
        taken = refs[:number]
        del refs[:number]
        return taken

    (knowledge, expr_table, owner_ids, gene_row, expr_bin, lengths) = take(6)
    (gain1, bias1, w_query, b_query, w_key, w_value, b_value, w_out1, b_out1) = take(9)
    (gain2, bias2, w_in, b_in, w_out, b_out, cotangent) = take(7)
    mixed, table_grad, gath = take(3)
    know_v, wq_v, wk_v, wv_v, wo_v, win_v, wout_v, cot_v = take(8)
    load_sems, ids_out, ids_in, rows_out, rows_in, back_in, row_hot_v, slot_hot_v = take(8)
    ids_sem, rows_sem, ids_sent, rows_sent, back_sent = take(5)
    (embedded_v, attn_in_v, query_v, key_v, value_v, probs_v, context_v) = take(7)
    (hidden1_v, ffn_in_v, grad_ffn_v, acc_v, gn2_v, biases_v) = take(6)
    (part,) = take(1)
    bufs, recv, sent = take(6), take(9), take(9)
    assert not refs

    side, layers, cap, offsets = cfg
    place = Place(side, layers)
    devices = place.count
    red = Reducer(place, part, gath, bufs, recv, sent)
    tokens, width = embedded_v.shape
    table_rows = knowledge.shape[1]
    half = width // 2
    blocks = w_in.shape[1] // width
    count = part.shape[0]
    slots = devices * cap

    loads = [
        (knowledge, know_v),
        (w_query, wq_v),
        (w_key, wk_v),
        (w_value, wv_v),
        (w_out1, wo_v),
        (cotangent, cot_v),
    ]
    for j in range(blocks):
        loads.append((w_in.at[:, pl.ds(j * width, width)], win_v.at[j % 2]))
        loads.append((w_out.at[pl.ds(j * width, width)], wout_v.at[j % 2]))
    loads = [
        pltpu.make_async_copy(src, dst, load_sems.at[i]) for i, (src, dst) in enumerate(loads)
    ]
    for load in loads[: 6 + 4]:
        load.start()
    place.greet_all()

    def iota(shape, dim):
        return lax.broadcasted_iota(jnp.int32, shape, dim)

    def hot(condition):
        return jnp.where(condition, 1.0, 0.0).astype(BF)

    owner_row = owner_ids[...]
    owner_hot = hot(iota((devices, tokens), 0) == owner_row)
    earlier = hot(iota((tokens, tokens), 0) < iota((tokens, tokens), 1))
    before = dot(owner_hot, earlier)
    rank_row = column_sum(before * owner_hot.astype(F32)).astype(jnp.int32)
    slot_hot_v[...] = hot(iota((slots, tokens), 0) == owner_row * cap + rank_row)
    rank_hot = hot(iota((128, tokens), 0) == rank_row)
    named = (owner_hot.astype(F32) * (gene_row[...] + 1).astype(F32)).astype(BF)
    wanted = dot(named, rank_hot, 1, 1)
    for d in range(devices):
        ids_out[d] = wanted[d : d + 1]

    place.await_all()
    place.exchange_start(ids_out, ids_in, ids_sent, ids_sem)
    ids_in[place.me] = ids_out[place.me]
    loads[0].wait()
    table_sum = know_v[0].astype(F32)
    for k in range(1, know_v.shape[0]):
        table_sum = table_sum + know_v[k].astype(F32)
    table_sum = table_sum.astype(BF)
    expr_hot = hot(iota((expr_table.shape[0], tokens), 0) == expr_bin[...])
    expr_part = dot(expr_hot, expr_table[...], 0, 0)
    place.exchange_wait(ids_in, ids_sem)
    asked = ids_in[...].reshape(devices, 128).astype(BF)
    spread = hot(iota((slots, devices), 0) // cap == iota((slots, devices), 1))
    asked = dot(spread, asked)
    own_lane = lax.rem(iota((slots, 128), 0), cap) == iota((slots, 128), 1)
    asked = jnp.sum(jnp.where(own_lane, asked, 0.0), axis=1, keepdims=True)
    row_hot = hot(iota((slots, table_rows), 1) + 1 == asked.astype(jnp.int32))
    row_hot_v[...] = row_hot
    rows_out[...] = dot(row_hot, table_sum).astype(BF).reshape(devices, cap, width)
    place.exchange_start(rows_out, rows_in, rows_sent, rows_sem)
    rows_in[place.me] = rows_out[place.me]

    end = lengths[0]
    ends = [end]
    for c in range(1, lengths.shape[0]):
        end = end + lengths[c]
        ends.append(end)

    def segments(shape, dim):
        spot = iota(shape, dim)
        segment = jnp.zeros(shape, jnp.int32)
        for stop in ends:
            segment = segment + jnp.where(spot >= stop, 1, 0)
        return segment

    spot = lax.rem(iota((2 * tokens, tokens), 0), tokens)
    segment = jnp.zeros((2 * tokens, tokens), jnp.int32)
    for stop in ends:
        segment = segment + jnp.where(spot >= stop, 1, 0)
    same_cell = segment == segments((2 * tokens, tokens), 1)
    live = jnp.where(iota((tokens, 1), 0) < ends[-1], 1.0, 0.0)

    place.exchange_wait(rows_in, rows_sem)
    gathered = rows_in[...].reshape(slots, width)
    embedded_v[...] = dot(slot_hot_v[...], gathered, 0, 0) + expr_part
    for load in loads[1:5]:
        load.wait()

    xhat1, recip1 = standardise(embedded_v[...])
    attn_in_v[...] = (xhat1 * gain1[...].reshape(1, width) + bias1[...].reshape(1, width)).astype(BF)
    query_v[...] = (dot(attn_in_v[...], wq_v[...]) + b_query[...].reshape(1, width)).astype(BF)
    key_v[...] = dot(attn_in_v[...], wk_v[...]).astype(BF)
    value_v[...] = (dot(attn_in_v[...], wv_v[...]) + b_value[...].reshape(1, width)).astype(BF)
    low_lane = iota((tokens, PAIR), 1) < HEAD_DIM

    def two_heads(values):
        zero = jnp.zeros_like(values)
        return jnp.concatenate(
            [jnp.where(low_lane, values, zero), jnp.where(low_lane, zero, values)], axis=0
        )

    def one_of_two(values):
        return jnp.where(low_lane, values[:tokens], values[tokens:])

    for pair in range(width // PAIR):
        lanes = slice(pair * PAIR, (pair + 1) * PAIR)
        scores = dot(two_heads(query_v[:, lanes]), key_v[:, lanes], 1, 1) * SCALE
        scores = jnp.where(same_cell, scores, MASKED)
        scores = jnp.exp(scores - jnp.max(scores, axis=1, keepdims=True))
        probs = scores / jnp.sum(scores, axis=1, keepdims=True)
        probs_v[pair] = probs
        context_v[:, lanes] = one_of_two(dot(probs.astype(BF), value_v[:, lanes])).astype(BF)
    hidden1_v[...] = (
        embedded_v[...] + dot(context_v[...], wo_v[...]) + b_out1[...].reshape(1, width)
    )
    loads[5].wait()

    xhat2, recip2 = standardise(hidden1_v[...])
    ffn_in_v[...] = (xhat2 * gain2[...].reshape(1, width) + bias2[...].reshape(1, width)).astype(BF)
    grad_hidden2 = cot_v[...].astype(F32) * live
    grad_ffn_v[...] = grad_hidden2.astype(BF)
    acc_v[...] = jnp.zeros_like(acc_v)
    gn2_v[...] = jnp.zeros_like(gn2_v)
    biases_v[...] = jnp.zeros_like(biases_v)
    shard = part.shape[1:]
    plans = []
    for stages, lags in zip((red.wide_stages, red.slim_stages), offsets):
        reach = [0]
        for lag in lags:
            reach.append(reach[-1] + lag)
        assert len(reach) == len(stages)
        plans.append(list(zip(stages, reach)))
    longest = max(plan[-1][1] for plan in plans)

    def step(i):
        for slim, plan in enumerate(plans):
            for stage, lag in sorted(plan, key=lambda entry: -entry[1]):
                k = i - lag
                ahead = side - 1 if slim else 0
                low, high = (0, red.slims) if slim else (red.slims, count)
                if isinstance(k, int):
                    if low <= k < high and (not slim or k % side == ahead):
                        stage(k - ahead)
                elif low < high:
                    now = (k >= low) & (k < high)
                    if slim:
                        now = now & (lax.rem(k, side) == ahead)

                    @pl.when(now)
                    def _():
                        stage(k - ahead)

    def put(k, values):
        part[k] = values.reshape(shard).astype(BF)
        red.core_send(k)

    done = [0]

    def pipe(where):
        for _ in range(PIPE.get(where, 0)):
            step(done[0])
            done[0] += 1

    def put_bias(row, values):
        biases_v[pl.ds(2 * row, 1), :] = values[:, :half]
        biases_v[pl.ds(2 * row + 1, 1), :] = values[:, half:]

    for j in range(blocks):
        loads[6 + 2 * j].wait()
        loads[7 + 2 * j].wait()
        win, wout = win_v.at[j % 2], wout_v.at[j % 2]
        pre = dot(ffn_in_v[...], win[...]) + b_in[pl.ds(j * width, width)].reshape(1, width)
        square = pre * pre
        bend = jnp.tanh(GELU_SLOPE * (pre + GELU_CUBIC * square * pre))
        act = (0.5 * pre * (1.0 + bend)).astype(BF)
        slope = 0.5 * (1.0 + bend) + 0.5 * pre * (1.0 - bend * bend) * (
            GELU_SLOPE * (1.0 + 3.0 * GELU_CUBIC * square)
        )
        grad_pre = dot(grad_ffn_v[...], wout[...], 1, 1) * slope
        grad_pre = grad_pre.astype(BF)
        if j:
            for q in range(4):
                red.core_sum(4 * (j - 1) + q)
        for h in range(2):
            put(4 * j + h, dot(act, grad_ffn_v[:, h * half : (h + 1) * half], 0, 0))
        for h in range(2):
            put(4 * j + 2 + h, dot(ffn_in_v[...], grad_pre[:, h * half : (h + 1) * half], 0, 0))
        acc_v[...] += dot(act, wout[...])
        gn2_v[...] += dot(grad_pre, win[...], 1, 1)
        if j + 2 < blocks:
            loads[10 + 2 * j].start()
            loads[11 + 2 * j].start()
        put_bias(j, column_sum(grad_pre.astype(F32)))
        pipe(f'ffn{j}')
    at = 4 * blocks
    mixed[...] = (
        (hidden1_v[...] + acc_v[...] + b_out[...].reshape(1, width)) * live
    ).astype(BF)
    put_bias(blocks, column_sum(grad_ffn_v[...].astype(F32)))
    grad_normed2 = gn2_v[...]
    put_bias(blocks + 1, column_sum(grad_normed2 * xhat2))
    put_bias(blocks + 2, column_sum(grad_normed2))
    for q in range(4):
        red.core_sum(at - 4 + q)
    grad_hidden1 = grad_hidden2 + norm_back(xhat2, recip2, gain2[...].reshape(1, width), grad_normed2)
    acc_v[...] = grad_hidden1
    grad_attn = grad_hidden1.astype(BF)
    put_bias(blocks + 3, column_sum(grad_attn.astype(F32)))
    for h in range(2):
        put(at + h, dot(context_v[...], grad_attn[:, h * half : (h + 1) * half], 0, 0))
    pipe('out')
    gctx_v = ffn_in_v
    gctx_v[...] = dot(grad_attn, wo_v[...], 1, 1).astype(BF)
    gq_v, gk_v, gv_v = query_v, key_v, value_v

    for pair in range(width // PAIR):
        lanes = slice(pair * PAIR, (pair + 1) * PAIR)
        probs = probs_v[pair]
        grads = two_heads(gctx_v[:, lanes])
        grad_probs = dot(grads, value_v[:, lanes], 1, 1)
        inner = jnp.sum(probs * grad_probs, axis=1, keepdims=True)
        grad_scores = (probs * (grad_probs - inner)).astype(BF)
        grad_query = one_of_two(dot(grad_scores, key_v[:, lanes])) * SCALE
        grad_key = dot(grad_scores, two_heads(query_v[:, lanes]), 0, 0) * SCALE
        gq_v[:, lanes] = grad_query.astype(BF)
        gk_v[:, lanes] = grad_key.astype(BF)
        gv_v[:, lanes] = dot(probs.astype(BF), grads, 0, 0).astype(BF)
        pipe(f'pair{pair}')
    for q in range(2):
        red.core_sum(at + q)
    at += 2
    for grad in (gq_v, gk_v, gv_v):
        for h in range(2):
            put(at + h, dot(attn_in_v[...], grad[:, h * half : (h + 1) * half], 0, 0))
        at += 2
        pipe(f'grad{at}')
    put_bias(blocks + 4, column_sum(gq_v[...].astype(F32)))
    put_bias(blocks + 5, column_sum(gv_v[...].astype(F32)))
    grad_normed1 = dot(gq_v[...], wq_v[...], 1, 1)
    grad_normed1 = grad_normed1 + dot(gk_v[...], wk_v[...], 1, 1)
    grad_normed1 = grad_normed1 + dot(gv_v[...], wv_v[...], 1, 1)
    xhat1, recip1 = standardise(embedded_v[...])
    put_bias(blocks + 6, column_sum(grad_normed1 * xhat1))
    put_bias(blocks + 7, column_sum(grad_normed1))
    grad_embedded = acc_v[...] + norm_back(
        xhat1, recip1, gain1[...].reshape(1, width), grad_normed1
    )
    grad_embedded = grad_embedded.astype(BF)
    back_out = rows_out
    place.sent(rows_out.at[pl.ds(0, devices - 1)], rows_sent)
    back_out[...] = dot(slot_hot_v[...], grad_embedded).astype(BF).reshape(devices, cap, width)
    expr_grad = dot(expr_hot, grad_embedded)
    bins = expr_grad.shape[0]
    filler = jnp.zeros((width - 2 * bins - biases_v.shape[0], half), F32)
    put(
        at,
        jnp.concatenate([expr_grad[:, :half], expr_grad[:, half:], biases_v[...], filler], axis=0),
    )
    place.exchange_start(back_out, back_in, back_sent, ids_sem)
    pipe('back')
    back_in[place.me] = back_out[place.me]
    for k in range(at - 6, at + 1):
        red.core_sum(k)

    def later(i, carry):
        step(i)
        return carry

    lax.fori_loop(done[0], count + longest, later, 0)
    place.exchange_wait(back_in, ids_sem)
    table_grad[...] = dot(row_hot_v[...], back_in[...].reshape(slots, width), 0, 0)
    place.sent(ids_out.at[pl.ds(0, devices - 1)], ids_sent)
    place.sent(back_out.at[pl.ds(0, devices - 1)], back_sent)
    red.drain()


def layer(side, layers, args):
    (knowledge, expr_table, gene_owner, gene_row, expr_bin, cell_lengths) = args[:6]
    cotangent, w_in = args[21], args[17]
    tokens, width = cotangent.shape
    devices = 2 * side * side * layers
    cap = max(8, 2 * tokens // devices)
    slots = devices * cap
    table_rows = knowledge.shape[1]
    blocks = w_in.shape[1] // width
    count = 4 * blocks + 9
    half = width // 2
    shard = width // (2 * side * layers)
    whole = (count, 2, side, layers, shard, half)
    bufs, recv, sent = reducer_scratch(count, side, layers, shard, half)
    wide = lambda dtype: pltpu.VMEM((tokens, width), dtype)
    square = pltpu.VMEM((width, width), BF)
    scratch = [
        pltpu.VMEM(knowledge.shape, BF),
        square,
        square,
        square,
        square,
        pltpu.VMEM((2, width, width), BF),
        pltpu.VMEM((2, width, width), BF),
        wide(BF),
        DMA((6 + 2 * blocks,)),
        pltpu.VMEM((devices, 1, 128), F32),
        pltpu.VMEM((devices, 1, 128), F32),
        pltpu.VMEM((devices, cap, width), BF),
        pltpu.VMEM((devices, cap, width), BF),
        pltpu.VMEM((devices, cap, width), BF),
        pltpu.VMEM((slots, table_rows), BF),
        pltpu.VMEM((slots, tokens), BF),
        DMA((devices,)),
        DMA((devices,)),
        DMA(()),
        DMA(()),
        DMA(()),
        wide(F32),
        wide(BF),
        wide(BF),
        wide(BF),
        wide(BF),
        pltpu.VMEM((width // PAIR, 2 * tokens, tokens), F32),
        wide(BF),
        wide(F32),
        wide(BF),
        wide(BF),
        wide(F32),
        wide(F32),
        pltpu.VMEM((8 * ((2 * (blocks + 8) + 7) // 8), half), F32),
        pltpu.VMEM(whole, BF),
    ]
    vmem = pl.BlockSpec(memory_space=pltpu.VMEM)
    hbm = pl.BlockSpec(memory_space=pl.ANY)
    smem = pl.BlockSpec(memory_space=pltpu.SMEM)
    in_hbm = {0, 8, 10, 11, 13, 17, 19, 21}
    specs = [hbm if i in in_hbm else smem if i == 5 else vmem for i in range(22)]
    offsets = OFFSETS
    flops = 2 * tokens * (3 * (4 * width * width + 2 * width * w_in.shape[1]))
    return pl.pallas_call(
        functools.partial(layer_kernel, (side, layers, cap, offsets)),
        out_shape=(
            jax.ShapeDtypeStruct((tokens, width), BF),
            jax.ShapeDtypeStruct((table_rows, width), F32),
            jax.ShapeDtypeStruct(whole, BF),
        ),
        in_specs=specs,
        out_specs=(vmem, vmem, hbm),
        scratch_shapes=scratch + bufs + recv + sent,
        compiler_params=pltpu.CompilerParams(
            collective_id=1, has_side_effects=True, vmem_limit_bytes=VMEM_BYTES
        ),
        cost_estimate=pl.CostEstimate(flops=flops, bytes_accessed=40 << 20, transcendentals=0),
    )(
        knowledge,
        expr_table,
        gene_owner.reshape(1, tokens),
        gene_row.reshape(1, tokens),
        expr_bin.reshape(1, tokens),
        *args[5:],
    )


OFFSETS = ([2, 1, 1, 3, 2, 2, 1, 4, 4], [3, 2, 2, 1, 2, 1, 0, 3, 4, 3])
SLIM = 10
PIPE = {"ffn2": 2, "ffn3": 2, "pair2": 1, "pair4": 1, "grad20": 1, "grad22": 1, "grad24": 1, "back": 2}
VMEM_BYTES = 62 << 20
DEPTH = 8


def spread_kernel(gath, table_grad, *refs):
    (know_out, expr_out, gain1_out, bias1_out, wq_out, bq_out, wk_out, wv_out, bv_out) = refs[:9]
    (wo_out, bo1_out, gain2_out, bias2_out, win_out, bin_out, wout_out, bout_out) = refs[9:17]
    narrow, broad, in_sems, out_sems, know_sems = refs[17:]
    count, width, half = gath.shape
    blocks = win_out.shape[1] // width
    places = []
    for j in range(blocks):
        rows = pl.ds(j * width, width)
        for h in range(2):
            places.append(wout_out.at[rows, pl.ds(h * half, half)])
        for h in range(2):
            places.append(win_out.at[:, pl.ds(j * width + h * half, half)])
    for out in (wo_out, wq_out, wk_out, wv_out):
        for h in range(2):
            places.append(out.at[:, pl.ds(h * half, half)])
    assert len(places) == count - 1

    def fetch(k):
        return pltpu.make_async_copy(gath.at[k], narrow.at[k % DEPTH], in_sems.at[k % DEPTH])

    def store(k):
        return pltpu.make_async_copy(broad.at[k % DEPTH], places[k], out_sems.at[k % DEPTH])

    for k in range(DEPTH - 1):
        fetch(k).start()
    knows = [
        pltpu.make_async_copy(table_grad, know_out.at[i], know_sems.at[i])
        for i in range(know_out.shape[0])
    ]
    for know in knows:
        know.start()
    for k in range(count):
        if k + DEPTH - 1 < count:
            fetch(k + DEPTH - 1).start()
        fetch(k).wait()
        if k == count - 1:
            break
        if k >= DEPTH:
            store(k - DEPTH).wait()
        broad[k % DEPTH] = narrow[k % DEPTH].astype(F32)
        store(k).start()
    small = narrow.at[(count - 1) % DEPTH]
    bins = expr_out.shape[0]
    expr_out[:, :half] = small[pl.ds(0, bins), :].astype(F32)
    expr_out[:, half:] = small[pl.ds(bins, bins), :].astype(F32)
    biases = small[pl.ds(2 * bins, 8 * ((2 * (blocks + 8) + 7) // 8)), :].astype(F32)

    def bias(i):
        return jnp.concatenate([biases[2 * i : 2 * i + 1], biases[2 * i + 1 : 2 * i + 2]], axis=1)[0]

    for j in range(blocks):
        bin_out[pl.ds(j * width, width)] = bias(j)
    for i, out in enumerate(
        (bout_out, gain2_out, bias2_out, bo1_out, bq_out, bv_out, gain1_out, bias1_out)
    ):
        out[...] = bias(blocks + i)
    for k in range(max(0, count - 1 - DEPTH), count - 1):
        store(k).wait()
    for know in knows:
        know.wait()


def spread(gath, table_grad, tables, bins, hidden):
    count, width, half = gath.shape
    shape = lambda *dims: jax.ShapeDtypeStruct(dims, F32)
    vector, square = shape(width), shape(width, width)
    vmem = pl.BlockSpec(memory_space=pltpu.VMEM)
    hbm = pl.BlockSpec(memory_space=pl.ANY)
    outs = (
        (shape(tables, *table_grad.shape), hbm),
        (shape(bins, width), vmem),
        (vector, vmem),
        (vector, vmem),
        (square, hbm),
        (vector, vmem),
        (square, hbm),
        (square, hbm),
        (vector, vmem),
        (square, hbm),
        (vector, vmem),
        (vector, vmem),
        (vector, vmem),
        (shape(width, hidden), hbm),
        (shape(hidden), vmem),
        (shape(hidden, width), hbm),
        (vector, vmem),
    )
    return pl.pallas_call(
        spread_kernel,
        out_shape=tuple(out for out, _ in outs),
        in_specs=[pl.BlockSpec(memory_space=pltpu.HBM), vmem],
        out_specs=tuple(spec for _, spec in outs),
        scratch_shapes=[
            pltpu.VMEM((DEPTH, width, half), BF),
            pltpu.VMEM((DEPTH, width, half), F32),
            DMA((DEPTH,)),
            DMA((DEPTH,)),
            DMA((tables,)),
        ],
        compiler_params=pltpu.CompilerParams(vmem_limit_bytes=56 << 20),
        cost_estimate=pl.CostEstimate(flops=0, bytes_accessed=48 << 20, transcendentals=0),
    )(gath, table_grad)


def local(*args):
    layers = lax.axis_size("table")
    side = math.isqrt(lax.axis_size("dp") // 2)
    knowledge, expr_table, w_in = args[0], args[1], args[17]
    width, hidden = w_in.shape
    mixed, table_grad, total = layer(side, layers, args)
    total = total.reshape(-1, width, width // 2)
    return (mixed, *spread(total, table_grad, knowledge.shape[0], expr_table.shape[0], hidden))


def solution(mesh):
    rows = P(("dp", "table"))
    by_token = P(("dp", "table"), None)
    by_row = P(None, ("dp", "table"), None)
    in_specs = (by_row, P(), by_token, rows, rows, rows) + (P(),) * 15 + (by_token,)
    out_specs = (by_token, by_row) + (P(),) * 16
    return jax.shard_map(local, mesh=mesh, in_specs=in_specs, out_specs=out_specs, check_vma=False)
```

```python
import functools
import math

import jax
import jax.numpy as jnp
from jax import lax
from jax.experimental import pallas as pl
from jax.experimental.pallas import tpu as pltpu
from jax.sharding import PartitionSpec as P

HEAD_DIM = 64
PAIR = 2 * HEAD_DIM
SCALE = HEAD_DIM ** (-0.5)
LAYER_EPS = 1e-05
GELU_SLOPE = 0.7978845608028654
GELU_CUBIC = 0.044715
MASKED = -1e30
MESH = pl.DeviceIdType.MESH
BF = jnp.bfloat16
F32 = jnp.float32
DMA = pltpu.SemaphoreType.DMA


def dot(lhs, rhs, lhs_dim=1, rhs_dim=0):
    return lax.dot_general(
        lhs, rhs, (((lhs_dim,), (rhs_dim,)), ((), ())), preferred_element_type=F32
    )


def column_sum(values):
    return jnp.sum(values, axis=0, keepdims=True)


def row_mean(values):
    return jnp.mean(values, axis=1, keepdims=True)


def standardise(values):
    centred = values - row_mean(values)
    recip = lax.rsqrt(row_mean(centred * centred) + LAYER_EPS)
    return centred * recip, recip


def norm_back(xhat, recip, gain, grad):
    scaled = gain * grad
    return recip * (scaled - row_mean(scaled) - xhat * row_mean(scaled * xhat))


class Place:
    def __init__(self, side, layers):
        self.side, self.layers = side, layers
        dp = lax.axis_index("dp")
        self.z = lax.axis_index("table")
        self.a, self.b, self.core = dp // (2 * side), (dp // 2) % side, dp % 2
        self.me = dp * layers + self.z
        self.count = 2 * side * side * layers
        self.other_core = self.at(self.a, self.b, 1 - self.core, self.z)
        self.up = self.at(self.a, self.b, self.core, jnp.minimum(self.z + 1, layers - 1))
        self.down = self.at(self.a, self.b, self.core, jnp.maximum(self.z - 1, 0))

    def at(self, a, b, core, z):
        return ((a * self.side + b) * 2 + core, z)

    def flat(self, index):
        return (index // self.layers, lax.rem(index, self.layers))

    def copy(self, src, dst, send_sem, recv_sem, to):
        return pltpu.make_async_remote_copy(
            src_ref=src,
            dst_ref=dst,
            send_sem=send_sem,
            recv_sem=recv_sem,
            device_id=to,
            device_id_type=MESH,
        )

    def send(self, src, dst, send_sem, recv_sem, to):
        self.copy(src, dst, send_sem, recv_sem, to).start()

    def arrived(self, dst, recv_sem):
        self.copy(dst, dst, recv_sem, recv_sem, self.other_core).wait_recv()

    def sent(self, src, send_sem):
        self.copy(src, src, send_sem, send_sem, self.other_core).wait_send()

    def each_other(self, act):
        layers = self.layers
        for dz in sorted(range(layers), key=lambda d: -min(d, layers - d)):

            def one(i, carry):
                act(i * layers + dz)
                return carry

            lax.fori_loop(0 if dz else 1, self.count // layers, one, 0)

    def greet_all(self):
        bar = pltpu.get_barrier_semaphore()

        def greet(step):
            to = self.flat(lax.rem(self.me + step, self.count))
            pl.semaphore_signal(bar, inc=1, device_id=to, device_id_type=MESH)

        self.each_other(greet)

    def await_all(self):
        pl.semaphore_wait(pltpu.get_barrier_semaphore(), self.count - 1)

    def exchange_start(self, out, into, send_sem, recv_sems):
        def start(step):
            to = lax.rem(self.me + step, self.count)
            self.send(out.at[to], into.at[self.me], send_sem, recv_sems.at[step], self.flat(to))

        self.each_other(start)

    def exchange_wait(self, into, recv_sems):
        def wait(step):
            origin = lax.rem(self.me + self.count - step, self.count)
            self.arrived(into.at[origin], recv_sems.at[step])

        self.each_other(wait)


class Reducer:
    def __init__(self, place, part, gath, bufs, recv, sent):
        self.p = place
        self.part, self.gath = part, gath
        self.core_buf, self.first_buf, self.z_buf, self.last_buf, self.z_sum, self.final = bufs
        self.core_in, self.first_in, self.z_in, self.last_in, self.own_in = recv[:5]
        self.z_back, self.first_back, self.core_back, self.last_back = recv[5:]
        self.core_out, self.first_out, self.first_ret, self.core_ret = sent[:4]
        self.z_out, self.z_ret, self.last_out, self.slim_out, self.slim_ret = sent[4:]
        layers = place.layers
        self.count = part.shape[0]
        self.slims = SLIM // place.side * place.side
        bind = functools.partial
        steps, returns = range(1, layers - 1), range(1, layers)
        self.wide_stages = (
            [self.first_sum]
            + [bind(self.z_step, s) for s in steps]
            + [self.z_final, self.last_sum]
            + [bind(self.z_return, s) for s in returns[:-1]]
            + [self.wide_z_return, self.core_return, self.finish]
        )
        self.slim_stages = (
            [self.slim_first_sum, self.slim_last_sum]
            + [self.of_own(bind(self.z_step, s)) for s in steps]
            + [self.slim_z_final]
            + [self.of_own(bind(self.z_return, s)) for s in returns[:-1]]
            + [self.slim_z_return, self.slim_last_return, self.slim_core_return, self.slim_finish]
        )

    def axes(self, k):
        p = self.p
        if isinstance(k, int):
            even = (k // p.side if k < self.slims else k) % 2 == 0
        else:
            even = lax.rem(jnp.where(k < self.slims, k // p.side, k), 2) == 0
        first = jnp.where(even, p.b, p.a)
        last = jnp.where(even, p.a, p.b)

        def first_peer(m):
            q = lax.rem(first + m, p.side)
            return q, p.at(jnp.where(even, p.a, q), jnp.where(even, q, p.b), p.core, p.z)

        def last_peer(m):
            q = lax.rem(last + m, p.side)
            return q, p.at(jnp.where(even, q, p.a), jnp.where(even, p.b, q), p.core, p.z)

        return first, last, first_peer, last_peer

    def before(self, position, m):
        return lax.rem(position - m + self.p.side, self.p.side)

    def of_own(self, act):
        return lambda base: act(base + self.axes(base)[1])

    def core_send(self, k):
        p = self.p
        p.send(
            self.part.at[k, 1 - p.core],
            self.core_buf.at[k],
            self.core_out,
            self.core_in.at[k],
            p.other_core,
        )

    def core_sum(self, k):
        p = self.p
        _, _, first_peer, _ = self.axes(k)
        p.arrived(self.core_buf.at[k], self.core_in.at[k])
        self.core_buf[k] = (
            self.core_buf[k].astype(F32) + self.part[k, p.core].astype(F32)
        ).astype(BF)
        for m in range(1, p.side):
            q, to = first_peer(m)
            p.send(
                self.core_buf.at[k, q],
                self.first_buf.at[k, m - 1],
                self.first_out,
                self.first_in.at[k, m - 1],
                to,
            )

    def add_first(self, k):
        p = self.p
        first, _, _, _ = self.axes(k)
        for m in range(1, p.side):
            p.arrived(self.first_buf.at[k, m - 1], self.first_in.at[k, m - 1])
        total = self.core_buf[k, first].astype(F32)
        for m in range(1, p.side):
            total = total + self.first_buf[k, m - 1].astype(F32)
        self.first_buf[k, 0] = total.astype(BF)

    def first_sum(self, k):
        self.add_first(k)
        self.z_start(k)

    def slim_first_sum(self, base):
        p = self.p
        for q in range(p.side):
            self.add_first(base + q)
        _, last, _, last_peer = self.axes(base)
        for m in range(1, p.side):
            q, to = last_peer(m)
            p.send(
                self.first_buf.at[base + q, 0],
                self.z_buf.at[base + last, pl.ds(0, p.layers)],
                self.slim_out,
                self.last_in.at[base + q, m - 1],
                to,
            )

    def slim_last_sum(self, base):
        p = self.p
        _, last, _, _ = self.axes(base)
        own = base + last
        total = self.first_buf[own, 0].astype(F32)
        for m in range(1, p.side):
            came = self.z_buf.at[base + self.before(last, m), pl.ds(0, p.layers)]
            p.arrived(came, self.last_in.at[own, m - 1])
            total = total + came[...].astype(F32)
        self.first_buf[own, 0] = total.astype(BF)
        self.z_start(own)

    def z_send(self, k, src, slot, to):
        self.p.send(src, self.z_buf.at[k, slot], self.z_out, self.z_in.at[k, slot], to)

    def z_start(self, k):
        p = self.p
        top = p.layers - 1

        @pl.when(p.z == 0)
        def _():
            for j in range(top, 0, -1):
                self.z_send(k, self.first_buf.at[k, 0, j], j if j > 1 else p.layers, p.up)

        @pl.when(p.z == top)
        def _():
            for j in range(0, top):
                self.z_send(k, self.first_buf.at[k, 0, j], j, p.down)

    def z_step(self, s, k):
        p = self.p
        top = p.layers - 1

        def add(j):
            p.arrived(self.z_buf.at[k, j], self.z_in.at[k, j])
            self.z_buf[k, j] = (
                self.z_buf[k, j].astype(F32) + self.first_buf[k, 0, j].astype(F32)
            ).astype(BF)
            return self.z_buf.at[k, j]

        @pl.when(p.z == s)
        def _():
            for j in range(top, s, -1):
                self.z_send(k, add(j), j if j > s + 1 else p.layers, p.up)

        @pl.when(p.z == top - s)
        def _():
            for j in range(0, top - s):
                self.z_send(k, add(j), j, p.down)

    def z_total(self, k, into):
        p = self.p
        top = p.layers - 1

        def arrival(slot):
            p.arrived(self.z_buf.at[k, slot], self.z_in.at[k, slot])
            return self.z_buf[k, slot].astype(F32)

        mine = self.first_buf[k, 0, p.z].astype(F32)

        @pl.when(p.z == 0)
        def _():
            into[k] = (mine + arrival(0)).astype(BF)

        @pl.when(p.z == top)
        def _():
            into[k] = (mine + arrival(p.layers)).astype(BF)

        @pl.when((p.z > 0) & (p.z < top))
        def _():
            into[k] = (mine + arrival(p.layers) + arrival(p.z)).astype(BF)

    def z_final(self, k):
        p = self.p
        _, _, _, last_peer = self.axes(k)
        self.z_total(k, self.z_sum)
        for m in range(1, p.side):
            _, to = last_peer(m)
            p.send(
                self.z_sum.at[k],
                self.last_buf.at[k, m - 1],
                self.last_out,
                self.last_in.at[k, m - 1],
                to,
            )

    def slim_z_final(self, base):
        own = base + self.axes(base)[1]
        self.z_total(own, self.final)
        self.z_return_start(own)

    def last_sum(self, k):
        p = self.p
        _, last, _, _ = self.axes(k)
        for m in range(1, p.side):
            p.arrived(self.last_buf.at[k, m - 1], self.last_in.at[k, m - 1])
        total = None
        for q in range(p.side):
            m = self.before(last, q)
            term = jnp.where(
                m == 0,
                self.z_sum[k].astype(F32),
                self.last_buf[k, jnp.maximum(m - 1, 0)].astype(F32),
            )
            total = term if total is None else total + term
        self.final[k] = total.astype(BF)
        self.z_return_start(k)

    def own_copy(self, k):
        p = self.p
        there = self.gath.at[k, p.core, self.axes(k)[0], p.z]
        return there, pltpu.make_async_copy(self.final.at[k], there, self.own_in.at[k])

    def z_return_start(self, k):
        p = self.p
        there, copy = self.own_copy(k)
        copy.start()

        @pl.when(p.z < p.layers - 1)
        def _():
            p.send(self.final.at[k], there, self.z_ret, self.z_back.at[k, p.z], p.up)

        @pl.when(p.z > 0)
        def _():
            p.send(self.final.at[k], there, self.z_ret, self.z_back.at[k, p.z], p.down)

    def z_return(self, s, k):
        p = self.p
        first, _, _, _ = self.axes(k)
        top = p.layers - 1

        def forward(j, ahead, to):
            shard = self.gath.at[k, p.core, first, j]
            p.arrived(shard, self.z_back.at[k, j])

            @pl.when(ahead)
            def _():
                p.send(shard, shard, self.z_ret, self.z_back.at[k, j], to)

        @pl.when(p.z >= s)
        def _():
            forward(jnp.maximum(p.z - s, 0), p.z < top, p.up)

        @pl.when(p.z <= top - s)
        def _():
            forward(jnp.minimum(p.z + s, top), p.z > 0, p.down)

        if s == top:
            self.own_copy(k)[1].wait()

    def send_first(self, k, chunks):
        p = self.p
        first, _, first_peer, _ = self.axes(k)
        mine = self.gath.at[chunks, p.core, first]
        for m in range(1, p.side):
            p.send(mine, mine, self.first_ret, self.first_back.at[k, m - 1], first_peer(m)[1])

    def send_core(self, k, chunks):
        p = self.p
        first, _, _, _ = self.axes(k)
        for m in range(1, p.side):
            came = self.gath.at[chunks, p.core, self.before(first, m)]
            p.arrived(came, self.first_back.at[k, m - 1])
        mine = self.gath.at[chunks, p.core]
        p.send(mine, mine, self.core_ret, self.core_back.at[k], p.other_core)

    def wide_z_return(self, k):
        self.z_return(self.p.layers - 1, k)
        self.send_first(k, k)

    def core_return(self, k):
        self.send_core(k, k)

    def finish(self, k):
        self.p.arrived(self.gath.at[k, 1 - self.p.core], self.core_back.at[k])

    def slim_z_return(self, base):
        p = self.p
        first, last, _, last_peer = self.axes(base)
        own = base + last
        self.z_return(p.layers - 1, own)
        mine = self.gath.at[own, p.core, first]
        for m in range(1, p.side):
            p.send(mine, mine, self.slim_ret, self.last_back.at[own, m - 1], last_peer(m)[1])

    def slim_last_return(self, base):
        p = self.p
        first, last, _, _ = self.axes(base)
        for m in range(1, p.side):
            k = base + self.before(last, m)
            p.arrived(self.gath.at[k, p.core, first], self.last_back.at[k, m - 1])
        self.send_first(base, pl.ds(base, p.side))

    def slim_core_return(self, base):
        self.send_core(base, pl.ds(base, self.p.side))

    def slim_finish(self, base):
        unit = self.gath.at[pl.ds(base, self.p.side), 1 - self.p.core]
        self.p.arrived(unit, self.core_back.at[base])

    def drain(self):
        p = self.p
        units = self.slims // p.side
        wides = self.count - self.slims
        chains = pl.ds(0, wides + units)
        p.sent(self.core_buf, self.core_out)
        p.sent(self.first_buf, self.first_out)
        p.sent(self.first_buf, self.first_ret)
        p.sent(self.core_buf, self.core_ret)
        p.sent(self.z_buf.at[chains, pl.ds(0, p.layers - 1)], self.z_out)
        middle = (p.z > 0) & (p.z < p.layers - 1)

        @pl.when(middle)
        def _():
            p.sent(self.z_buf.at[chains], self.z_ret)

        @pl.when(jnp.logical_not(middle))
        def _():
            p.sent(self.z_buf.at[chains, pl.ds(0, 1)], self.z_ret)

        if wides:
            p.sent(self.last_buf.at[pl.ds(0, wides)], self.last_out)
        if units:
            p.sent(self.first_buf.at[pl.ds(0, units)], self.slim_out)
            p.sent(self.first_buf.at[pl.ds(0, units)], self.slim_ret)


def reducer_scratch(count, side, layers, rows, wide):
    bufs = [
        pltpu.VMEM((count, side, layers, rows, wide), BF),
        pltpu.VMEM((count, side - 1, layers, rows, wide), BF),
        pltpu.VMEM((count, layers + 1, rows, wide), BF),
        pltpu.VMEM((count, side - 1, rows, wide), BF),
        pltpu.VMEM((count, rows, wide), BF),
        pltpu.VMEM((count, rows, wide), BF),
    ]
    recv = [
        DMA((count,)),
        DMA((count, side - 1)),
        DMA((count, layers + 1)),
        DMA((count, side - 1)),
        DMA((count,)),
        DMA((count, layers)),
        DMA((count, side - 1)),
        DMA((count,)),
        DMA((count, side - 1)),
    ]
    return bufs, recv, [DMA(())] * 9


def layer_kernel(cfg, *refs):
    refs = list(refs)

    def take(number):
        taken = refs[:number]
        del refs[:number]
        return taken

    (knowledge, expr_table, owner_ids, gene_row, expr_bin, lengths) = take(6)
    (gain1, bias1, w_query, b_query, w_key, w_value, b_value, w_out1, b_out1) = take(9)
    (gain2, bias2, w_in, b_in, w_out, b_out, cotangent) = take(7)
    mixed, table_grad, gath = take(3)
    know_v, wq_v, wk_v, wv_v, wo_v, win_v, wout_v, cot_v = take(8)
    load_sems, ids_out, ids_in, rows_out, rows_in, back_in, row_hot_v, slot_hot_v = take(8)
    ids_sem, rows_sem, ids_sent, rows_sent, back_sent = take(5)
    (embedded_v, attn_in_v, query_v, key_v, value_v, probs_v, context_v) = take(7)
    (hidden1_v, ffn_in_v, grad_ffn_v, acc_v, gn2_v, biases_v) = take(6)
    part, table_v, mixed_v, result_sems = take(4)
    bufs, recv, sent = take(6), take(9), take(9)
    assert not refs

    side, layers, cap, offsets = cfg
    place = Place(side, layers)
    devices = place.count
    red = Reducer(place, part, gath, bufs, recv, sent)
    tokens, width = embedded_v.shape
    table_rows = knowledge.shape[1]
    half = width // 2
    blocks = w_in.shape[1] // width
    count = part.shape[0]
    slots = devices * cap

    loads = [
        (knowledge, know_v),
        (w_query, wq_v),
        (w_key, wk_v),
        (w_value, wv_v),
        (w_out1, wo_v),
        (cotangent, cot_v),
    ]
    for j in range(blocks):
        loads.append((w_in.at[:, pl.ds(j * width, width)], win_v.at[j % 2]))
        loads.append((w_out.at[pl.ds(j * width, width)], wout_v.at[j % 2]))
    loads = [
        pltpu.make_async_copy(src, dst, load_sems.at[i]) for i, (src, dst) in enumerate(loads)
    ]
    for load in loads[: 6 + 4]:
        load.start()
    place.greet_all()

    def iota(shape, dim):
        return lax.broadcasted_iota(jnp.int32, shape, dim)

    def hot(condition):
        return jnp.where(condition, 1.0, 0.0).astype(BF)

    owner_row = owner_ids[...]
    owner_hot = hot(iota((devices, tokens), 0) == owner_row)
    earlier = hot(iota((tokens, tokens), 0) < iota((tokens, tokens), 1))
    before = dot(owner_hot, earlier)
    rank_row = column_sum(before * owner_hot.astype(F32)).astype(jnp.int32)
    slot_hot_v[...] = hot(iota((slots, tokens), 0) == owner_row * cap + rank_row)
    rank_hot = hot(iota((128, tokens), 0) == rank_row)
    named = (owner_hot.astype(F32) * (gene_row[...] + 1).astype(F32)).astype(BF)
    wanted = dot(named, rank_hot, 1, 1)
    for d in range(devices):
        ids_out[d] = wanted[d : d + 1]

    place.await_all()
    place.exchange_start(ids_out, ids_in, ids_sent, ids_sem)
    ids_in[place.me] = ids_out[place.me]
    loads[0].wait()
    table_sum = know_v[0].astype(F32)
    for k in range(1, know_v.shape[0]):
        table_sum = table_sum + know_v[k].astype(F32)
    table_sum = table_sum.astype(BF)
    expr_hot = hot(iota((expr_table.shape[0], tokens), 0) == expr_bin[...])
    expr_part = dot(expr_hot, expr_table[...], 0, 0)
    place.exchange_wait(ids_in, ids_sem)
    asked = ids_in[...].reshape(devices, 128).astype(BF)
    spread = hot(iota((slots, devices), 0) // cap == iota((slots, devices), 1))
    asked = dot(spread, asked)
    own_lane = lax.rem(iota((slots, 128), 0), cap) == iota((slots, 128), 1)
    asked = jnp.sum(jnp.where(own_lane, asked, 0.0), axis=1, keepdims=True)
    row_hot = hot(iota((slots, table_rows), 1) + 1 == asked.astype(jnp.int32))
    row_hot_v[...] = row_hot
    rows_out[...] = dot(row_hot, table_sum).astype(BF).reshape(devices, cap, width)
    place.exchange_start(rows_out, rows_in, rows_sent, rows_sem)
    rows_in[place.me] = rows_out[place.me]

    end = lengths[0]
    ends = [end]
    for c in range(1, lengths.shape[0]):
        end = end + lengths[c]
        ends.append(end)

    def segments(shape, dim):
        spot = iota(shape, dim)
        segment = jnp.zeros(shape, jnp.int32)
        for stop in ends:
            segment = segment + jnp.where(spot >= stop, 1, 0)
        return segment

    spot = lax.rem(iota((2 * tokens, tokens), 0), tokens)
    segment = jnp.zeros((2 * tokens, tokens), jnp.int32)
    for stop in ends:
        segment = segment + jnp.where(spot >= stop, 1, 0)
    same_cell = segment == segments((2 * tokens, tokens), 1)
    live = jnp.where(iota((tokens, 1), 0) < ends[-1], 1.0, 0.0)

    place.exchange_wait(rows_in, rows_sem)
    gathered = rows_in[...].reshape(slots, width)
    embedded_v[...] = dot(slot_hot_v[...], gathered, 0, 0) + expr_part
    for load in loads[1:5]:
        load.wait()

    xhat1, recip1 = standardise(embedded_v[...])
    attn_in_v[...] = (xhat1 * gain1[...].reshape(1, width) + bias1[...].reshape(1, width)).astype(BF)
    query_v[...] = (dot(attn_in_v[...], wq_v[...]) + b_query[...].reshape(1, width)).astype(BF)
    key_v[...] = dot(attn_in_v[...], wk_v[...]).astype(BF)
    value_v[...] = (dot(attn_in_v[...], wv_v[...]) + b_value[...].reshape(1, width)).astype(BF)
    low_lane = iota((tokens, PAIR), 1) < HEAD_DIM

    def two_heads(values):
        zero = jnp.zeros_like(values)
        return jnp.concatenate(
            [jnp.where(low_lane, values, zero), jnp.where(low_lane, zero, values)], axis=0
        )

    def one_of_two(values):
        return jnp.where(low_lane, values[:tokens], values[tokens:])

    for pair in range(width // PAIR):
        lanes = slice(pair * PAIR, (pair + 1) * PAIR)
        scores = dot(two_heads(query_v[:, lanes]), key_v[:, lanes], 1, 1) * SCALE
        scores = jnp.where(same_cell, scores, MASKED)
        scores = jnp.exp(scores - jnp.max(scores, axis=1, keepdims=True))
        probs = scores / jnp.sum(scores, axis=1, keepdims=True)
        probs_v[pair] = probs
        context_v[:, lanes] = one_of_two(dot(probs.astype(BF), value_v[:, lanes])).astype(BF)
    hidden1_v[...] = (
        embedded_v[...] + dot(context_v[...], wo_v[...]) + b_out1[...].reshape(1, width)
    )
    loads[5].wait()

    xhat2, recip2 = standardise(hidden1_v[...])
    ffn_in_v[...] = (xhat2 * gain2[...].reshape(1, width) + bias2[...].reshape(1, width)).astype(BF)
    grad_hidden2 = cot_v[...].astype(F32) * live
    grad_ffn_v[...] = grad_hidden2.astype(BF)
    acc_v[...] = jnp.zeros_like(acc_v)
    gn2_v[...] = jnp.zeros_like(gn2_v)
    biases_v[...] = jnp.zeros_like(biases_v)
    shard = part.shape[1:]
    plans = []
    for stages, lags in zip((red.wide_stages, red.slim_stages), offsets):
        reach = [0]
        for lag in lags:
            reach.append(reach[-1] + lag)
        assert len(reach) == len(stages)
        plans.append(list(zip(stages, reach)))
    longest = max(plan[-1][1] for plan in plans)

    def step(i):
        for slim, plan in enumerate(plans):
            for stage, lag in sorted(plan, key=lambda entry: -entry[1]):
                k = i - lag
                ahead = side - 1 if slim else 0
                low, high = (0, red.slims) if slim else (red.slims, count)
                if isinstance(k, int):
                    if low <= k < high and (not slim or k % side == ahead):
                        stage(k - ahead)
                elif low < high:
                    now = (k >= low) & (k < high)
                    if slim:
                        now = now & (lax.rem(k, side) == ahead)

                    @pl.when(now)
                    def _():
                        stage(k - ahead)

    def put(k, values):
        part[k] = values.reshape(shard).astype(BF)
        red.core_send(k)

    done = [0]

    def pipe(where):
        for _ in range(PIPE.get(where, 0)):
            step(done[0])
            done[0] += 1

    def put_bias(row, values):
        biases_v[pl.ds(2 * row, 1), :] = values[:, :half]
        biases_v[pl.ds(2 * row + 1, 1), :] = values[:, half:]

    for j in range(blocks):
        loads[6 + 2 * j].wait()
        loads[7 + 2 * j].wait()
        win, wout = win_v.at[j % 2], wout_v.at[j % 2]
        pre = dot(ffn_in_v[...], win[...]) + b_in[pl.ds(j * width, width)].reshape(1, width)
        square = pre * pre
        bend = jnp.tanh(GELU_SLOPE * (pre + GELU_CUBIC * square * pre))
        act = (0.5 * pre * (1.0 + bend)).astype(BF)
        slope = 0.5 * (1.0 + bend) + 0.5 * pre * (1.0 - bend * bend) * (
            GELU_SLOPE * (1.0 + 3.0 * GELU_CUBIC * square)
        )
        grad_pre = dot(grad_ffn_v[...], wout[...], 1, 1) * slope
        grad_pre = grad_pre.astype(BF)
        if j:
            for q in range(4):
                red.core_sum(4 * (j - 1) + q)
        for h in range(2):
            put(4 * j + h, dot(act, grad_ffn_v[:, h * half : (h + 1) * half], 0, 0))
        for h in range(2):
            put(4 * j + 2 + h, dot(ffn_in_v[...], grad_pre[:, h * half : (h + 1) * half], 0, 0))
        acc_v[...] += dot(act, wout[...])
        gn2_v[...] += dot(grad_pre, win[...], 1, 1)
        if j + 2 < blocks:
            loads[10 + 2 * j].start()
            loads[11 + 2 * j].start()
        put_bias(j, column_sum(grad_pre.astype(F32)))
        pipe(f'ffn{j}')
    at = 4 * blocks
    mixed_v[...] = (
        (hidden1_v[...] + acc_v[...] + b_out[...].reshape(1, width)) * live
    ).astype(BF)
    put_bias(blocks, column_sum(grad_ffn_v[...].astype(F32)))
    grad_normed2 = gn2_v[...]
    put_bias(blocks + 1, column_sum(grad_normed2 * xhat2))
    put_bias(blocks + 2, column_sum(grad_normed2))
    for q in range(4):
        red.core_sum(at - 4 + q)
    grad_hidden1 = grad_hidden2 + norm_back(xhat2, recip2, gain2[...].reshape(1, width), grad_normed2)
    acc_v[...] = grad_hidden1
    grad_attn = grad_hidden1.astype(BF)
    put_bias(blocks + 3, column_sum(grad_attn.astype(F32)))
    for h in range(2):
        put(at + h, dot(context_v[...], grad_attn[:, h * half : (h + 1) * half], 0, 0))
    pipe('out')
    gctx_v = ffn_in_v
    gctx_v[...] = dot(grad_attn, wo_v[...], 1, 1).astype(BF)
    gq_v, gk_v, gv_v = query_v, key_v, value_v

    for pair in range(width // PAIR):
        lanes = slice(pair * PAIR, (pair + 1) * PAIR)
        probs = probs_v[pair]
        grads = two_heads(gctx_v[:, lanes])
        grad_probs = dot(grads, value_v[:, lanes], 1, 1)
        inner = jnp.sum(probs * grad_probs, axis=1, keepdims=True)
        grad_scores = (probs * (grad_probs - inner)).astype(BF)
        grad_query = one_of_two(dot(grad_scores, key_v[:, lanes])) * SCALE
        grad_key = dot(grad_scores, two_heads(query_v[:, lanes]), 0, 0) * SCALE
        gq_v[:, lanes] = grad_query.astype(BF)
        gk_v[:, lanes] = grad_key.astype(BF)
        gv_v[:, lanes] = dot(probs.astype(BF), grads, 0, 0).astype(BF)
        pipe(f'pair{pair}')
    for q in range(2):
        red.core_sum(at + q)
    at += 2
    for grad in (gq_v, gk_v, gv_v):
        for h in range(2):
            put(at + h, dot(attn_in_v[...], grad[:, h * half : (h + 1) * half], 0, 0))
        at += 2
        pipe(f'grad{at}')
    put_bias(blocks + 4, column_sum(gq_v[...].astype(F32)))
    put_bias(blocks + 5, column_sum(gv_v[...].astype(F32)))
    grad_normed1 = dot(gq_v[...], wq_v[...], 1, 1)
    grad_normed1 = grad_normed1 + dot(gk_v[...], wk_v[...], 1, 1)
    grad_normed1 = grad_normed1 + dot(gv_v[...], wv_v[...], 1, 1)
    xhat1, recip1 = standardise(embedded_v[...])
    put_bias(blocks + 6, column_sum(grad_normed1 * xhat1))
    put_bias(blocks + 7, column_sum(grad_normed1))
    grad_embedded = acc_v[...] + norm_back(
        xhat1, recip1, gain1[...].reshape(1, width), grad_normed1
    )
    grad_embedded = grad_embedded.astype(BF)
    back_out = rows_out
    place.sent(rows_out.at[pl.ds(0, devices - 1)], rows_sent)
    back_out[...] = dot(slot_hot_v[...], grad_embedded).astype(BF).reshape(devices, cap, width)
    expr_grad = dot(expr_hot, grad_embedded)
    bins = expr_grad.shape[0]
    filler = jnp.zeros((width - 2 * bins - biases_v.shape[0], half), F32)
    put(
        at,
        jnp.concatenate([expr_grad[:, :half], expr_grad[:, half:], biases_v[...], filler], axis=0),
    )
    place.exchange_start(back_out, back_in, back_sent, ids_sem)
    pipe('back')
    back_in[place.me] = back_out[place.me]
    for k in range(at - 6, at + 1):
        red.core_sum(k)

    def later(i, carry):
        step(i)
        return carry

    middle = min(done[0] + MIDDLE, count + longest)
    lax.fori_loop(done[0], middle, later, 0)
    place.exchange_wait(back_in, ids_sem)
    table_v[...] = dot(row_hot_v[...], back_in[...].reshape(slots, width), 0, 0)
    results = [
        pltpu.make_async_copy(table_v, table_grad, result_sems.at[0]),
        pltpu.make_async_copy(mixed_v, mixed, result_sems.at[1]),
    ]
    for result in results:
        result.start()
    lax.fori_loop(middle, count + longest, later, 0)
    for result in results:
        result.wait()
    place.sent(ids_out.at[pl.ds(0, devices - 1)], ids_sent)
    place.sent(back_out.at[pl.ds(0, devices - 1)], back_sent)
    red.drain()


def layer(side, layers, args):
    (knowledge, expr_table, gene_owner, gene_row, expr_bin, cell_lengths) = args[:6]
    cotangent, w_in = args[21], args[17]
    tokens, width = cotangent.shape
    devices = 2 * side * side * layers
    cap = max(8, 2 * tokens // devices)
    slots = devices * cap
    table_rows = knowledge.shape[1]
    blocks = w_in.shape[1] // width
    count = 4 * blocks + 9
    half = width // 2
    shard = width // (2 * side * layers)
    whole = (count, 2, side, layers, shard, half)
    bufs, recv, sent = reducer_scratch(count, side, layers, shard, half)
    wide = lambda dtype: pltpu.VMEM((tokens, width), dtype)
    square = pltpu.VMEM((width, width), BF)
    scratch = [
        pltpu.VMEM(knowledge.shape, BF),
        square,
        square,
        square,
        square,
        pltpu.VMEM((2, width, width), BF),
        pltpu.VMEM((2, width, width), BF),
        wide(BF),
        DMA((6 + 2 * blocks,)),
        pltpu.VMEM((devices, 1, 128), F32),
        pltpu.VMEM((devices, 1, 128), F32),
        pltpu.VMEM((devices, cap, width), BF),
        pltpu.VMEM((devices, cap, width), BF),
        pltpu.VMEM((devices, cap, width), BF),
        pltpu.VMEM((slots, table_rows), BF),
        pltpu.VMEM((slots, tokens), BF),
        DMA((devices,)),
        DMA((devices,)),
        DMA(()),
        DMA(()),
        DMA(()),
        wide(F32),
        wide(BF),
        wide(BF),
        wide(BF),
        wide(BF),
        pltpu.VMEM((width // PAIR, 2 * tokens, tokens), F32),
        wide(BF),
        wide(F32),
        wide(BF),
        wide(BF),
        wide(F32),
        wide(F32),
        pltpu.VMEM((8 * ((2 * (blocks + 8) + 7) // 8), half), F32),
        pltpu.VMEM(whole, BF),
        pltpu.VMEM((table_rows, width), F32),
        wide(BF),
        DMA((2,)),
    ]
    vmem = pl.BlockSpec(memory_space=pltpu.VMEM)
    hbm = pl.BlockSpec(memory_space=pl.ANY)
    smem = pl.BlockSpec(memory_space=pltpu.SMEM)
    in_hbm = {0, 8, 10, 11, 13, 17, 19, 21}
    specs = [hbm if i in in_hbm else smem if i == 5 else vmem for i in range(22)]
    offsets = OFFSETS
    flops = 2 * tokens * (3 * (4 * width * width + 2 * width * w_in.shape[1]))
    return pl.pallas_call(
        functools.partial(layer_kernel, (side, layers, cap, offsets)),
        out_shape=(
            jax.ShapeDtypeStruct((tokens, width), BF),
            jax.ShapeDtypeStruct((table_rows, width), F32),
            jax.ShapeDtypeStruct(whole, BF),
        ),
        in_specs=specs,
        out_specs=(hbm, hbm, hbm),
        scratch_shapes=scratch + bufs + recv + sent,
        compiler_params=pltpu.CompilerParams(
            collective_id=1, has_side_effects=True, vmem_limit_bytes=VMEM_BYTES
        ),
        cost_estimate=pl.CostEstimate(flops=flops, bytes_accessed=40 << 20, transcendentals=0),
    )(
        knowledge,
        expr_table,
        gene_owner.reshape(1, tokens),
        gene_row.reshape(1, tokens),
        expr_bin.reshape(1, tokens),
        *args[5:],
    )


OFFSETS = ([2, 1, 1, 3, 2, 2, 1, 4, 4], [3, 2, 2, 1, 2, 1, 0, 3, 4, 3])
SLIM = 10
PIPE = {"ffn2": 2, "ffn3": 2, "pair2": 1, "pair4": 1, "grad20": 1, "grad22": 1, "grad24": 1, "back": 2}
MIDDLE = 14
VMEM_BYTES = 62 << 20
DEPTH = 8


def spread_kernel(gath, table_grad, mixed, *refs):
    (mixed_out, know_out, expr_out, gain1_out, bias1_out, wq_out, bq_out, wk_out, wv_out) = refs[:9]
    (bv_out, wo_out, bo1_out, gain2_out, bias2_out, win_out, bin_out, wout_out, bout_out) = refs[9:18]
    narrow, broad, small, table_v, in_sems, out_sems, know_sems, more_sems = refs[18:]
    count, width, half = gath.shape
    blocks = win_out.shape[1] // width
    places = []
    for j in range(blocks):
        rows = pl.ds(j * width, width)
        for h in range(2):
            places.append(wout_out.at[rows, pl.ds(h * half, half)])
        for h in range(2):
            places.append(win_out.at[:, pl.ds(j * width + h * half, half)])
    for out in (wo_out, wq_out, wk_out, wv_out):
        for h in range(2):
            places.append(out.at[:, pl.ds(h * half, half)])
    last = count - 1
    assert len(places) == last

    def fetch(k):
        return pltpu.make_async_copy(gath.at[k], narrow.at[k % DEPTH], in_sems.at[k % DEPTH])

    def store(k):
        return pltpu.make_async_copy(broad.at[k % DEPTH], places[k], out_sems.at[k % DEPTH])

    for k in range(DEPTH - 1):
        fetch(k).start()
    more = [
        pltpu.make_async_copy(gath.at[last, pl.ds(0, small.shape[0])], small, more_sems.at[0]),
        pltpu.make_async_copy(table_grad, table_v, more_sems.at[1]),
        pltpu.make_async_copy(mixed, mixed_out, more_sems.at[2]),
    ]
    for copy in more:
        copy.start()
    knows = [
        pltpu.make_async_copy(table_v, know_out.at[i], know_sems.at[i])
        for i in range(know_out.shape[0])
    ]

    def convert(k):
        fetch(k).wait()
        if k >= DEPTH:
            store(k - DEPTH).wait()
        broad[k % DEPTH] = narrow[k % DEPTH].astype(F32)
        store(k).start()
        if k + DEPTH < last:
            fetch(k + DEPTH).start()

    fetch(DEPTH - 1).start()
    for k in range(DEPTH):
        convert(k)
    more[1].wait()
    for know in knows:
        know.start()
    more[0].wait()
    bins = expr_out.shape[0]
    expr_out[:, :half] = small[pl.ds(0, bins), :].astype(F32)
    expr_out[:, half:] = small[pl.ds(bins, bins), :].astype(F32)
    biases = small[pl.ds(2 * bins, small.shape[0] - 2 * bins), :].astype(F32)

    def bias(i):
        return jnp.concatenate([biases[2 * i : 2 * i + 1], biases[2 * i + 1 : 2 * i + 2]], axis=1)[0]

    for j in range(blocks):
        bin_out[pl.ds(j * width, width)] = bias(j)
    for i, out in enumerate(
        (bout_out, gain2_out, bias2_out, bo1_out, bq_out, bv_out, gain1_out, bias1_out)
    ):
        out[...] = bias(blocks + i)
    for k in range(DEPTH, last):
        convert(k)
    for k in range(last - DEPTH, last):
        store(k).wait()
    for know in knows:
        know.wait()
    more[2].wait()


def spread(gath, table_grad, mixed, tables, bins, hidden):
    count, width, half = gath.shape
    shape = lambda *dims: jax.ShapeDtypeStruct(dims, F32)
    vector, square = shape(width), shape(width, width)
    vmem = pl.BlockSpec(memory_space=pltpu.VMEM)
    hbm = pl.BlockSpec(memory_space=pl.ANY)
    outs = (
        (jax.ShapeDtypeStruct(mixed.shape, mixed.dtype), hbm),
        (shape(tables, *table_grad.shape), hbm),
        (shape(bins, width), vmem),
        (vector, vmem),
        (vector, vmem),
        (square, hbm),
        (vector, vmem),
        (square, hbm),
        (square, hbm),
        (vector, vmem),
        (square, hbm),
        (vector, vmem),
        (vector, vmem),
        (vector, vmem),
        (shape(width, hidden), hbm),
        (shape(hidden), vmem),
        (shape(hidden, width), hbm),
        (vector, vmem),
    )
    return pl.pallas_call(
        spread_kernel,
        out_shape=tuple(out for out, _ in outs),
        in_specs=[pl.BlockSpec(memory_space=pltpu.HBM)] * 3,
        out_specs=tuple(spec for _, spec in outs),
        scratch_shapes=[
            pltpu.VMEM((DEPTH, width, half), BF),
            pltpu.VMEM((DEPTH, width, half), F32),
            pltpu.VMEM((2 * bins + 16 * ((2 * (hidden // width + 8) + 15) // 16), half), BF),
            pltpu.VMEM(table_grad.shape, F32),
            DMA((DEPTH,)),
            DMA((DEPTH,)),
            DMA((tables,)),
            DMA((3,)),
        ],
        compiler_params=pltpu.CompilerParams(vmem_limit_bytes=60 << 20),
        cost_estimate=pl.CostEstimate(flops=0, bytes_accessed=48 << 20, transcendentals=0),
    )(gath, table_grad, mixed)


def local(*args):
    layers = lax.axis_size("table")
    side = math.isqrt(lax.axis_size("dp") // 2)
    knowledge, expr_table, w_in = args[0], args[1], args[17]
    width, hidden = w_in.shape
    mixed, table_grad, total = layer(side, layers, args)
    total = total.reshape(-1, width, width // 2)
    return spread(total, table_grad, mixed, knowledge.shape[0], expr_table.shape[0], hidden)


def solution(mesh):
    rows = P(("dp", "table"))
    by_token = P(("dp", "table"), None)
    by_row = P(None, ("dp", "table"), None)
    in_specs = (by_row, P(), by_token, rows, rows, rows) + (P(),) * 15 + (by_token,)
    out_specs = (by_token, by_row) + (P(),) * 16
    return jax.shard_map(local, mesh=mesh, in_specs=in_specs, out_specs=out_specs, check_vma=False)
```

```python
import functools
import math

import jax
import jax.numpy as jnp
from jax import lax
from jax.experimental import pallas as pl
from jax.experimental.pallas import tpu as pltpu
from jax.sharding import PartitionSpec as P

HEAD_DIM = 64
PAIR = 2 * HEAD_DIM
SCALE = HEAD_DIM ** (-0.5)
LAYER_EPS = 1e-05
GELU_SLOPE = 0.7978845608028654
GELU_CUBIC = 0.044715
MASKED = -1e30
MESH = pl.DeviceIdType.MESH
BF = jnp.bfloat16
F32 = jnp.float32
DMA = pltpu.SemaphoreType.DMA


def dot(lhs, rhs, lhs_dim=1, rhs_dim=0):
    return lax.dot_general(
        lhs, rhs, (((lhs_dim,), (rhs_dim,)), ((), ())), preferred_element_type=F32
    )


def column_sum(values):
    return jnp.sum(values, axis=0, keepdims=True)


def row_mean(values):
    return jnp.mean(values, axis=1, keepdims=True)


def standardise(values):
    centred = values - row_mean(values)
    recip = lax.rsqrt(row_mean(centred * centred) + LAYER_EPS)
    return centred * recip, recip


def norm_back(xhat, recip, gain, grad):
    scaled = gain * grad
    return recip * (scaled - row_mean(scaled) - xhat * row_mean(scaled * xhat))


class Place:
    def __init__(self, side, layers):
        self.side, self.layers = side, layers
        dp = lax.axis_index("dp")
        self.z = lax.axis_index("table")
        self.a, self.b, self.core = dp // (2 * side), (dp // 2) % side, dp % 2
        self.me = dp * layers + self.z
        self.count = 2 * side * side * layers
        self.other_core = self.at(self.a, self.b, 1 - self.core, self.z)
        self.up = self.at(self.a, self.b, self.core, jnp.minimum(self.z + 1, layers - 1))
        self.down = self.at(self.a, self.b, self.core, jnp.maximum(self.z - 1, 0))

    def at(self, a, b, core, z):
        return ((a * self.side + b) * 2 + core, z)

    def flat(self, index):
        return (index // self.layers, lax.rem(index, self.layers))

    def copy(self, src, dst, send_sem, recv_sem, to):
        return pltpu.make_async_remote_copy(
            src_ref=src,
            dst_ref=dst,
            send_sem=send_sem,
            recv_sem=recv_sem,
            device_id=to,
            device_id_type=MESH,
        )

    def send(self, src, dst, send_sem, recv_sem, to):
        self.copy(src, dst, send_sem, recv_sem, to).start()

    def arrived(self, dst, recv_sem):
        self.copy(dst, dst, recv_sem, recv_sem, self.other_core).wait_recv()

    def sent(self, src, send_sem):
        self.copy(src, src, send_sem, send_sem, self.other_core).wait_send()

    def far_first(self):
        layers = self.layers
        return sorted(range(layers), key=lambda d: -min(d, layers - d))

    def each_other(self, act, offsets=None):
        layers = self.layers
        for dz in self.far_first() if offsets is None else offsets:

            def one(i, carry):
                act(i * layers + dz)
                return carry

            lax.fori_loop(0 if dz else 1, self.count // layers, one, 0)

    def greet_all(self):
        bar = pltpu.get_barrier_semaphore()

        def greet(step):
            to = self.flat(lax.rem(self.me + step, self.count))
            pl.semaphore_signal(bar, inc=1, device_id=to, device_id_type=MESH)

        self.each_other(greet)

    def await_all(self):
        pl.semaphore_wait(pltpu.get_barrier_semaphore(), self.count - 1)

    def exchange_start(self, out, into, send_sem, recv_sems, offsets=None):
        def start(step):
            to = lax.rem(self.me + step, self.count)
            self.send(out.at[to], into.at[self.me], send_sem, recv_sems.at[step], self.flat(to))

        self.each_other(start, offsets)

    def exchange_wait(self, into, recv_sems):
        def wait(step):
            origin = lax.rem(self.me + self.count - step, self.count)
            self.arrived(into.at[origin], recv_sems.at[step])

        self.each_other(wait)


class Reducer:
    def __init__(self, place, part, gath, bufs, recv, sent):
        self.p = place
        self.part, self.gath = part, gath
        self.core_buf, self.first_buf, self.z_buf, self.last_buf, self.z_sum, self.final = bufs
        self.core_in, self.first_in, self.z_in, self.last_in, self.own_in = recv[:5]
        self.z_back, self.first_back, self.core_back, self.last_back = recv[5:]
        self.core_out, self.first_out, self.first_ret, self.core_ret = sent[:4]
        self.z_out, self.z_ret, self.last_out, self.slim_out, self.slim_ret = sent[4:]
        layers = place.layers
        self.count = part.shape[0]
        self.slims = SLIM // place.side * place.side
        bind = functools.partial
        steps, returns = range(1, layers - 1), range(1, layers)
        self.wide_stages = (
            [self.first_sum]
            + [bind(self.z_step, s) for s in steps]
            + [self.z_final, self.last_sum]
            + [bind(self.z_return, s) for s in returns[:-1]]
            + [self.wide_z_return, self.core_return, self.finish]
        )
        self.slim_stages = (
            [self.slim_first_sum, self.slim_last_sum]
            + [self.of_own(bind(self.z_step, s)) for s in steps]
            + [self.slim_z_final]
            + [self.of_own(bind(self.z_return, s)) for s in returns[:-1]]
            + [self.slim_z_return, self.slim_last_return, self.slim_core_return, self.slim_finish]
        )

    def axes(self, k):
        p = self.p
        if isinstance(k, int):
            even = (k // p.side if k < self.slims else k) % 2 == 0
        else:
            even = lax.rem(jnp.where(k < self.slims, k // p.side, k), 2) == 0
        first = jnp.where(even, p.b, p.a)
        last = jnp.where(even, p.a, p.b)

        def first_peer(m):
            q = lax.rem(first + m, p.side)
            return q, p.at(jnp.where(even, p.a, q), jnp.where(even, q, p.b), p.core, p.z)

        def last_peer(m):
            q = lax.rem(last + m, p.side)
            return q, p.at(jnp.where(even, q, p.a), jnp.where(even, p.b, q), p.core, p.z)

        return first, last, first_peer, last_peer

    def before(self, position, m):
        return lax.rem(position - m + self.p.side, self.p.side)

    def of_own(self, act):
        return lambda base: act(base + self.axes(base)[1])

    def core_send(self, k):
        p = self.p
        p.send(
            self.part.at[k, 1 - p.core],
            self.core_buf.at[k],
            self.core_out,
            self.core_in.at[k],
            p.other_core,
        )

    def core_sum(self, k):
        p = self.p
        _, _, first_peer, _ = self.axes(k)
        p.arrived(self.core_buf.at[k], self.core_in.at[k])
        self.core_buf[k] = (
            self.core_buf[k].astype(F32) + self.part[k, p.core].astype(F32)
        ).astype(BF)
        for m in range(1, p.side):
            q, to = first_peer(m)
            p.send(
                self.core_buf.at[k, q],
                self.first_buf.at[k, m - 1],
                self.first_out,
                self.first_in.at[k, m - 1],
                to,
            )

    def add_first(self, k):
        p = self.p
        first, _, _, _ = self.axes(k)
        for m in range(1, p.side):
            p.arrived(self.first_buf.at[k, m - 1], self.first_in.at[k, m - 1])
        total = self.core_buf[k, first].astype(F32)
        for m in range(1, p.side):
            total = total + self.first_buf[k, m - 1].astype(F32)
        self.first_buf[k, 0] = total.astype(BF)

    def first_sum(self, k):
        self.add_first(k)
        self.z_start(k)

    def slim_first_sum(self, base):
        p = self.p
        for q in range(p.side):
            self.add_first(base + q)
        _, last, _, last_peer = self.axes(base)
        for m in range(1, p.side):
            q, to = last_peer(m)
            p.send(
                self.first_buf.at[base + q, 0],
                self.z_buf.at[base + last, pl.ds(0, p.layers)],
                self.slim_out,
                self.last_in.at[base + q, m - 1],
                to,
            )

    def slim_last_sum(self, base):
        p = self.p
        _, last, _, _ = self.axes(base)
        own = base + last
        total = self.first_buf[own, 0].astype(F32)
        for m in range(1, p.side):
            came = self.z_buf.at[base + self.before(last, m), pl.ds(0, p.layers)]
            p.arrived(came, self.last_in.at[own, m - 1])
            total = total + came[...].astype(F32)
        self.first_buf[own, 0] = total.astype(BF)
        self.z_start(own)

    def z_send(self, k, src, slot, to):
        self.p.send(src, self.z_buf.at[k, slot], self.z_out, self.z_in.at[k, slot], to)

    def z_start(self, k):
        p = self.p
        top = p.layers - 1

        @pl.when(p.z == 0)
        def _():
            for j in range(top, 0, -1):
                self.z_send(k, self.first_buf.at[k, 0, j], j if j > 1 else p.layers, p.up)

        @pl.when(p.z == top)
        def _():
            for j in range(0, top):
                self.z_send(k, self.first_buf.at[k, 0, j], j, p.down)

    def z_step(self, s, k):
        p = self.p
        top = p.layers - 1

        def add(j):
            p.arrived(self.z_buf.at[k, j], self.z_in.at[k, j])
            self.z_buf[k, j] = (
                self.z_buf[k, j].astype(F32) + self.first_buf[k, 0, j].astype(F32)
            ).astype(BF)
            return self.z_buf.at[k, j]

        @pl.when(p.z == s)
        def _():
            for j in range(top, s, -1):
                self.z_send(k, add(j), j if j > s + 1 else p.layers, p.up)

        @pl.when(p.z == top - s)
        def _():
            for j in range(0, top - s):
                self.z_send(k, add(j), j, p.down)

    def z_total(self, k, into):
        p = self.p
        top = p.layers - 1

        def arrival(slot):
            p.arrived(self.z_buf.at[k, slot], self.z_in.at[k, slot])
            return self.z_buf[k, slot].astype(F32)

        mine = self.first_buf[k, 0, p.z].astype(F32)

        @pl.when(p.z == 0)
        def _():
            into[k] = (mine + arrival(0)).astype(BF)

        @pl.when(p.z == top)
        def _():
            into[k] = (mine + arrival(p.layers)).astype(BF)

        @pl.when((p.z > 0) & (p.z < top))
        def _():
            into[k] = (mine + arrival(p.layers) + arrival(p.z)).astype(BF)

    def z_final(self, k):
        p = self.p
        _, _, _, last_peer = self.axes(k)
        self.z_total(k, self.z_sum)
        for m in range(1, p.side):
            _, to = last_peer(m)
            p.send(
                self.z_sum.at[k],
                self.last_buf.at[k, m - 1],
                self.last_out,
                self.last_in.at[k, m - 1],
                to,
            )

    def slim_z_final(self, base):
        own = base + self.axes(base)[1]
        self.z_total(own, self.final)
        self.z_return_start(own)

    def last_sum(self, k):
        p = self.p
        _, last, _, _ = self.axes(k)
        for m in range(1, p.side):
            p.arrived(self.last_buf.at[k, m - 1], self.last_in.at[k, m - 1])
        total = None
        for q in range(p.side):
            m = self.before(last, q)
            term = jnp.where(
                m == 0,
                self.z_sum[k].astype(F32),
                self.last_buf[k, jnp.maximum(m - 1, 0)].astype(F32),
            )
            total = term if total is None else total + term
        self.final[k] = total.astype(BF)
        self.z_return_start(k)

    def own_copy(self, k):
        p = self.p
        there = self.gath.at[k, p.core, self.axes(k)[0], p.z]
        return there, pltpu.make_async_copy(self.final.at[k], there, self.own_in.at[k])

    def z_return_start(self, k):
        p = self.p
        there, copy = self.own_copy(k)
        copy.start()

        @pl.when(p.z < p.layers - 1)
        def _():
            p.send(self.final.at[k], there, self.z_ret, self.z_back.at[k, p.z], p.up)

        @pl.when(p.z > 0)
        def _():
            p.send(self.final.at[k], there, self.z_ret, self.z_back.at[k, p.z], p.down)

    def z_return(self, s, k):
        p = self.p
        first, _, _, _ = self.axes(k)
        top = p.layers - 1

        def forward(j, ahead, to):
            shard = self.gath.at[k, p.core, first, j]
            p.arrived(shard, self.z_back.at[k, j])

            @pl.when(ahead)
            def _():
                p.send(shard, shard, self.z_ret, self.z_back.at[k, j], to)

        @pl.when(p.z >= s)
        def _():
            forward(jnp.maximum(p.z - s, 0), p.z < top, p.up)

        @pl.when(p.z <= top - s)
        def _():
            forward(jnp.minimum(p.z + s, top), p.z > 0, p.down)

        if s == top:
            self.own_copy(k)[1].wait()

    def send_first(self, k, chunks):
        p = self.p
        first, _, first_peer, _ = self.axes(k)
        mine = self.gath.at[chunks, p.core, first]
        for m in range(1, p.side):
            p.send(mine, mine, self.first_ret, self.first_back.at[k, m - 1], first_peer(m)[1])

    def send_core(self, k, chunks):
        p = self.p
        first, _, _, _ = self.axes(k)
        for m in range(1, p.side):
            came = self.gath.at[chunks, p.core, self.before(first, m)]
            p.arrived(came, self.first_back.at[k, m - 1])
        mine = self.gath.at[chunks, p.core]
        p.send(mine, mine, self.core_ret, self.core_back.at[k], p.other_core)

    def wide_z_return(self, k):
        self.z_return(self.p.layers - 1, k)
        self.send_first(k, k)

    def core_return(self, k):
        self.send_core(k, k)

    def finish(self, k):
        self.p.arrived(self.gath.at[k, 1 - self.p.core], self.core_back.at[k])

    def slim_z_return(self, base):
        p = self.p
        first, last, _, last_peer = self.axes(base)
        own = base + last
        self.z_return(p.layers - 1, own)
        mine = self.gath.at[own, p.core, first]
        for m in range(1, p.side):
            p.send(mine, mine, self.slim_ret, self.last_back.at[own, m - 1], last_peer(m)[1])

    def slim_last_return(self, base):
        p = self.p
        first, last, _, _ = self.axes(base)
        for m in range(1, p.side):
            k = base + self.before(last, m)
            p.arrived(self.gath.at[k, p.core, first], self.last_back.at[k, m - 1])
        self.send_first(base, pl.ds(base, p.side))

    def slim_core_return(self, base):
        self.send_core(base, pl.ds(base, self.p.side))

    def slim_finish(self, base):
        unit = self.gath.at[pl.ds(base, self.p.side), 1 - self.p.core]
        self.p.arrived(unit, self.core_back.at[base])

    def drain(self):
        p = self.p
        units = self.slims // p.side
        wides = self.count - self.slims
        chains = pl.ds(0, wides + units)
        p.sent(self.core_buf, self.core_out)
        p.sent(self.first_buf, self.first_out)
        p.sent(self.first_buf, self.first_ret)
        p.sent(self.core_buf, self.core_ret)
        p.sent(self.z_buf.at[chains, pl.ds(0, p.layers - 1)], self.z_out)
        middle = (p.z > 0) & (p.z < p.layers - 1)

        @pl.when(middle)
        def _():
            p.sent(self.z_buf.at[chains], self.z_ret)

        @pl.when(jnp.logical_not(middle))
        def _():
            p.sent(self.z_buf.at[chains, pl.ds(0, 1)], self.z_ret)

        if wides:
            p.sent(self.last_buf.at[pl.ds(0, wides)], self.last_out)
        if units:
            p.sent(self.first_buf.at[pl.ds(0, units)], self.slim_out)
            p.sent(self.first_buf.at[pl.ds(0, units)], self.slim_ret)


def reducer_scratch(count, side, layers, rows, wide):
    bufs = [
        pltpu.VMEM((count, side, layers, rows, wide), BF),
        pltpu.VMEM((count, side - 1, layers, rows, wide), BF),
        pltpu.VMEM((count, layers + 1, rows, wide), BF),
        pltpu.VMEM((count, side - 1, rows, wide), BF),
        pltpu.VMEM((count, rows, wide), BF),
        pltpu.VMEM((count, rows, wide), BF),
    ]
    recv = [
        DMA((count,)),
        DMA((count, side - 1)),
        DMA((count, layers + 1)),
        DMA((count, side - 1)),
        DMA((count,)),
        DMA((count, layers)),
        DMA((count, side - 1)),
        DMA((count,)),
        DMA((count, side - 1)),
    ]
    return bufs, recv, [DMA(())] * 9


def layer_kernel(cfg, *refs):
    refs = list(refs)

    def take(number):
        taken = refs[:number]
        del refs[:number]
        return taken

    (knowledge, expr_table, owner_ids, gene_row, expr_bin, lengths) = take(6)
    (gain1, bias1, w_query, b_query, w_key, w_value, b_value, w_out1, b_out1) = take(9)
    (gain2, bias2, w_in, b_in, w_out, b_out, cotangent) = take(7)
    mixed, table_grad, gath = take(3)
    know_v, wq_v, wk_v, wv_v, wo_v, win_v, wout_v, cot_v = take(8)
    load_sems, ids_out, ids_in, rows_out, rows_in, back_in, row_hot_v, slot_hot_v = take(8)
    ids_sem, rows_sem, ids_sent, rows_sent, back_sent = take(5)
    (embedded_v, attn_in_v, query_v, key_v, value_v, probs_v, context_v) = take(7)
    (hidden1_v, ffn_in_v, grad_ffn_v, acc_v, gn2_v, biases_v) = take(6)
    part, table_v, mixed_v, result_sems = take(4)
    bufs, recv, sent = take(6), take(9), take(9)
    assert not refs

    side, layers, cap, offsets = cfg
    place = Place(side, layers)
    devices = place.count
    red = Reducer(place, part, gath, bufs, recv, sent)
    tokens, width = embedded_v.shape
    table_rows = knowledge.shape[1]
    half = width // 2
    blocks = w_in.shape[1] // width
    count = part.shape[0]
    slots = devices * cap

    loads = [
        (knowledge, know_v),
        (w_query, wq_v),
        (w_key, wk_v),
        (w_value, wv_v),
        (w_out1, wo_v),
        (cotangent, cot_v),
    ]
    for j in range(blocks):
        loads.append((w_in.at[:, pl.ds(j * width, width)], win_v.at[j % 2]))
        loads.append((w_out.at[pl.ds(j * width, width)], wout_v.at[j % 2]))
    loads = [
        pltpu.make_async_copy(src, dst, load_sems.at[i]) for i, (src, dst) in enumerate(loads)
    ]
    for load in loads[: 6 + 4]:
        load.start()
    place.greet_all()

    def iota(shape, dim):
        return lax.broadcasted_iota(jnp.int32, shape, dim)

    def hot(condition):
        return jnp.where(condition, 1.0, 0.0).astype(BF)

    owner_row = owner_ids[...]
    owner_hot = hot(iota((devices, tokens), 0) == owner_row)
    earlier = hot(iota((tokens, tokens), 0) < iota((tokens, tokens), 1))
    before = dot(owner_hot, earlier)
    rank_row = column_sum(before * owner_hot.astype(F32)).astype(jnp.int32)
    slot_hot_v[...] = hot(iota((slots, tokens), 0) == owner_row * cap + rank_row)
    rank_hot = hot(iota((128, tokens), 0) == rank_row)
    named = (owner_hot.astype(F32) * (gene_row[...] + 1).astype(F32)).astype(BF)
    wanted = dot(named, rank_hot, 1, 1)
    for d in range(devices):
        ids_out[d] = wanted[d : d + 1]

    place.await_all()
    place.exchange_start(ids_out, ids_in, ids_sent, ids_sem)
    ids_in[place.me] = ids_out[place.me]
    loads[0].wait()
    table_sum = know_v[0].astype(F32)
    for k in range(1, know_v.shape[0]):
        table_sum = table_sum + know_v[k].astype(F32)
    table_sum = table_sum.astype(BF)
    expr_hot = hot(iota((expr_table.shape[0], tokens), 0) == expr_bin[...])
    expr_part = dot(expr_hot, expr_table[...], 0, 0)
    place.exchange_wait(ids_in, ids_sem)
    asked = ids_in[...].reshape(devices, 128).astype(BF)
    spread = hot(iota((slots, devices), 0) // cap == iota((slots, devices), 1))
    asked = dot(spread, asked)
    own_lane = lax.rem(iota((slots, 128), 0), cap) == iota((slots, 128), 1)
    asked = jnp.sum(jnp.where(own_lane, asked, 0.0), axis=1, keepdims=True)
    row_hot = hot(iota((slots, table_rows), 1) + 1 == asked.astype(jnp.int32))
    row_hot_v[...] = row_hot
    rows_out[...] = dot(row_hot, table_sum).astype(BF).reshape(devices, cap, width)
    place.exchange_start(rows_out, rows_in, rows_sent, rows_sem)
    rows_in[place.me] = rows_out[place.me]

    end = lengths[0]
    ends = [end]
    for c in range(1, lengths.shape[0]):
        end = end + lengths[c]
        ends.append(end)

    def segments(shape, dim):
        spot = iota(shape, dim)
        segment = jnp.zeros(shape, jnp.int32)
        for stop in ends:
            segment = segment + jnp.where(spot >= stop, 1, 0)
        return segment

    spot = lax.rem(iota((2 * tokens, tokens), 0), tokens)
    segment = jnp.zeros((2 * tokens, tokens), jnp.int32)
    for stop in ends:
        segment = segment + jnp.where(spot >= stop, 1, 0)
    same_cell = segment == segments((2 * tokens, tokens), 1)
    live = jnp.where(iota((tokens, 1), 0) < ends[-1], 1.0, 0.0)

    place.exchange_wait(rows_in, rows_sem)
    gathered = rows_in[...].reshape(slots, width)
    embedded_v[...] = dot(slot_hot_v[...], gathered, 0, 0) + expr_part
    for load in loads[1:5]:
        load.wait()

    xhat1, recip1 = standardise(embedded_v[...])
    attn_in_v[...] = (xhat1 * gain1[...].reshape(1, width) + bias1[...].reshape(1, width)).astype(BF)
    query_v[...] = (dot(attn_in_v[...], wq_v[...]) + b_query[...].reshape(1, width)).astype(BF)
    key_v[...] = dot(attn_in_v[...], wk_v[...]).astype(BF)
    value_v[...] = (dot(attn_in_v[...], wv_v[...]) + b_value[...].reshape(1, width)).astype(BF)
    low_lane = iota((tokens, PAIR), 1) < HEAD_DIM

    def two_heads(values):
        zero = jnp.zeros_like(values)
        return jnp.concatenate(
            [jnp.where(low_lane, values, zero), jnp.where(low_lane, zero, values)], axis=0
        )

    def one_of_two(values):
        return jnp.where(low_lane, values[:tokens], values[tokens:])

    for pair in range(width // PAIR):
        lanes = slice(pair * PAIR, (pair + 1) * PAIR)
        scores = dot(two_heads(query_v[:, lanes]), key_v[:, lanes], 1, 1) * SCALE
        scores = jnp.where(same_cell, scores, MASKED)
        scores = jnp.exp(scores - jnp.max(scores, axis=1, keepdims=True))
        probs = scores / jnp.sum(scores, axis=1, keepdims=True)
        probs_v[pair] = probs
        context_v[:, lanes] = one_of_two(dot(probs.astype(BF), value_v[:, lanes])).astype(BF)
    hidden1_v[...] = (
        embedded_v[...] + dot(context_v[...], wo_v[...]) + b_out1[...].reshape(1, width)
    )
    loads[5].wait()

    xhat2, recip2 = standardise(hidden1_v[...])
    ffn_in_v[...] = (xhat2 * gain2[...].reshape(1, width) + bias2[...].reshape(1, width)).astype(BF)
    grad_hidden2 = cot_v[...].astype(F32) * live
    grad_ffn_v[...] = grad_hidden2.astype(BF)
    acc_v[...] = jnp.zeros_like(acc_v)
    gn2_v[...] = jnp.zeros_like(gn2_v)
    biases_v[...] = jnp.zeros_like(biases_v)
    shard = part.shape[1:]
    plans = []
    for stages, lags in zip((red.wide_stages, red.slim_stages), offsets):
        reach = [0]
        for lag in lags:
            reach.append(reach[-1] + lag)
        assert len(reach) == len(stages)
        plans.append(list(zip(stages, reach)))
    longest = max(plan[-1][1] for plan in plans)

    def step(i):
        for slim, plan in enumerate(plans):
            for stage, lag in sorted(plan, key=lambda entry: -entry[1]):
                k = i - lag
                ahead = side - 1 if slim else 0
                low, high = (0, red.slims) if slim else (red.slims, count)
                if isinstance(k, int):
                    if low <= k < high and (not slim or k % side == ahead):
                        stage(k - ahead)
                elif low < high:
                    now = (k >= low) & (k < high)
                    if slim:
                        now = now & (lax.rem(k, side) == ahead)

                    @pl.when(now)
                    def _():
                        stage(k - ahead)

    def put(k, values):
        part[k] = values.reshape(shard).astype(BF)
        red.core_send(k)

    done = [0]

    def pipe(where):
        for _ in range(PIPE.get(where, 0)):
            step(done[0])
            done[0] += 1

    def put_bias(row, values):
        biases_v[pl.ds(2 * row, 1), :] = values[:, :half]
        biases_v[pl.ds(2 * row + 1, 1), :] = values[:, half:]

    for j in range(blocks):
        loads[6 + 2 * j].wait()
        loads[7 + 2 * j].wait()
        win, wout = win_v.at[j % 2], wout_v.at[j % 2]
        pre = dot(ffn_in_v[...], win[...]) + b_in[pl.ds(j * width, width)].reshape(1, width)
        square = pre * pre
        bend = jnp.tanh(GELU_SLOPE * (pre + GELU_CUBIC * square * pre))
        act = (0.5 * pre * (1.0 + bend)).astype(BF)
        slope = 0.5 * (1.0 + bend) + 0.5 * pre * (1.0 - bend * bend) * (
            GELU_SLOPE * (1.0 + 3.0 * GELU_CUBIC * square)
        )
        grad_pre = dot(grad_ffn_v[...], wout[...], 1, 1) * slope
        grad_pre = grad_pre.astype(BF)
        if j:
            for q in range(4):
                red.core_sum(4 * (j - 1) + q)
        for h in range(2):
            put(4 * j + h, dot(act, grad_ffn_v[:, h * half : (h + 1) * half], 0, 0))
        for h in range(2):
            put(4 * j + 2 + h, dot(ffn_in_v[...], grad_pre[:, h * half : (h + 1) * half], 0, 0))
        acc_v[...] += dot(act, wout[...])
        gn2_v[...] += dot(grad_pre, win[...], 1, 1)
        if j + 2 < blocks:
            loads[10 + 2 * j].start()
            loads[11 + 2 * j].start()
        put_bias(j, column_sum(grad_pre.astype(F32)))
        pipe(f'ffn{j}')
    at = 4 * blocks
    mixed_v[...] = (
        (hidden1_v[...] + acc_v[...] + b_out[...].reshape(1, width)) * live
    ).astype(BF)
    put_bias(blocks, column_sum(grad_ffn_v[...].astype(F32)))
    grad_normed2 = gn2_v[...]
    put_bias(blocks + 1, column_sum(grad_normed2 * xhat2))
    put_bias(blocks + 2, column_sum(grad_normed2))
    for q in range(4):
        red.core_sum(at - 4 + q)
    grad_hidden1 = grad_hidden2 + norm_back(xhat2, recip2, gain2[...].reshape(1, width), grad_normed2)
    acc_v[...] = grad_hidden1
    grad_attn = grad_hidden1.astype(BF)
    put_bias(blocks + 3, column_sum(grad_attn.astype(F32)))
    for h in range(2):
        put(at + h, dot(context_v[...], grad_attn[:, h * half : (h + 1) * half], 0, 0))
    pipe('out')
    gctx_v = ffn_in_v
    gctx_v[...] = dot(grad_attn, wo_v[...], 1, 1).astype(BF)
    gq_v, gk_v, gv_v = query_v, key_v, value_v

    for pair in range(width // PAIR):
        lanes = slice(pair * PAIR, (pair + 1) * PAIR)
        probs = probs_v[pair]
        grads = two_heads(gctx_v[:, lanes])
        grad_probs = dot(grads, value_v[:, lanes], 1, 1)
        inner = jnp.sum(probs * grad_probs, axis=1, keepdims=True)
        grad_scores = (probs * (grad_probs - inner)).astype(BF)
        grad_query = one_of_two(dot(grad_scores, key_v[:, lanes])) * SCALE
        grad_key = dot(grad_scores, two_heads(query_v[:, lanes]), 0, 0) * SCALE
        gq_v[:, lanes] = grad_query.astype(BF)
        gk_v[:, lanes] = grad_key.astype(BF)
        gv_v[:, lanes] = dot(probs.astype(BF), grads, 0, 0).astype(BF)
        pipe(f'pair{pair}')
    for q in range(2):
        red.core_sum(at + q)
    at += 2
    for grad in (gq_v, gk_v, gv_v):
        for h in range(2):
            put(at + h, dot(attn_in_v[...], grad[:, h * half : (h + 1) * half], 0, 0))
        at += 2
        pipe(f'grad{at}')
    put_bias(blocks + 4, column_sum(gq_v[...].astype(F32)))
    put_bias(blocks + 5, column_sum(gv_v[...].astype(F32)))
    grad_normed1 = dot(gq_v[...], wq_v[...], 1, 1)
    grad_normed1 = grad_normed1 + dot(gk_v[...], wk_v[...], 1, 1)
    grad_normed1 = grad_normed1 + dot(gv_v[...], wv_v[...], 1, 1)
    xhat1, recip1 = standardise(embedded_v[...])
    put_bias(blocks + 6, column_sum(grad_normed1 * xhat1))
    put_bias(blocks + 7, column_sum(grad_normed1))
    grad_embedded = acc_v[...] + norm_back(
        xhat1, recip1, gain1[...].reshape(1, width), grad_normed1
    )
    grad_embedded = grad_embedded.astype(BF)
    back_out = rows_out
    place.sent(rows_out.at[pl.ds(0, devices - 1)], rows_sent)
    back_out[...] = dot(slot_hot_v[...], grad_embedded).astype(BF).reshape(devices, cap, width)
    expr_grad = dot(expr_hot, grad_embedded)
    bins = expr_grad.shape[0]
    filler = jnp.zeros((width - 2 * bins - biases_v.shape[0], half), F32)
    put(
        at,
        jnp.concatenate([expr_grad[:, :half], expr_grad[:, half:], biases_v[...], filler], axis=0),
    )
    pipe('back')
    back_in[place.me] = back_out[place.me]
    for k in range(at - 6, at + 1):
        red.core_sum(k)

    def later(i, carry):
        step(i)
        return carry

    total = count + longest
    middle = min(max(MIDDLE, done[0]), total)
    lax.fori_loop(done[0], middle, later, 0)
    for dz in place.far_first():
        place.exchange_start(back_out, back_in, back_sent, ids_sem, [dz])
        if middle < total:
            step(middle)
            middle += 1
    end = min(middle + SETTLE, total)
    lax.fori_loop(middle, end, later, 0)
    place.exchange_wait(back_in, ids_sem)
    table_v[...] = dot(row_hot_v[...], back_in[...].reshape(slots, width), 0, 0)
    results = [
        pltpu.make_async_copy(table_v, table_grad, result_sems.at[0]),
        pltpu.make_async_copy(mixed_v, mixed, result_sems.at[1]),
    ]
    for result in results:
        result.start()
    lax.fori_loop(end, total, later, 0)
    for result in results:
        result.wait()
    place.sent(ids_out.at[pl.ds(0, devices - 1)], ids_sent)
    place.sent(back_out.at[pl.ds(0, devices - 1)], back_sent)
    red.drain()


def layer(side, layers, args):
    (knowledge, expr_table, gene_owner, gene_row, expr_bin, cell_lengths) = args[:6]
    cotangent, w_in = args[21], args[17]
    tokens, width = cotangent.shape
    devices = 2 * side * side * layers
    cap = max(8, 2 * tokens // devices)
    slots = devices * cap
    table_rows = knowledge.shape[1]
    blocks = w_in.shape[1] // width
    count = 4 * blocks + 9
    half = width // 2
    shard = width // (2 * side * layers)
    whole = (count, 2, side, layers, shard, half)
    bufs, recv, sent = reducer_scratch(count, side, layers, shard, half)
    wide = lambda dtype: pltpu.VMEM((tokens, width), dtype)
    square = pltpu.VMEM((width, width), BF)
    scratch = [
        pltpu.VMEM(knowledge.shape, BF),
        square,
        square,
        square,
        square,
        pltpu.VMEM((2, width, width), BF),
        pltpu.VMEM((2, width, width), BF),
        wide(BF),
        DMA((6 + 2 * blocks,)),
        pltpu.VMEM((devices, 1, 128), F32),
        pltpu.VMEM((devices, 1, 128), F32),
        pltpu.VMEM((devices, cap, width), BF),
        pltpu.VMEM((devices, cap, width), BF),
        pltpu.VMEM((devices, cap, width), BF),
        pltpu.VMEM((slots, table_rows), BF),
        pltpu.VMEM((slots, tokens), BF),
        DMA((devices,)),
        DMA((devices,)),
        DMA(()),
        DMA(()),
        DMA(()),
        wide(F32),
        wide(BF),
        wide(BF),
        wide(BF),
        wide(BF),
        pltpu.VMEM((width // PAIR, 2 * tokens, tokens), F32),
        wide(BF),
        wide(F32),
        wide(BF),
        wide(BF),
        wide(F32),
        wide(F32),
        pltpu.VMEM((8 * ((2 * (blocks + 8) + 7) // 8), half), F32),
        pltpu.VMEM(whole, BF),
        pltpu.VMEM((table_rows, width), F32),
        wide(BF),
        DMA((2,)),
    ]
    vmem = pl.BlockSpec(memory_space=pltpu.VMEM)
    hbm = pl.BlockSpec(memory_space=pl.ANY)
    smem = pl.BlockSpec(memory_space=pltpu.SMEM)
    in_hbm = {0, 8, 10, 11, 13, 17, 19, 21}
    specs = [hbm if i in in_hbm else smem if i == 5 else vmem for i in range(22)]
    offsets = OFFSETS
    flops = 2 * tokens * (3 * (4 * width * width + 2 * width * w_in.shape[1]))
    return pl.pallas_call(
        functools.partial(layer_kernel, (side, layers, cap, offsets)),
        out_shape=(
            jax.ShapeDtypeStruct((tokens, width), BF),
            jax.ShapeDtypeStruct((table_rows, width), F32),
            jax.ShapeDtypeStruct(whole, BF),
        ),
        in_specs=specs,
        out_specs=(hbm, hbm, hbm),
        scratch_shapes=scratch + bufs + recv + sent,
        compiler_params=pltpu.CompilerParams(
            collective_id=1, has_side_effects=True, vmem_limit_bytes=VMEM_BYTES
        ),
        cost_estimate=pl.CostEstimate(flops=flops, bytes_accessed=40 << 20, transcendentals=0),
    )(
        knowledge,
        expr_table,
        gene_owner.reshape(1, tokens),
        gene_row.reshape(1, tokens),
        expr_bin.reshape(1, tokens),
        *args[5:],
    )


OFFSETS = ([2, 1, 1, 3, 2, 2, 1, 6, 6], [4, 2, 2, 1, 2, 1, 0, 3, 7, 2])
SLIM = 10
PIPE = {"ffn2": 2, "ffn3": 2, "pair2": 2, "pair4": 1, "grad20": 1, "grad22": 1, "grad24": 2, "back": 1, "pair5": 1}
MIDDLE = 35
SETTLE = 8
VMEM_BYTES = 62 << 20
DEPTH = 8


def spread_kernel(gath, table_grad, mixed, *refs):
    (mixed_out, know_out, expr_out, gain1_out, bias1_out, wq_out, bq_out, wk_out, wv_out) = refs[:9]
    (bv_out, wo_out, bo1_out, gain2_out, bias2_out, win_out, bin_out, wout_out, bout_out) = refs[9:18]
    narrow, broad, small, table_v, in_sems, out_sems, know_sems, more_sems = refs[18:]
    count, width, half = gath.shape
    blocks = win_out.shape[1] // width
    places = []
    for j in range(blocks):
        rows = pl.ds(j * width, width)
        for h in range(2):
            places.append(wout_out.at[rows, pl.ds(h * half, half)])
        for h in range(2):
            places.append(win_out.at[:, pl.ds(j * width + h * half, half)])
    for out in (wo_out, wq_out, wk_out, wv_out):
        for h in range(2):
            places.append(out.at[:, pl.ds(h * half, half)])
    last = count - 1
    assert len(places) == last

    def fetch(k):
        return pltpu.make_async_copy(gath.at[k], narrow.at[k % DEPTH], in_sems.at[k % DEPTH])

    def store(k):
        return pltpu.make_async_copy(broad.at[k % DEPTH], places[k], out_sems.at[k % DEPTH])

    for k in range(DEPTH - 1):
        fetch(k).start()
    more = [
        pltpu.make_async_copy(gath.at[last, pl.ds(0, small.shape[0])], small, more_sems.at[0]),
        pltpu.make_async_copy(table_grad, table_v, more_sems.at[1]),
        pltpu.make_async_copy(mixed, mixed_out, more_sems.at[2]),
    ]
    for copy in more:
        copy.start()
    knows = [
        pltpu.make_async_copy(table_v, know_out.at[i], know_sems.at[i])
        for i in range(know_out.shape[0])
    ]

    def convert(k):
        fetch(k).wait()
        if k >= DEPTH:
            store(k - DEPTH).wait()
        broad[k % DEPTH] = narrow[k % DEPTH].astype(F32)
        store(k).start()
        if k + DEPTH < last:
            fetch(k + DEPTH).start()

    fetch(DEPTH - 1).start()
    for k in range(DEPTH):
        convert(k)
    more[1].wait()
    for know in knows:
        know.start()
    more[0].wait()
    bins = expr_out.shape[0]
    expr_out[:, :half] = small[pl.ds(0, bins), :].astype(F32)
    expr_out[:, half:] = small[pl.ds(bins, bins), :].astype(F32)
    biases = small[pl.ds(2 * bins, small.shape[0] - 2 * bins), :].astype(F32)

    def bias(i):
        return jnp.concatenate([biases[2 * i : 2 * i + 1], biases[2 * i + 1 : 2 * i + 2]], axis=1)[0]

    for j in range(blocks):
        bin_out[pl.ds(j * width, width)] = bias(j)
    for i, out in enumerate(
        (bout_out, gain2_out, bias2_out, bo1_out, bq_out, bv_out, gain1_out, bias1_out)
    ):
        out[...] = bias(blocks + i)
    for k in range(DEPTH, last):
        convert(k)
    for k in range(last - DEPTH, last):
        store(k).wait()
    for know in knows:
        know.wait()
    more[2].wait()


def spread(gath, table_grad, mixed, tables, bins, hidden):
    count, width, half = gath.shape
    shape = lambda *dims: jax.ShapeDtypeStruct(dims, F32)
    vector, square = shape(width), shape(width, width)
    vmem = pl.BlockSpec(memory_space=pltpu.VMEM)
    hbm = pl.BlockSpec(memory_space=pl.ANY)
    outs = (
        (jax.ShapeDtypeStruct(mixed.shape, mixed.dtype), hbm),
        (shape(tables, *table_grad.shape), hbm),
        (shape(bins, width), vmem),
        (vector, vmem),
        (vector, vmem),
        (square, hbm),
        (vector, vmem),
        (square, hbm),
        (square, hbm),
        (vector, vmem),
        (square, hbm),
        (vector, vmem),
        (vector, vmem),
        (vector, vmem),
        (shape(width, hidden), hbm),
        (shape(hidden), vmem),
        (shape(hidden, width), hbm),
        (vector, vmem),
    )
    return pl.pallas_call(
        spread_kernel,
        out_shape=tuple(out for out, _ in outs),
        in_specs=[pl.BlockSpec(memory_space=pltpu.HBM)] * 3,
        out_specs=tuple(spec for _, spec in outs),
        scratch_shapes=[
            pltpu.VMEM((DEPTH, width, half), BF),
            pltpu.VMEM((DEPTH, width, half), F32),
            pltpu.VMEM((2 * bins + 16 * ((2 * (hidden // width + 8) + 15) // 16), half), BF),
            pltpu.VMEM(table_grad.shape, F32),
            DMA((DEPTH,)),
            DMA((DEPTH,)),
            DMA((tables,)),
            DMA((3,)),
        ],
        compiler_params=pltpu.CompilerParams(vmem_limit_bytes=60 << 20),
        cost_estimate=pl.CostEstimate(flops=0, bytes_accessed=48 << 20, transcendentals=0),
    )(gath, table_grad, mixed)


def local(*args):
    layers = lax.axis_size("table")
    side = math.isqrt(lax.axis_size("dp") // 2)
    knowledge, expr_table, w_in = args[0], args[1], args[17]
    width, hidden = w_in.shape
    mixed, table_grad, total = layer(side, layers, args)
    total = total.reshape(-1, width, width // 2)
    return spread(total, table_grad, mixed, knowledge.shape[0], expr_table.shape[0], hidden)


def solution(mesh):
    rows = P(("dp", "table"))
    by_token = P(("dp", "table"), None)
    by_row = P(None, ("dp", "table"), None)
    in_specs = (by_row, P(), by_token, rows, rows, rows) + (P(),) * 15 + (by_token,)
    out_specs = (by_token, by_row) + (P(),) * 16
    return jax.shard_map(local, mesh=mesh, in_specs=in_specs, out_specs=out_specs, check_vma=False)
```

```python
import functools
import math

import jax
import jax.numpy as jnp
from jax import lax
from jax.experimental import pallas as pl
from jax.experimental.pallas import tpu as pltpu
from jax.sharding import PartitionSpec as P

HEAD_DIM = 64
PAIR = 2 * HEAD_DIM
SCALE = HEAD_DIM ** (-0.5)
LAYER_EPS = 1e-05
GELU_SLOPE = 0.7978845608028654
GELU_CUBIC = 0.044715
MASKED = -1e30
MESH = pl.DeviceIdType.MESH
BF = jnp.bfloat16
F32 = jnp.float32
DMA = pltpu.SemaphoreType.DMA


def dot(lhs, rhs, lhs_dim=1, rhs_dim=0):
    return lax.dot_general(
        lhs, rhs, (((lhs_dim,), (rhs_dim,)), ((), ())), preferred_element_type=F32
    )


def column_sum(values):
    return jnp.sum(values, axis=0, keepdims=True)


def row_mean(values):
    return jnp.mean(values, axis=1, keepdims=True)


def standardise(values):
    centred = values - row_mean(values)
    recip = lax.rsqrt(row_mean(centred * centred) + LAYER_EPS)
    return centred * recip, recip


def norm_back(xhat, recip, gain, grad):
    scaled = gain * grad
    return recip * (scaled - row_mean(scaled) - xhat * row_mean(scaled * xhat))


class Place:
    def __init__(self, side, layers):
        self.side, self.layers = side, layers
        dp = lax.axis_index("dp")
        self.z = lax.axis_index("table")
        self.a, self.b, self.core = dp // (2 * side), (dp // 2) % side, dp % 2
        self.me = dp * layers + self.z
        self.count = 2 * side * side * layers
        self.other_core = self.at(self.a, self.b, 1 - self.core, self.z)
        self.up = self.at(self.a, self.b, self.core, jnp.minimum(self.z + 1, layers - 1))
        self.down = self.at(self.a, self.b, self.core, jnp.maximum(self.z - 1, 0))

    def at(self, a, b, core, z):
        return ((a * self.side + b) * 2 + core, z)

    def flat(self, index):
        return (index // self.layers, lax.rem(index, self.layers))

    def copy(self, src, dst, send_sem, recv_sem, to):
        return pltpu.make_async_remote_copy(
            src_ref=src,
            dst_ref=dst,
            send_sem=send_sem,
            recv_sem=recv_sem,
            device_id=to,
            device_id_type=MESH,
        )

    def send(self, src, dst, send_sem, recv_sem, to):
        self.copy(src, dst, send_sem, recv_sem, to).start()

    def arrived(self, dst, recv_sem):
        self.copy(dst, dst, recv_sem, recv_sem, self.other_core).wait_recv()

    def sent(self, src, send_sem):
        self.copy(src, src, send_sem, send_sem, self.other_core).wait_send()

    def far_first(self):
        layers = self.layers
        return sorted(range(layers), key=lambda d: -min(d, layers - d))

    def each_other(self, act, offsets=None):
        layers = self.layers
        for dz in self.far_first() if offsets is None else offsets:

            def one(i, carry):
                act(i * layers + dz)
                return carry

            lax.fori_loop(0 if dz else 1, self.count // layers, one, 0)

    def greet_all(self):
        bar = pltpu.get_barrier_semaphore()

        def greet(step):
            to = self.flat(lax.rem(self.me + step, self.count))
            pl.semaphore_signal(bar, inc=1, device_id=to, device_id_type=MESH)

        self.each_other(greet)

    def await_all(self):
        pl.semaphore_wait(pltpu.get_barrier_semaphore(), self.count - 1)

    def exchange_start(self, out, into, send_sem, recv_sems, offsets=None):
        def start(step):
            to = lax.rem(self.me + step, self.count)
            self.send(out.at[to], into.at[self.me], send_sem, recv_sems.at[step], self.flat(to))

        self.each_other(start, offsets)

    def exchange_wait(self, into, recv_sems):
        def wait(step):
            origin = lax.rem(self.me + self.count - step, self.count)
            self.arrived(into.at[origin], recv_sems.at[step])

        self.each_other(wait)


class Reducer:
    def __init__(self, place, part, gath, bufs, recv, sent):
        self.p = place
        self.part, self.gath = part, gath
        self.core_buf, self.first_buf, self.z_buf, self.last_buf, self.z_sum, self.final = bufs
        self.core_in, self.first_in, self.z_in, self.last_in, self.own_in = recv[:5]
        self.z_back, self.first_back, self.core_back, self.last_back = recv[5:]
        self.core_out, self.first_out, self.first_ret, self.core_ret = sent[:4]
        self.z_out, self.z_ret, self.last_out, self.slim_out, self.slim_ret = sent[4:]
        layers = place.layers
        self.count = part.shape[0]
        self.slims = SLIM // place.side * place.side
        bind = functools.partial
        steps, returns = range(1, layers - 1), range(1, layers)
        self.wide_stages = (
            [self.first_sum]
            + [bind(self.z_step, s) for s in steps]
            + [self.z_final, self.last_sum]
            + [bind(self.z_return, s) for s in returns[:-1]]
            + [self.wide_z_return, self.core_return, self.finish]
        )
        self.slim_stages = (
            [self.slim_first_sum, self.slim_last_sum]
            + [self.of_own(bind(self.z_step, s)) for s in steps]
            + [self.slim_z_final]
            + [self.of_own(bind(self.z_return, s)) for s in returns[:-1]]
            + [self.slim_z_return, self.slim_last_return, self.slim_core_return, self.slim_finish]
        )

    def axes(self, k):
        p = self.p
        if isinstance(k, int):
            even = (k // p.side if k < self.slims else k) % 2 == 0
        else:
            even = lax.rem(jnp.where(k < self.slims, k // p.side, k), 2) == 0
        first = jnp.where(even, p.b, p.a)
        last = jnp.where(even, p.a, p.b)

        def first_peer(m):
            q = lax.rem(first + m, p.side)
            return q, p.at(jnp.where(even, p.a, q), jnp.where(even, q, p.b), p.core, p.z)

        def last_peer(m):
            q = lax.rem(last + m, p.side)
            return q, p.at(jnp.where(even, q, p.a), jnp.where(even, p.b, q), p.core, p.z)

        return first, last, first_peer, last_peer

    def before(self, position, m):
        return lax.rem(position - m + self.p.side, self.p.side)

    def of_own(self, act):
        return lambda base: act(base + self.axes(base)[1])

    def core_send(self, k):
        p = self.p
        p.send(
            self.part.at[k, 1 - p.core],
            self.core_buf.at[k],
            self.core_out,
            self.core_in.at[k],
            p.other_core,
        )

    def core_sum(self, k):
        p = self.p
        _, _, first_peer, _ = self.axes(k)
        p.arrived(self.core_buf.at[k], self.core_in.at[k])
        self.core_buf[k] = (
            self.core_buf[k].astype(F32) + self.part[k, p.core].astype(F32)
        ).astype(BF)
        for m in range(1, p.side):
            q, to = first_peer(m)
            p.send(
                self.core_buf.at[k, q],
                self.first_buf.at[k, m - 1],
                self.first_out,
                self.first_in.at[k, m - 1],
                to,
            )

    def add_first(self, k):
        p = self.p
        first, _, _, _ = self.axes(k)
        for m in range(1, p.side):
            p.arrived(self.first_buf.at[k, m - 1], self.first_in.at[k, m - 1])
        total = self.core_buf[k, first].astype(F32)
        for m in range(1, p.side):
            total = total + self.first_buf[k, m - 1].astype(F32)
        self.first_buf[k, 0] = total.astype(BF)

    def first_sum(self, k):
        self.add_first(k)
        self.z_start(k)

    def slim_first_sum(self, base):
        p = self.p
        for q in range(p.side):
            self.add_first(base + q)
        _, last, _, last_peer = self.axes(base)
        for m in range(1, p.side):
            q, to = last_peer(m)
            p.send(
                self.first_buf.at[base + q, 0],
                self.z_buf.at[base + last, pl.ds(0, p.layers)],
                self.slim_out,
                self.last_in.at[base + q, m - 1],
                to,
            )

    def slim_last_sum(self, base):
        p = self.p
        _, last, _, _ = self.axes(base)
        own = base + last
        total = self.first_buf[own, 0].astype(F32)
        for m in range(1, p.side):
            came = self.z_buf.at[base + self.before(last, m), pl.ds(0, p.layers)]
            p.arrived(came, self.last_in.at[own, m - 1])
            total = total + came[...].astype(F32)
        self.first_buf[own, 0] = total.astype(BF)
        self.z_start(own)

    def z_send(self, k, src, slot, to):
        self.p.send(src, self.z_buf.at[k, slot], self.z_out, self.z_in.at[k, slot], to)

    def z_start(self, k):
        p = self.p
        top = p.layers - 1

        @pl.when(p.z == 0)
        def _():
            for j in range(top, 0, -1):
                self.z_send(k, self.first_buf.at[k, 0, j], j if j > 1 else p.layers, p.up)

        @pl.when(p.z == top)
        def _():
            for j in range(0, top):
                self.z_send(k, self.first_buf.at[k, 0, j], j, p.down)

    def z_step(self, s, k):
        p = self.p
        top = p.layers - 1

        def add(j):
            p.arrived(self.z_buf.at[k, j], self.z_in.at[k, j])
            self.z_buf[k, j] = (
                self.z_buf[k, j].astype(F32) + self.first_buf[k, 0, j].astype(F32)
            ).astype(BF)
            return self.z_buf.at[k, j]

        @pl.when(p.z == s)
        def _():
            for j in range(top, s, -1):
                self.z_send(k, add(j), j if j > s + 1 else p.layers, p.up)

        @pl.when(p.z == top - s)
        def _():
            for j in range(0, top - s):
                self.z_send(k, add(j), j, p.down)

    def z_total(self, k, into):
        p = self.p
        top = p.layers - 1

        def arrival(slot):
            p.arrived(self.z_buf.at[k, slot], self.z_in.at[k, slot])
            return self.z_buf[k, slot].astype(F32)

        mine = self.first_buf[k, 0, p.z].astype(F32)

        @pl.when(p.z == 0)
        def _():
            into[k] = (mine + arrival(0)).astype(BF)

        @pl.when(p.z == top)
        def _():
            into[k] = (mine + arrival(p.layers)).astype(BF)

        @pl.when((p.z > 0) & (p.z < top))
        def _():
            into[k] = (mine + arrival(p.layers) + arrival(p.z)).astype(BF)

    def z_final(self, k):
        p = self.p
        _, _, _, last_peer = self.axes(k)
        self.z_total(k, self.z_sum)
        for m in range(1, p.side):
            _, to = last_peer(m)
            p.send(
                self.z_sum.at[k],
                self.last_buf.at[k, m - 1],
                self.last_out,
                self.last_in.at[k, m - 1],
                to,
            )

    def slim_z_final(self, base):
        own = base + self.axes(base)[1]
        self.z_total(own, self.final)
        self.z_return_start(own)

    def last_sum(self, k):
        p = self.p
        _, last, _, _ = self.axes(k)
        for m in range(1, p.side):
            p.arrived(self.last_buf.at[k, m - 1], self.last_in.at[k, m - 1])
        total = None
        for q in range(p.side):
            m = self.before(last, q)
            term = jnp.where(
                m == 0,
                self.z_sum[k].astype(F32),
                self.last_buf[k, jnp.maximum(m - 1, 0)].astype(F32),
            )
            total = term if total is None else total + term
        self.final[k] = total.astype(BF)
        self.z_return_start(k)

    def own_copy(self, k):
        p = self.p
        there = self.gath.at[k, p.core, self.axes(k)[0], p.z]
        return there, pltpu.make_async_copy(self.final.at[k], there, self.own_in.at[k])

    def z_return_start(self, k):
        p = self.p
        there, copy = self.own_copy(k)
        copy.start()

        @pl.when(p.z < p.layers - 1)
        def _():
            p.send(self.final.at[k], there, self.z_ret, self.z_back.at[k, p.z], p.up)

        @pl.when(p.z > 0)
        def _():
            p.send(self.final.at[k], there, self.z_ret, self.z_back.at[k, p.z], p.down)

    def z_return(self, s, k):
        p = self.p
        first, _, _, _ = self.axes(k)
        top = p.layers - 1

        def forward(j, ahead, to):
            shard = self.gath.at[k, p.core, first, j]
            p.arrived(shard, self.z_back.at[k, j])

            @pl.when(ahead)
            def _():
                p.send(shard, shard, self.z_ret, self.z_back.at[k, j], to)

        @pl.when(p.z >= s)
        def _():
            forward(jnp.maximum(p.z - s, 0), p.z < top, p.up)

        @pl.when(p.z <= top - s)
        def _():
            forward(jnp.minimum(p.z + s, top), p.z > 0, p.down)

        if s == top:
            self.own_copy(k)[1].wait()

    def send_first(self, k, chunks):
        p = self.p
        first, _, first_peer, _ = self.axes(k)
        mine = self.gath.at[chunks, p.core, first]
        for m in range(1, p.side):
            p.send(mine, mine, self.first_ret, self.first_back.at[k, m - 1], first_peer(m)[1])

    def send_core(self, k, chunks):
        p = self.p
        first, _, _, _ = self.axes(k)
        for m in range(1, p.side):
            came = self.gath.at[chunks, p.core, self.before(first, m)]
            p.arrived(came, self.first_back.at[k, m - 1])
        mine = self.gath.at[chunks, p.core]
        p.send(mine, mine, self.core_ret, self.core_back.at[k], p.other_core)

    def wide_z_return(self, k):
        self.z_return(self.p.layers - 1, k)
        self.send_first(k, k)

    def core_return(self, k):
        self.send_core(k, k)

    def finish(self, k):
        self.p.arrived(self.gath.at[k, 1 - self.p.core], self.core_back.at[k])

    def slim_z_return(self, base):
        p = self.p
        first, last, _, last_peer = self.axes(base)
        own = base + last
        self.z_return(p.layers - 1, own)
        mine = self.gath.at[own, p.core, first]
        for m in range(1, p.side):
            p.send(mine, mine, self.slim_ret, self.last_back.at[own, m - 1], last_peer(m)[1])

    def slim_last_return(self, base):
        p = self.p
        first, last, _, _ = self.axes(base)
        for m in range(1, p.side):
            k = base + self.before(last, m)
            p.arrived(self.gath.at[k, p.core, first], self.last_back.at[k, m - 1])
        self.send_first(base, pl.ds(base, p.side))

    def slim_core_return(self, base):
        self.send_core(base, pl.ds(base, self.p.side))

    def slim_finish(self, base):
        unit = self.gath.at[pl.ds(base, self.p.side), 1 - self.p.core]
        self.p.arrived(unit, self.core_back.at[base])

    def drain(self):
        p = self.p
        units = self.slims // p.side
        wides = self.count - self.slims
        chains = pl.ds(0, wides + units)
        p.sent(self.core_buf, self.core_out)
        p.sent(self.first_buf, self.first_out)
        p.sent(self.first_buf, self.first_ret)
        p.sent(self.core_buf, self.core_ret)
        p.sent(self.z_buf.at[chains, pl.ds(0, p.layers - 1)], self.z_out)
        middle = (p.z > 0) & (p.z < p.layers - 1)

        @pl.when(middle)
        def _():
            p.sent(self.z_buf.at[chains], self.z_ret)

        @pl.when(jnp.logical_not(middle))
        def _():
            p.sent(self.z_buf.at[chains, pl.ds(0, 1)], self.z_ret)

        if wides:
            p.sent(self.last_buf.at[pl.ds(0, wides)], self.last_out)
        if units:
            p.sent(self.first_buf.at[pl.ds(0, units)], self.slim_out)
            p.sent(self.first_buf.at[pl.ds(0, units)], self.slim_ret)


def reducer_scratch(count, side, layers, rows, wide):
    bufs = [
        pltpu.VMEM((count, side, layers, rows, wide), BF),
        pltpu.VMEM((count, side - 1, layers, rows, wide), BF),
        pltpu.VMEM((count, layers + 1, rows, wide), BF),
        pltpu.VMEM((count, side - 1, rows, wide), BF),
        pltpu.VMEM((count, rows, wide), BF),
        pltpu.VMEM((count, rows, wide), BF),
    ]
    recv = [
        DMA((count,)),
        DMA((count, side - 1)),
        DMA((count, layers + 1)),
        DMA((count, side - 1)),
        DMA((count,)),
        DMA((count, layers)),
        DMA((count, side - 1)),
        DMA((count,)),
        DMA((count, side - 1)),
    ]
    return bufs, recv, [DMA(())] * 9


def layer_kernel(cfg, *refs):
    refs = list(refs)

    def take(number):
        taken = refs[:number]
        del refs[:number]
        return taken

    (knowledge, expr_table, owner_ids, gene_row, expr_bin, lengths) = take(6)
    (gain1, bias1, w_query, b_query, w_key, w_value, b_value, w_out1, b_out1) = take(9)
    (gain2, bias2, w_in, b_in, w_out, b_out, cotangent) = take(7)
    mixed, table_grad, gath = take(3)
    know_v, wq_v, wk_v, wv_v, wo_v, win_v, wout_v, cot_v = take(8)
    load_sems, ids_out, ids_in, rows_out, rows_in, back_in, row_hot_v, slot_hot_v = take(8)
    ids_sem, rows_sem, ids_sent, rows_sent, back_sent = take(5)
    (embedded_v, attn_in_v, query_v, key_v, value_v, probs_v, context_v) = take(7)
    (hidden1_v, ffn_in_v, grad_ffn_v, acc_v, gn2_v, biases_v) = take(6)
    part, table_v, mixed_v, result_sems = take(4)
    bufs, recv, sent = take(6), take(9), take(9)
    assert not refs

    side, layers, cap, offsets = cfg
    place = Place(side, layers)
    devices = place.count
    red = Reducer(place, part, gath, bufs, recv, sent)
    tokens, width = embedded_v.shape
    table_rows = knowledge.shape[1]
    half = width // 2
    blocks = w_in.shape[1] // width
    count = part.shape[0]
    slots = devices * cap

    place.greet_all()

    loads = [
        (knowledge, know_v),
        (w_query, wq_v),
        (w_key, wk_v),
        (w_value, wv_v),
        (w_out1, wo_v),
        (cotangent, cot_v),
    ]
    for j in range(blocks):
        loads.append((w_in.at[:, pl.ds(j * width, width)], win_v.at[j % 2]))
        loads.append((w_out.at[pl.ds(j * width, width)], wout_v.at[j % 2]))
    loads = [
        pltpu.make_async_copy(src, dst, load_sems.at[i]) for i, (src, dst) in enumerate(loads)
    ]
    for load in loads[: 6 + 4]:
        load.start()

    def iota(shape, dim):
        return lax.broadcasted_iota(jnp.int32, shape, dim)

    def hot(condition):
        return jnp.where(condition, 1.0, 0.0).astype(BF)

    owner_row = owner_ids[...]
    owner_hot = hot(iota((devices, tokens), 0) == owner_row)
    earlier = hot(iota((tokens, tokens), 0) < iota((tokens, tokens), 1))
    before = dot(owner_hot, earlier)
    rank_row = column_sum(before * owner_hot.astype(F32)).astype(jnp.int32)
    slot_hot_v[...] = hot(iota((slots, tokens), 0) == owner_row * cap + rank_row)
    rank_hot = hot(iota((128, tokens), 0) == rank_row)
    named = (owner_hot.astype(F32) * (gene_row[...] + 1).astype(F32)).astype(BF)
    wanted = dot(named, rank_hot, 1, 1)
    for d in range(devices):
        ids_out[d] = wanted[d : d + 1]

    place.await_all()
    place.exchange_start(ids_out, ids_in, ids_sent, ids_sem)
    ids_in[place.me] = ids_out[place.me]
    loads[0].wait()
    table_sum = know_v[0].astype(F32)
    for k in range(1, know_v.shape[0]):
        table_sum = table_sum + know_v[k].astype(F32)
    table_sum = table_sum.astype(BF)
    expr_hot = hot(iota((expr_table.shape[0], tokens), 0) == expr_bin[...])
    expr_part = dot(expr_hot, expr_table[...], 0, 0)
    place.exchange_wait(ids_in, ids_sem)
    asked = ids_in[...].reshape(devices, 128).astype(BF)
    spread = hot(iota((slots, devices), 0) // cap == iota((slots, devices), 1))
    asked = dot(spread, asked)
    own_lane = lax.rem(iota((slots, 128), 0), cap) == iota((slots, 128), 1)
    asked = jnp.sum(jnp.where(own_lane, asked, 0.0), axis=1, keepdims=True)
    row_hot = hot(iota((slots, table_rows), 1) + 1 == asked.astype(jnp.int32))
    row_hot_v[...] = row_hot
    rows_out[...] = dot(row_hot, table_sum).astype(BF).reshape(devices, cap, width)
    place.exchange_start(rows_out, rows_in, rows_sent, rows_sem)
    rows_in[place.me] = rows_out[place.me]

    end = lengths[0]
    ends = [end]
    for c in range(1, lengths.shape[0]):
        end = end + lengths[c]
        ends.append(end)

    def segments(shape, dim):
        spot = iota(shape, dim)
        segment = jnp.zeros(shape, jnp.int32)
        for stop in ends:
            segment = segment + jnp.where(spot >= stop, 1, 0)
        return segment

    spot = lax.rem(iota((2 * tokens, tokens), 0), tokens)
    segment = jnp.zeros((2 * tokens, tokens), jnp.int32)
    for stop in ends:
        segment = segment + jnp.where(spot >= stop, 1, 0)
    same_cell = segment == segments((2 * tokens, tokens), 1)
    live = jnp.where(iota((tokens, 1), 0) < ends[-1], 1.0, 0.0)

    place.exchange_wait(rows_in, rows_sem)
    gathered = rows_in[...].reshape(slots, width)
    embedded_v[...] = dot(slot_hot_v[...], gathered, 0, 0) + expr_part
    for load in loads[1:5]:
        load.wait()

    xhat1, recip1 = standardise(embedded_v[...])
    attn_in_v[...] = (xhat1 * gain1[...].reshape(1, width) + bias1[...].reshape(1, width)).astype(BF)
    query_v[...] = (dot(attn_in_v[...], wq_v[...]) + b_query[...].reshape(1, width)).astype(BF)
    key_v[...] = dot(attn_in_v[...], wk_v[...]).astype(BF)
    value_v[...] = (dot(attn_in_v[...], wv_v[...]) + b_value[...].reshape(1, width)).astype(BF)
    low_lane = iota((tokens, PAIR), 1) < HEAD_DIM

    def two_heads(values):
        zero = jnp.zeros_like(values)
        return jnp.concatenate(
            [jnp.where(low_lane, values, zero), jnp.where(low_lane, zero, values)], axis=0
        )

    def one_of_two(values):
        return jnp.where(low_lane, values[:tokens], values[tokens:])

    for pair in range(width // PAIR):
        lanes = slice(pair * PAIR, (pair + 1) * PAIR)
        scores = dot(two_heads(query_v[:, lanes]), key_v[:, lanes], 1, 1) * SCALE
        scores = jnp.where(same_cell, scores, MASKED)
        scores = jnp.exp(scores - jnp.max(scores, axis=1, keepdims=True))
        probs = scores / jnp.sum(scores, axis=1, keepdims=True)
        probs_v[pair] = probs
        context_v[:, lanes] = one_of_two(dot(probs.astype(BF), value_v[:, lanes])).astype(BF)
    hidden1_v[...] = (
        embedded_v[...] + dot(context_v[...], wo_v[...]) + b_out1[...].reshape(1, width)
    )
    loads[5].wait()

    xhat2, recip2 = standardise(hidden1_v[...])
    ffn_in_v[...] = (xhat2 * gain2[...].reshape(1, width) + bias2[...].reshape(1, width)).astype(BF)
    grad_hidden2 = cot_v[...].astype(F32) * live
    grad_ffn_v[...] = grad_hidden2.astype(BF)
    acc_v[...] = jnp.zeros_like(acc_v)
    gn2_v[...] = jnp.zeros_like(gn2_v)
    biases_v[...] = jnp.zeros_like(biases_v)
    shard = part.shape[1:]
    plans = []
    for stages, lags in zip((red.wide_stages, red.slim_stages), offsets):
        reach = [0]
        for lag in lags:
            reach.append(reach[-1] + lag)
        assert len(reach) == len(stages)
        plans.append(list(zip(stages, reach)))
    longest = max(plan[-1][1] for plan in plans)

    def step(i):
        for slim, plan in enumerate(plans):
            for stage, lag in sorted(plan, key=lambda entry: -entry[1]):
                k = i - lag
                ahead = side - 1 if slim else 0
                low, high = (0, red.slims) if slim else (red.slims, count)
                if isinstance(k, int):
                    if low <= k < high and (not slim or k % side == ahead):
                        stage(k - ahead)
                elif low < high:
                    now = (k >= low) & (k < high)
                    if slim:
                        now = now & (lax.rem(k, side) == ahead)

                    @pl.when(now)
                    def _():
                        stage(k - ahead)

    def put(k, values):
        part[k] = values.reshape(shard).astype(BF)
        red.core_send(k)

    done = [0]

    def pipe(where):
        for _ in range(PIPE.get(where, 0)):
            step(done[0])
            done[0] += 1

    def put_bias(row, values):
        biases_v[pl.ds(2 * row, 1), :] = values[:, :half]
        biases_v[pl.ds(2 * row + 1, 1), :] = values[:, half:]

    for j in range(blocks):
        loads[6 + 2 * j].wait()
        loads[7 + 2 * j].wait()
        win, wout = win_v.at[j % 2], wout_v.at[j % 2]
        pre = dot(ffn_in_v[...], win[...]) + b_in[pl.ds(j * width, width)].reshape(1, width)
        square = pre * pre
        bend = jnp.tanh(GELU_SLOPE * (pre + GELU_CUBIC * square * pre))
        act = (0.5 * pre * (1.0 + bend)).astype(BF)
        slope = 0.5 * (1.0 + bend) + 0.5 * pre * (1.0 - bend * bend) * (
            GELU_SLOPE * (1.0 + 3.0 * GELU_CUBIC * square)
        )
        grad_pre = dot(grad_ffn_v[...], wout[...], 1, 1) * slope
        grad_pre = grad_pre.astype(BF)
        if j:
            for q in range(4):
                red.core_sum(4 * (j - 1) + q)
        for h in range(2):
            put(4 * j + h, dot(act, grad_ffn_v[:, h * half : (h + 1) * half], 0, 0))
        for h in range(2):
            put(4 * j + 2 + h, dot(ffn_in_v[...], grad_pre[:, h * half : (h + 1) * half], 0, 0))
        acc_v[...] += dot(act, wout[...])
        gn2_v[...] += dot(grad_pre, win[...], 1, 1)
        if j + 2 < blocks:
            loads[10 + 2 * j].start()
            loads[11 + 2 * j].start()
        put_bias(j, column_sum(grad_pre.astype(F32)))
        pipe(f'ffn{j}')
    at = 4 * blocks
    mixed_v[...] = (
        (hidden1_v[...] + acc_v[...] + b_out[...].reshape(1, width)) * live
    ).astype(BF)
    put_bias(blocks, column_sum(grad_ffn_v[...].astype(F32)))
    grad_normed2 = gn2_v[...]
    put_bias(blocks + 1, column_sum(grad_normed2 * xhat2))
    put_bias(blocks + 2, column_sum(grad_normed2))
    for q in range(4):
        red.core_sum(at - 4 + q)
    grad_hidden1 = grad_hidden2 + norm_back(xhat2, recip2, gain2[...].reshape(1, width), grad_normed2)
    acc_v[...] = grad_hidden1
    grad_attn = grad_hidden1.astype(BF)
    put_bias(blocks + 3, column_sum(grad_attn.astype(F32)))
    for h in range(2):
        put(at + h, dot(context_v[...], grad_attn[:, h * half : (h + 1) * half], 0, 0))
    pipe('out')
    gctx_v = ffn_in_v
    gctx_v[...] = dot(grad_attn, wo_v[...], 1, 1).astype(BF)
    gq_v, gk_v, gv_v = query_v, key_v, value_v

    for pair in range(width // PAIR):
        lanes = slice(pair * PAIR, (pair + 1) * PAIR)
        probs = probs_v[pair]
        grads = two_heads(gctx_v[:, lanes])
        grad_probs = dot(grads, value_v[:, lanes], 1, 1)
        inner = jnp.sum(probs * grad_probs, axis=1, keepdims=True)
        grad_scores = (probs * (grad_probs - inner)).astype(BF)
        grad_query = one_of_two(dot(grad_scores, key_v[:, lanes])) * SCALE
        grad_key = dot(grad_scores, two_heads(query_v[:, lanes]), 0, 0) * SCALE
        gq_v[:, lanes] = grad_query.astype(BF)
        gk_v[:, lanes] = grad_key.astype(BF)
        gv_v[:, lanes] = dot(probs.astype(BF), grads, 0, 0).astype(BF)
        pipe(f'pair{pair}')
    for q in range(2):
        red.core_sum(at + q)
    at += 2
    for grad in (gq_v, gk_v, gv_v):
        for h in range(2):
            put(at + h, dot(attn_in_v[...], grad[:, h * half : (h + 1) * half], 0, 0))
        at += 2
        pipe(f'grad{at}')
    put_bias(blocks + 4, column_sum(gq_v[...].astype(F32)))
    put_bias(blocks + 5, column_sum(gv_v[...].astype(F32)))
    grad_normed1 = dot(gq_v[...], wq_v[...], 1, 1)
    grad_normed1 = grad_normed1 + dot(gk_v[...], wk_v[...], 1, 1)
    grad_normed1 = grad_normed1 + dot(gv_v[...], wv_v[...], 1, 1)
    xhat1, recip1 = standardise(embedded_v[...])
    put_bias(blocks + 6, column_sum(grad_normed1 * xhat1))
    put_bias(blocks + 7, column_sum(grad_normed1))
    grad_embedded = acc_v[...] + norm_back(
        xhat1, recip1, gain1[...].reshape(1, width), grad_normed1
    )
    grad_embedded = grad_embedded.astype(BF)
    back_out = rows_out
    place.sent(rows_out.at[pl.ds(0, devices - 1)], rows_sent)
    back_out[...] = dot(slot_hot_v[...], grad_embedded).astype(BF).reshape(devices, cap, width)
    expr_grad = dot(expr_hot, grad_embedded)
    bins = expr_grad.shape[0]
    filler = jnp.zeros((width - 2 * bins - biases_v.shape[0], half), F32)
    put(
        at,
        jnp.concatenate([expr_grad[:, :half], expr_grad[:, half:], biases_v[...], filler], axis=0),
    )
    pipe('back')
    back_in[place.me] = back_out[place.me]
    for k in range(at - 6, at + 1):
        red.core_sum(k)

    def later(i, carry):
        step(i)
        return carry

    total = count + longest
    middle = min(max(MIDDLE, done[0]), total)
    lax.fori_loop(done[0], middle, later, 0)
    for dz in place.far_first():
        place.exchange_start(back_out, back_in, back_sent, ids_sem, [dz])
        if middle < total:
            step(middle)
            middle += 1
    end = min(middle + SETTLE, total)
    lax.fori_loop(middle, end, later, 0)
    place.exchange_wait(back_in, ids_sem)
    table_v[...] = dot(row_hot_v[...], back_in[...].reshape(slots, width), 0, 0)
    results = [
        pltpu.make_async_copy(table_v, table_grad, result_sems.at[0]),
        pltpu.make_async_copy(mixed_v, mixed, result_sems.at[1]),
    ]
    for result in results:
        result.start()
    lax.fori_loop(end, total, later, 0)
    for result in results:
        result.wait()
    place.sent(ids_out.at[pl.ds(0, devices - 1)], ids_sent)
    place.sent(back_out.at[pl.ds(0, devices - 1)], back_sent)
    red.drain()


def layer(side, layers, args):
    (knowledge, expr_table, gene_owner, gene_row, expr_bin, cell_lengths) = args[:6]
    cotangent, w_in = args[21], args[17]
    tokens, width = cotangent.shape
    devices = 2 * side * side * layers
    cap = max(8, 2 * tokens // devices)
    slots = devices * cap
    table_rows = knowledge.shape[1]
    blocks = w_in.shape[1] // width
    count = 4 * blocks + 9
    half = width // 2
    shard = width // (2 * side * layers)
    whole = (count, 2, side, layers, shard, half)
    bufs, recv, sent = reducer_scratch(count, side, layers, shard, half)
    wide = lambda dtype: pltpu.VMEM((tokens, width), dtype)
    square = pltpu.VMEM((width, width), BF)
    scratch = [
        pltpu.VMEM(knowledge.shape, BF),
        square,
        square,
        square,
        square,
        pltpu.VMEM((2, width, width), BF),
        pltpu.VMEM((2, width, width), BF),
        wide(BF),
        DMA((6 + 2 * blocks,)),
        pltpu.VMEM((devices, 1, 128), F32),
        pltpu.VMEM((devices, 1, 128), F32),
        pltpu.VMEM((devices, cap, width), BF),
        pltpu.VMEM((devices, cap, width), BF),
        pltpu.VMEM((devices, cap, width), BF),
        pltpu.VMEM((slots, table_rows), BF),
        pltpu.VMEM((slots, tokens), BF),
        DMA((devices,)),
        DMA((devices,)),
        DMA(()),
        DMA(()),
        DMA(()),
        wide(F32),
        wide(BF),
        wide(BF),
        wide(BF),
        wide(BF),
        pltpu.VMEM((width // PAIR, 2 * tokens, tokens), F32),
        wide(BF),
        wide(F32),
        wide(BF),
        wide(BF),
        wide(F32),
        wide(F32),
        pltpu.VMEM((8 * ((2 * (blocks + 8) + 7) // 8), half), F32),
        pltpu.VMEM(whole, BF),
        pltpu.VMEM((table_rows, width), F32),
        wide(BF),
        DMA((2,)),
    ]
    vmem = pl.BlockSpec(memory_space=pltpu.VMEM)
    hbm = pl.BlockSpec(memory_space=pl.ANY)
    smem = pl.BlockSpec(memory_space=pltpu.SMEM)
    in_hbm = {0, 8, 10, 11, 13, 17, 19, 21}
    specs = [hbm if i in in_hbm else smem if i == 5 else vmem for i in range(22)]
    offsets = OFFSETS
    flops = 2 * tokens * (3 * (4 * width * width + 2 * width * w_in.shape[1]))
    return pl.pallas_call(
        functools.partial(layer_kernel, (side, layers, cap, offsets)),
        out_shape=(
            jax.ShapeDtypeStruct((tokens, width), BF),
            jax.ShapeDtypeStruct((table_rows, width), F32),
            jax.ShapeDtypeStruct(whole, BF),
        ),
        in_specs=specs,
        out_specs=(hbm, hbm, hbm),
        scratch_shapes=scratch + bufs + recv + sent,
        compiler_params=pltpu.CompilerParams(
            collective_id=1, has_side_effects=True, vmem_limit_bytes=VMEM_BYTES
        ),
        cost_estimate=pl.CostEstimate(flops=flops, bytes_accessed=40 << 20, transcendentals=0),
    )(
        knowledge,
        expr_table,
        gene_owner.reshape(1, tokens),
        gene_row.reshape(1, tokens),
        expr_bin.reshape(1, tokens),
        *args[5:],
    )


OFFSETS = ([2, 1, 1, 3, 2, 2, 1, 6, 6], [4, 2, 2, 1, 2, 1, 0, 3, 7, 2])
SLIM = 10
PIPE = {"ffn2": 2, "ffn3": 2, "pair2": 2, "pair4": 1, "grad20": 1, "grad22": 1, "grad24": 2, "back": 1, "pair5": 1}
MIDDLE = 35
SETTLE = 8
VMEM_BYTES = 62 << 20
DEPTH = 8


def spread_kernel(gath, table_grad, mixed, *refs):
    (mixed_out, know_out, expr_out, gain1_out, bias1_out, wq_out, bq_out, wk_out, wv_out) = refs[:9]
    (bv_out, wo_out, bo1_out, gain2_out, bias2_out, win_out, bin_out, wout_out, bout_out) = refs[9:18]
    narrow, broad, small, table_v, in_sems, out_sems, know_sems, more_sems = refs[18:]
    count, width, half = gath.shape
    blocks = win_out.shape[1] // width
    places = []
    for j in range(blocks):
        rows = pl.ds(j * width, width)
        for h in range(2):
            places.append(wout_out.at[rows, pl.ds(h * half, half)])
        for h in range(2):
            places.append(win_out.at[:, pl.ds(j * width + h * half, half)])
    for out in (wo_out, wq_out, wk_out, wv_out):
        for h in range(2):
            places.append(out.at[:, pl.ds(h * half, half)])
    last = count - 1
    assert len(places) == last

    def fetch(k):
        return pltpu.make_async_copy(gath.at[k], narrow.at[k % DEPTH], in_sems.at[k % DEPTH])

    def store(k):
        return pltpu.make_async_copy(broad.at[k % DEPTH], places[k], out_sems.at[k % DEPTH])

    for k in range(DEPTH - 1):
        fetch(k).start()
    more = [
        pltpu.make_async_copy(gath.at[last, pl.ds(0, small.shape[0])], small, more_sems.at[0]),
        pltpu.make_async_copy(table_grad, table_v, more_sems.at[1]),
        pltpu.make_async_copy(mixed, mixed_out, more_sems.at[2]),
    ]
    for copy in more:
        copy.start()
    knows = [
        pltpu.make_async_copy(table_v, know_out.at[i], know_sems.at[i])
        for i in range(know_out.shape[0])
    ]

    def convert(k):
        fetch(k).wait()
        if k >= DEPTH:
            store(k - DEPTH).wait()
        broad[k % DEPTH] = narrow[k % DEPTH].astype(F32)
        store(k).start()
        if k + DEPTH < last:
            fetch(k + DEPTH).start()

    fetch(DEPTH - 1).start()
    for k in range(DEPTH):
        convert(k)
    more[1].wait()
    for know in knows:
        know.start()
    more[0].wait()
    bins = expr_out.shape[0]
    expr_out[:, :half] = small[pl.ds(0, bins), :].astype(F32)
    expr_out[:, half:] = small[pl.ds(bins, bins), :].astype(F32)
    biases = small[pl.ds(2 * bins, small.shape[0] - 2 * bins), :].astype(F32)

    def bias(i):
        return jnp.concatenate([biases[2 * i : 2 * i + 1], biases[2 * i + 1 : 2 * i + 2]], axis=1)[0]

    for j in range(blocks):
        bin_out[pl.ds(j * width, width)] = bias(j)
    for i, out in enumerate(
        (bout_out, gain2_out, bias2_out, bo1_out, bq_out, bv_out, gain1_out, bias1_out)
    ):
        out[...] = bias(blocks + i)
    for k in range(DEPTH, last):
        convert(k)
    for k in range(last - DEPTH, last):
        store(k).wait()
    for know in knows:
        know.wait()
    more[2].wait()


def spread(gath, table_grad, mixed, tables, bins, hidden):
    count, width, half = gath.shape
    shape = lambda *dims: jax.ShapeDtypeStruct(dims, F32)
    vector, square = shape(width), shape(width, width)
    vmem = pl.BlockSpec(memory_space=pltpu.VMEM)
    hbm = pl.BlockSpec(memory_space=pl.ANY)
    outs = (
        (jax.ShapeDtypeStruct(mixed.shape, mixed.dtype), hbm),
        (shape(tables, *table_grad.shape), hbm),
        (shape(bins, width), vmem),
        (vector, vmem),
        (vector, vmem),
        (square, hbm),
        (vector, vmem),
        (square, hbm),
        (square, hbm),
        (vector, vmem),
        (square, hbm),
        (vector, vmem),
        (vector, vmem),
        (vector, vmem),
        (shape(width, hidden), hbm),
        (shape(hidden), vmem),
        (shape(hidden, width), hbm),
        (vector, vmem),
    )
    return pl.pallas_call(
        spread_kernel,
        out_shape=tuple(out for out, _ in outs),
        in_specs=[pl.BlockSpec(memory_space=pltpu.HBM)] * 3,
        out_specs=tuple(spec for _, spec in outs),
        scratch_shapes=[
            pltpu.VMEM((DEPTH, width, half), BF),
            pltpu.VMEM((DEPTH, width, half), F32),
            pltpu.VMEM((2 * bins + 16 * ((2 * (hidden // width + 8) + 15) // 16), half), BF),
            pltpu.VMEM(table_grad.shape, F32),
            DMA((DEPTH,)),
            DMA((DEPTH,)),
            DMA((tables,)),
            DMA((3,)),
        ],
        compiler_params=pltpu.CompilerParams(vmem_limit_bytes=60 << 20),
        cost_estimate=pl.CostEstimate(flops=0, bytes_accessed=48 << 20, transcendentals=0),
    )(gath, table_grad, mixed)


def local(*args):
    layers = lax.axis_size("table")
    side = math.isqrt(lax.axis_size("dp") // 2)
    knowledge, expr_table, w_in = args[0], args[1], args[17]
    width, hidden = w_in.shape
    mixed, table_grad, total = layer(side, layers, args)
    total = total.reshape(-1, width, width // 2)
    return spread(total, table_grad, mixed, knowledge.shape[0], expr_table.shape[0], hidden)


def solution(mesh):
    rows = P(("dp", "table"))
    by_token = P(("dp", "table"), None)
    by_row = P(None, ("dp", "table"), None)
    in_specs = (by_row, P(), by_token, rows, rows, rows) + (P(),) * 15 + (by_token,)
    out_specs = (by_token, by_row) + (P(),) * 16
    return jax.shard_map(local, mesh=mesh, in_specs=in_specs, out_specs=out_specs, check_vma=False)
```
